32 devices in a mesh: dp: 4 (over y, x), expert: 8 (over z, core).
Axes of the slice: x: 2, y: 2, z: 4, core: 2. Of those that a mesh axis runs over, the one named last changes fastest.
Arguments:
- tokens: bfloat16 [512, 1024], P(('dp', 'expert')), may hold values from -6 to 6
- upstream: bfloat16 [512, 1024], P(('dp', 'expert')), may hold values from -6 to 6
- expert_ids: int32 [512, 8], P(('dp', 'expert')), may hold values from 0 to 7, all different within a row; in each aligned block of 16 rows (0 to 15, 16 to 31, ...) at most 16 rows name the same one
- gates: float32 [512, 8], P(('dp', 'expert')), may hold values from 0.05 to 1
- relocate: int32 [8, 1], replicated, may hold values from 0 to 1, as said below
- w_gate_up: bfloat16 [8, 4, 384, 1024], P('expert', 'dp'), may hold values from -0.1875 to 0.1875
- w_down: bfloat16 [8, 4, 192, 1024], P('expert', 'dp'), may hold values from -0.21875 to 0.21875
Outputs:
- grad_tokens: bfloat16 [512, 1024], P(('dp', 'expert'))
- grad_gate_up: bfloat16 [8, 4, 384, 1024], P('expert', 'dp')
- grad_down: bfloat16 [8, 4, 192, 1024], P('expert', 'dp')
The draws below stay inside these ranges and needn't reach their ends.
Inputs may be any that keep to these rules, and one draw needn't show every extreme that they name: `expert_ids`: each row names 8 different experts; the rows of one device name one expert at most 16 times, and some device reaches 16. `relocate`: the first and the second half of the rows are equal; both values occur.
All inputs are finite; a program needn't handle non-finite values.
Results may differ from the reference program's by a relative error of at most 0.0064.
Values may be sent and summed in bfloat16 or wider, within the bound.
No kernel may reach another device: no remote copies, remote signals or barrier semaphores. Data moves between devices by JAX's collectives and lax.ppermute only.
A program may use at most 64 MiB of HBM per device.

```python
import math
import jax
import jax.numpy as jnp
import numpy as np
from jax import lax

D = 1024
F = 768
SLICES = 4
TOP = 8
TOK_DEV = 16
FS = 192
SLOTS = 1
EXPERTS = 8
CAP = 16
TOKENS = 512
N_DP = 4
N_EXPERT = 8


def draw_relocate(key, part):
    half_rows = N_EXPERT // 2
    entry_count = half_rows * SLOTS
    flat_bits = jax.random.randint(jax.random.fold_in(key, 11), (entry_count,), 0, 2, dtype=jnp.int32)
    order = jax.random.permutation(jax.random.fold_in(key, 23), entry_count).astype(jnp.int32)
    flat_bits = flat_bits.at[order[0]].set(0)
    flat_bits = flat_bits.at[order[1]].set(1)
    first_half = flat_bits.reshape(half_rows, SLOTS)
    return jnp.concatenate([first_half, first_half], axis=0)


def block_scale(stream_key, shape, cuts, smallest, high):
    gain, own = 1.0, jax.random.fold_in(stream_key, 6)
    for dim, shards_of in cuts:
        steps = jnp.exp(jax.random.uniform(jax.random.fold_in(own, dim), (shards_of,), jnp.float32, smallest / len(cuts), high / len(cuts)))
        gain = gain * jnp.repeat(steps, shape[dim] // shards_of).reshape([-1 if axis == dim else 1 for axis in range(len(shape))])
    return gain


def shared_out(key, own, number, rows, amount, top, reach, skew):
    sequence = jax.random.permutation(key, amount)
    packed, ordinary = shares(amount, rows * top, reach, skew, True), shares(amount, rows * top, reach, skew, False)
    places = jnp.arange(amount)

    def named(sizes, offset_by):
        used = int((sizes > 0).sum())
        fixed = max(1, used // 4)
        passed = fixed + (places - fixed + offset_by * (used - fixed)) % max(1, amount - fixed)
        return jnp.zeros((amount,), jnp.int32).at[sequence[jnp.where(places < fixed, places, passed)]].set(jnp.asarray(sizes, jnp.int32))

    sizes = jnp.where(number % 4 == 0, named(packed, number // 4), named(ordinary, number - number // 4 - 1))
    mixed = jax.random.permutation(jax.random.fold_in(own, 3), amount)
    donor, receiver = mixed[0:amount // 2 * 2:2], mixed[1:amount // 2 * 2:2]
    margin = jnp.minimum(sizes[donor] - 1, reach - sizes[receiver]) // 2
    margin = jnp.where((donor == sequence[0]) | (receiver == sequence[0]) | (sizes[receiver] == 0), 0, jnp.maximum(margin, 0))
    passed = jax.random.randint(jax.random.fold_in(own, 4), (amount // 2,), 0, 1 << 20) % (margin + 1)
    sizes = sizes.at[donor].add(-passed).at[receiver].add(passed)
    items = jnp.searchsorted(jnp.cumsum(sizes), jnp.arange(rows * top), side="right").astype(jnp.int32)
    grid = items.reshape(top, rows).T
    grid = grid[jax.random.permutation(jax.random.fold_in(own, 1), rows)]
    offset_by = jax.random.randint(jax.random.fold_in(own, 2), (rows, 1), 0, top)
    return jnp.take_along_axis(grid, (jnp.arange(top)[None, :] + offset_by) % top, axis=1)


def shares(amount, total, bound, lean, full):
    loads = [(1 << 20) // math.isqrt(rank ** lean) + 1 for rank in range(1, amount + 1)]
    largest = bound if full else min(bound, max(-(-total // amount), total * loads[0] // sum(loads)))
    least = 1 if total - largest >= amount - 1 else 0
    given, surplus = [largest] + [least] * (amount - 1), total - largest - least * (amount - 1)
    while surplus > 0:
        candidates = [i for i in range(1, amount) if given[i] < largest] or [i for i in range(1, amount) if given[i] < bound]
        whole, budget = sum([loads[i] for i in candidates]), surplus
        for i in candidates:
            extra = min(bound - given[i], max(1, budget * loads[i] // whole), surplus)
            given[i] = given[i] + extra
            surplus = surplus - extra
    return np.array(given)


def normal_values(stream_key, extent, spread, most, shards=(), held_as=jnp.bfloat16):
    array = spread * jax.random.normal(stream_key, extent, jnp.float32)
    if shards:
        array = array * block_scale(stream_key, extent, shards, -0.22, 0.18)
    return jnp.clip(array, -most, most).astype(held_as)


def setup_inputs(seed: int = 0) -> dict:
    seeds = jax.random.split(jax.random.key(seed), 8)
    tokens = normal_values(seeds[0], (TOKENS, D), 1.0, 6.0, ((0, 32),))
    upstream = normal_values(seeds[1], (TOKENS, D), 1.0, 6.0, ((0, 32),))
    expert_ids_keys = jax.random.split(jax.random.fold_in(seeds[2], 1), TOKENS // TOK_DEV)
    expert_ids_turns = jax.random.permutation(jax.random.fold_in(seeds[2], 3), TOKENS // TOK_DEV)
    expert_ids = jax.vmap(lambda own, number: shared_out(jax.random.fold_in(seeds[2], 2), own, number, TOK_DEV, EXPERTS, TOP, CAP, 2))(expert_ids_keys, expert_ids_turns).reshape((TOKENS, TOP))
    gates = jnp.clip(jnp.exp(math.log(1.0) - 2.9957323 * jax.random.uniform(seeds[3], (TOKENS, TOP), jnp.float32) ** block_scale(seeds[3], (TOKENS, TOP), ((0, 32),), -0.2, 0.2)), 0.05, 1.0)
    relocate = draw_relocate(jax.random.fold_in(seeds[7], 71), 0)
    w_gate_up = normal_values(seeds[5], (N_EXPERT, N_DP, 2 * FS, D), D ** -0.5, 0.1875, ((0, 8), (1, 4)))
    w_down = normal_values(seeds[6], (N_EXPERT, N_DP, FS, D), F ** -0.5, 0.21875, ((0, 8), (1, 4)))
    return dict(tokens=tokens, upstream=upstream, expert_ids=expert_ids, gates=gates, relocate=relocate, w_gate_up=w_gate_up, w_down=w_down)


def silu_parts(values_in):
    sigmoid_of = jax.nn.sigmoid(values_in)
    return values_in * sigmoid_of, sigmoid_of * (1.0 + values_in * (1.0 - sigmoid_of))


def reference(tokens, upstream, expert_ids, gates, relocate, w_gate_up, w_down):
    rows_most = N_DP * N_EXPERT * CAP
    pair_count = TOKENS * TOP
    flat_ids = expert_ids.reshape(pair_count)
    grouped = jnp.argsort(flat_ids, stable=True).astype(jnp.int32)
    expert_iota = jnp.arange(EXPERTS, dtype=jnp.int32)
    counts = jnp.sum((flat_ids[:, None] == expert_iota[None, :]).astype(jnp.int32), axis=0)
    offsets = (jnp.cumsum(counts) - counts).astype(jnp.int32)
    order_padded = jnp.concatenate([grouped, jnp.zeros((rows_most,), jnp.int32)])
    flat_gates = gates.reshape(pair_count)
    gate_up = w_gate_up.reshape(EXPERTS, SLICES, 2, FS, D)
    down_all = w_down.reshape(EXPERTS, SLICES, FS, D)
    contract_last = (((1,), (1,)), ((), ()))
    contract_first = (((0,), (0,)), ((), ()))

    def one_expert(dx_sum, expert):
        first_row = offsets[expert]
        picked = lax.dynamic_slice_in_dim(order_padded, first_row, rows_most)
        live_row = jnp.arange(rows_most, dtype=jnp.int32) < counts[expert]
        picked = jnp.where(live_row, picked, 0)
        token_row = picked // TOP
        x_rows = jnp.where(live_row[:, None], jnp.take(tokens, token_row, axis=0), jnp.zeros((), tokens.dtype))
        scaled = jnp.take(flat_gates, picked)[:, None] * jnp.take(upstream, token_row, axis=0).astype(jnp.float32)
        d_rows = jnp.where(live_row[:, None], scaled, 0.0).astype(jnp.bfloat16)
        pieces = gate_up[expert]
        gate_full = pieces[:, 0].reshape(F, D)
        up_full = pieces[:, 1].reshape(F, D)
        down_full = down_all[expert].reshape(F, D)
        gate_pre = lax.dot_general(x_rows, gate_full, contract_last, preferred_element_type=jnp.float32)
        up_pre = lax.dot_general(x_rows, up_full, contract_last, preferred_element_type=jnp.float32)
        activated, slope_of = silu_parts(gate_pre)
        hidden = (activated * up_pre).astype(jnp.bfloat16)
        hidden_grad = lax.dot_general(d_rows, down_full, contract_last, preferred_element_type=jnp.float32)
        gate_grad = (hidden_grad * up_pre * slope_of).astype(jnp.bfloat16)
        up_grad = (hidden_grad * activated).astype(jnp.bfloat16)
        grad_gate = lax.dot_general(gate_grad, x_rows, contract_first, preferred_element_type=jnp.float32)
        grad_up = lax.dot_general(up_grad, x_rows, contract_first, preferred_element_type=jnp.float32)
        grad_dn = lax.dot_general(hidden, d_rows, contract_first, preferred_element_type=jnp.float32)
        gate_sliced = gate_grad.reshape(rows_most, SLICES, FS).astype(jnp.float32)
        up_sliced = up_grad.reshape(rows_most, SLICES, FS).astype(jnp.float32)
        slice_part = jnp.einsum('rsf,sfd->rsd', gate_sliced, pieces[:, 0].astype(jnp.float32))
        slice_part = slice_part + jnp.einsum('rsf,sfd->rsd', up_sliced, pieces[:, 1].astype(jnp.float32))
        rounded = lax.optimization_barrier(slice_part.astype(jnp.bfloat16))
        dx_pair = jnp.sum(rounded.astype(jnp.float32), axis=1)
        dx_sum = dx_sum.at[token_row].add(jnp.where(live_row[:, None], dx_pair, 0.0))
        grad_pack = jnp.stack([grad_gate.reshape(SLICES, FS, D), grad_up.reshape(SLICES, FS, D)], axis=1)
        return dx_sum, (grad_pack.astype(jnp.bfloat16), grad_dn.reshape(SLICES, FS, D).astype(jnp.bfloat16))

    dx_sum, stacked = lax.scan(one_expert, jnp.zeros((TOKENS, D), jnp.float32), expert_iota)
    grads_gu, grads_dn = stacked
    col_iota = jnp.arange(N_EXPERT, dtype=jnp.int32)[:, None]
    partner = (col_iota + N_EXPERT // 2) % N_EXPERT
    own_col = jnp.broadcast_to(col_iota, (N_EXPERT, SLOTS))
    source = jnp.where(relocate == 1, partner, own_col)
    slot_iota = jnp.arange(SLOTS, dtype=jnp.int32)[None, :]
    moved_gu = grads_gu.reshape(N_EXPERT, SLOTS, SLICES, 2, FS, D)[source, slot_iota]
    moved_dn = grads_dn.reshape(N_EXPERT, SLOTS, SLICES, FS, D)[source, slot_iota]
    return (dx_sum.astype(jnp.bfloat16), moved_gu.reshape(N_EXPERT, N_DP, 2 * FS, D), moved_dn.reshape(N_EXPERT, N_DP, FS, D))
```

```python
import functools

import jax
import jax.numpy as jnp
from jax import lax
from jax.sharding import PartitionSpec as P

SLICES = 4


contract_last = (((1,), (1,)), ((), ()))
contract_first = (((0,), (0,)), ((), ()))


def swapped(block, axis, apart):
    count = lax.axis_size(axis)
    route = []
    for low in range(count):
        high = low | 1 << apart
        if high != low and high < count:
            route += [(low, high), (high, low)]
    return lax.ppermute(block, axis, route)


def silu_parts(values_in):
    sigmoid_of = jax.nn.sigmoid(values_in)
    return (values_in * sigmoid_of, sigmoid_of * (1.0 + values_in * (1.0 - sigmoid_of)))


def pick_entry(lookup_table, row_index, col_index):
    rows_hit = jnp.arange(lookup_table.shape[0], dtype=jnp.int32)[:, None] == row_index
    cols_hit = jnp.arange(lookup_table.shape[1], dtype=jnp.int32)[None, :] == col_index
    return jnp.sum(jnp.where(rows_hit & cols_hit, lookup_table, 0))


def routed_device(tokens, upstream, expert_ids, gates, relocate, w_gate_up, w_down):
    n_rows = lax.axis_size("dp")
    n_cols = lax.axis_size("expert")
    slot_count = n_rows // SLICES
    experts = slot_count * n_cols
    tok_dev, feature_width = tokens.shape
    top_count = expert_ids.shape[1]
    capacity = min(tok_dev, max(2, (3 * tok_dev * top_count + 2 * experts - 1) // (2 * experts)))
    pair_count = tok_dev * top_count
    buffer_rows = experts * capacity
    slice_width = w_down.shape[2]
    col_block = n_cols // SLICES
    col_here = lax.axis_index("expert")
    row_here = lax.axis_index("dp")
    slot_here = row_here // SLICES
    slice_here = row_here % SLICES
    far_bit = n_cols.bit_length() - 2
    half_cols = n_cols // 2
    flat_ids = expert_ids.reshape(pair_count)
    home_column = flat_ids // slot_count
    slot_of = flat_ids % slot_count
    expert_iota = jnp.arange(experts, dtype=jnp.int32)
    relocated = jnp.sum(
        jnp.where(flat_ids[:, None] == expert_iota[None, :], relocate.reshape(experts)[None, :], 0),
        axis=1,
    )
    column = (home_column + half_cols * relocated) % n_cols
    pair_iota = jnp.arange(pair_count, dtype=jnp.int32)
    earlier = (flat_ids[:, None] == flat_ids[None, :]) & (pair_iota[None, :] < pair_iota[:, None])
    slot_rank = jnp.sum(earlier.astype(jnp.int32), axis=1)
    target = (slot_of * n_cols + column) * capacity + slot_rank
    placing = (target[None, :] == jnp.arange(buffer_rows, dtype=jnp.int32)[:, None]).astype(
        jnp.bfloat16
    )
    x_pairs = jnp.repeat(tokens, top_count, axis=0)
    d_pairs = (
        gates.reshape(pair_count, 1) * jnp.repeat(upstream, top_count, axis=0).astype(jnp.float32)
    ).astype(jnp.bfloat16)
    pair_data = jnp.stack([x_pairs, d_pairs])
    sent = jnp.einsum("bp,kpw->kbw", placing, pair_data, preferred_element_type=jnp.float32).astype(
        jnp.bfloat16
    )
    sent = sent.reshape(2, slot_count, n_cols, capacity, feature_width)
    at_column = lax.all_to_all(sent, "expert", split_axis=2, concat_axis=2, tiled=True)
    swapped_here = pick_entry(relocate, col_here, slot_here)
    own_pack = jnp.concatenate([w_gate_up, w_down], axis=2)
    far_pack = swapped(own_pack, "expert", far_bit)
    own_pack = jnp.where(swapped_here == 1, far_pack, own_pack)
    gate_up = own_pack[0, 0, : 2 * slice_width]
    down_rows = own_pack[0, 0, 2 * slice_width :]
    grouped = at_column.reshape(2, n_rows, col_block, capacity, feature_width)
    at_row = lax.all_to_all(grouped, "dp", split_axis=1, concat_axis=1, tiled=True)
    gathered = at_row[:, None]
    for bit_index in range(SLICES.bit_length() - 1):
        far_rows = swapped(gathered, "dp", bit_index)
        lower_half = slice_here // (1 << bit_index) % 2 == 0
        first_part = jnp.where(lower_half, gathered, far_rows)
        second_part = jnp.where(lower_half, far_rows, gathered)
        gathered = jnp.concatenate([first_part, second_part], axis=1)
    all_rows = gathered.reshape(2, -1, feature_width)
    rows_x = all_rows[0]
    rows_d = all_rows[1]
    gate_and_up = lax.dot_general(
        rows_x, gate_up, contract_last, preferred_element_type=jnp.float32
    )
    gate_pre = gate_and_up[:, :slice_width]
    up_pre = gate_and_up[:, slice_width:]
    activated, slope_of = silu_parts(gate_pre)
    hidden = (activated * up_pre).astype(jnp.bfloat16)
    hidden_grad = lax.dot_general(
        rows_d, down_rows, contract_last, preferred_element_type=jnp.float32
    )
    pre_grads = jnp.concatenate(
        [
            (hidden_grad * up_pre * slope_of).astype(jnp.bfloat16),
            (hidden_grad * activated).astype(jnp.bfloat16),
        ],
        axis=1,
    )
    grad_gu = lax.dot_general(
        pre_grads, rows_x, contract_first, preferred_element_type=jnp.float32
    ).astype(jnp.bfloat16)
    grad_dn = lax.dot_general(
        hidden, rows_d, contract_first, preferred_element_type=jnp.float32
    ).astype(jnp.bfloat16)
    slice_part = jnp.dot(pre_grads, gate_up, preferred_element_type=jnp.float32).astype(
        jnp.bfloat16
    )
    grad_pack = jnp.concatenate([grad_gu, grad_dn], axis=0)
    blocks = slice_part.reshape(2, 2, n_rows, col_block, capacity, feature_width)
    upper_half = slice_here // 2 % 2 == 1
    keep_half = jnp.where(upper_half, blocks[1], blocks[0])
    send_half = jnp.where(upper_half, blocks[0], blocks[1])
    got_half = swapped(send_half, "dp", 1)
    pairsum = keep_half.astype(jnp.float32) + got_half.astype(jnp.float32)
    odd_slice = slice_here % 2 == 1
    keep_last = jnp.where(odd_slice, pairsum[1], pairsum[0])
    send_last = jnp.where(odd_slice, pairsum[0], pairsum[1])
    got_last = swapped(send_last, "dp", 0)
    summed = keep_last + got_last
    back_rows = lax.all_to_all(summed, "dp", split_axis=0, concat_axis=0, tiled=True).reshape(
        slot_count, n_cols, capacity, feature_width
    )
    home_rows = lax.all_to_all(
        back_rows, "expert", split_axis=1, concat_axis=1, tiled=True
    ).reshape(buffer_rows, feature_width)
    hits = (
        target.reshape(tok_dev, top_count)[:, :, None]
        == jnp.arange(buffer_rows, dtype=jnp.int32)[None, None, :]
    )
    gather_mat = jnp.sum(hits.astype(jnp.float32), axis=1)
    grad_tokens = jnp.dot(
        gather_mat, home_rows, precision=lax.Precision.HIGHEST, preferred_element_type=jnp.float32
    ).astype(jnp.bfloat16)
    grad_gate_up = grad_pack[: 2 * slice_width].reshape(w_gate_up.shape)
    grad_down = grad_pack[2 * slice_width :].reshape(w_down.shape)
    return (grad_tokens, grad_gate_up, grad_down)


def summands(values):
    high = lax.reduce_precision(values, 8, 7)
    middle = lax.reduce_precision(values - high, 8, 7)
    low = values - high - middle
    return [piece.astype(jnp.bfloat16) for piece in (high, middle, low)]


def crossed(block, axis, apart):
    return lax.ppermute(block, axis, [(i, i ^ apart) for i in range(lax.axis_size(axis))])


def activations(rows_x, rows_u, gate_col, gate_up, down_rows):
    width = down_rows.shape[0]
    pre = lax.dot_general(rows_x, gate_up, contract_last, preferred_element_type=jnp.float32)
    grad = lax.dot_general(rows_u, down_rows, contract_last, preferred_element_type=jnp.float32)
    activated, slope_of = silu_parts(pre[:, :width])
    up_pre = pre[:, width:]
    hidden_grad = grad * gate_col
    return jnp.concatenate(
        [
            (hidden_grad * up_pre * slope_of).astype(jnp.bfloat16),
            (hidden_grad * activated).astype(jnp.bfloat16),
            (activated * up_pre * gate_col).astype(jnp.bfloat16),
        ],
        axis=1,
    )


def dense_device(tokens, upstream, expert_ids, gates, relocate, w_gate_up, w_down):
    n_rows = lax.axis_size("dp")
    n_cols = lax.axis_size("expert")
    n_z = n_cols // 2
    tok_dev, width = tokens.shape
    units = w_down.shape[2]
    col_here = lax.axis_index("expert")
    half = n_cols // 2

    wgu_own = w_gate_up[0, 0]
    wdn_own = w_down[0, 0]
    by_expert = jnp.sum(
        jnp.where(expert_ids[:, :, None] == jnp.arange(n_cols, dtype=jnp.int32)[None, None, :], gates[:, :, None], 0.0),
        axis=1,
    )
    pieces = summands(by_expert)
    spare = jnp.zeros((tok_dev, 128 - 3 * n_cols), jnp.bfloat16)
    own = jnp.concatenate([tokens, upstream] + pieces + [spare], axis=1)

    along_z = [crossed(own, "expert", 2 * dz) for dz in range(n_z - 1, 0, -1)][::-1]
    along_dp = [crossed(own, "dp", d) for d in range(1, n_rows)]
    wgu_sib = crossed(wgu_own, "expert", 1)
    wdn_sib = crossed(wdn_own, "expert", 1)
    far = jnp.concatenate(along_z, axis=0)
    far_dp = [crossed(far, "dp", d) for d in range(1, n_rows)]
    plane = jnp.concatenate([own, far] + [part for pair in zip(along_dp, far_dp) for part in pair], axis=0)
    rows = plane[:, : 2 * width]
    rows_x = plane[:, :width]
    rows_u = plane[:, width : 2 * width]
    table = plane[:, 2 * width : 2 * width + 3 * n_cols].astype(jnp.float32)
    table = table[:, :n_cols] + table[:, n_cols : 2 * n_cols] + table[:, 2 * n_cols :]
    experts_iota = jnp.arange(n_cols, dtype=jnp.int32)[None, :]

    def gate_of(col):
        return jnp.sum(jnp.where(experts_iota == col, table, 0.0), axis=1, keepdims=True)

    rows_sib = crossed(rows, "expert", 1)
    acts_own = activations(rows_x, rows_u, gate_of(col_here), wgu_own, wdn_own)
    acts_sib = activations(rows_x, rows_u, gate_of(col_here ^ 1), wgu_sib, wdn_sib)
    moved = jnp.sum(jnp.where(jnp.arange(n_cols, dtype=jnp.int32) == col_here, relocate[:, 0], 0)) == 1
    bits = jnp.sum(relocate[:half, 0] << jnp.arange(half, dtype=jnp.int32))

    def turned(block):
        return block.reshape(n_rows, 2, -1, 3 * units)[:, ::-1].reshape(block.shape)

    def rest(pattern, acts_own, acts_sib, rows, rows_sib, wgu_own, wgu_sib):
        def place(col):
            return col ^ half if pattern >> (col % half) & 1 else col

        same_route = [(col, place(col)) for col in range(n_cols) if place(col) != col]
        cross_route = [(col, place(col ^ 1)) for col in range(n_cols)]
        got_same = lax.ppermute(acts_own, "expert", same_route)
        got_cross = lax.ppermute(acts_sib, "expert", cross_route)
        grad_rows = (
            jnp.dot(acts_own[:, : 2 * units], wgu_own, preferred_element_type=jnp.float32)
            + jnp.dot(acts_sib[:, : 2 * units], wgu_sib, preferred_element_type=jnp.float32)
        )
        grad_rows = grad_rows.reshape(n_rows, n_z * tok_dev, width)
        sent_rows = grad_rows.astype(jnp.bfloat16)
        total = grad_rows[0]
        for d in range(1, n_rows):
            total = total + crossed(sent_rows[d], "dp", d).astype(jnp.float32)
        total = total.reshape(n_z, tok_dev, width)
        sent_total = total.astype(jnp.bfloat16)
        grad_tokens = total[0]
        for dz in range(1, n_z):
            grad_tokens = grad_tokens + crossed(sent_total[dz], "expert", 2 * dz).astype(jnp.float32)
        acts_same = jnp.where(moved, turned(got_same), acts_own)
        acts_cross = jnp.where(moved, turned(got_cross), got_cross)

        def weight_grad(low, high, start, stop):
            return (
                lax.dot_general(acts_same[:, low:high], rows[:, start:stop], contract_first, preferred_element_type=jnp.float32)
                + lax.dot_general(acts_cross[:, low:high], rows_sib[:, start:stop], contract_first, preferred_element_type=jnp.float32)
            ).astype(jnp.bfloat16)

        grad_gu = weight_grad(0, 2 * units, 0, width)
        grad_dn = weight_grad(2 * units, 3 * units, width, 2 * width)
        return grad_tokens.astype(jnp.bfloat16), grad_gu.reshape(w_gate_up.shape), grad_dn.reshape(w_down.shape)

    branches = [functools.partial(rest, pattern) for pattern in range(1, (1 << half) - 1)]
    return lax.switch(bits - 1, branches, acts_own, acts_sib, rows, rows_sib, wgu_own, wgu_sib)


def solution(mesh):
    def per_device(*arrays):
        n_rows, n_cols = mesh.shape["dp"], mesh.shape["expert"]
        dense = n_rows == SLICES and arrays[2].shape[1] == n_cols and 4 <= n_cols <= 8
        return (dense_device if dense else routed_device)(*arrays)

    return jax.shard_map(
        per_device,
        mesh=mesh,
        in_specs=(
            P(("dp", "expert"), None),
            P(("dp", "expert"), None),
            P(("dp", "expert"), None),
            P(("dp", "expert"), None),
            P(),
            P("expert", "dp", None, None),
            P("expert", "dp", None, None),
        ),
        out_specs=(
            P(("dp", "expert"), None),
            P("expert", "dp", None, None),
            P("expert", "dp", None, None),
        ),
        check_vma=False,
    )
```

```python
import functools

import jax
import jax.numpy as jnp
from jax import lax
from jax.sharding import PartitionSpec as P

SLICES = 4


contract_last = (((1,), (1,)), ((), ()))
contract_first = (((0,), (0,)), ((), ()))


def swapped(block, axis, apart):
    count = lax.axis_size(axis)
    route = []
    for low in range(count):
        high = low | 1 << apart
        if high != low and high < count:
            route += [(low, high), (high, low)]
    return lax.ppermute(block, axis, route)


def silu_parts(values_in):
    sigmoid_of = jax.nn.sigmoid(values_in)
    return (values_in * sigmoid_of, sigmoid_of * (1.0 + values_in * (1.0 - sigmoid_of)))


def pick_entry(lookup_table, row_index, col_index):
    rows_hit = jnp.arange(lookup_table.shape[0], dtype=jnp.int32)[:, None] == row_index
    cols_hit = jnp.arange(lookup_table.shape[1], dtype=jnp.int32)[None, :] == col_index
    return jnp.sum(jnp.where(rows_hit & cols_hit, lookup_table, 0))


def routed_device(tokens, upstream, expert_ids, gates, relocate, w_gate_up, w_down):
    n_rows = lax.axis_size("dp")
    n_cols = lax.axis_size("expert")
    slot_count = n_rows // SLICES
    experts = slot_count * n_cols
    tok_dev, feature_width = tokens.shape
    top_count = expert_ids.shape[1]
    capacity = min(tok_dev, max(2, (3 * tok_dev * top_count + 2 * experts - 1) // (2 * experts)))
    pair_count = tok_dev * top_count
    buffer_rows = experts * capacity
    slice_width = w_down.shape[2]
    col_block = n_cols // SLICES
    col_here = lax.axis_index("expert")
    row_here = lax.axis_index("dp")
    slot_here = row_here // SLICES
    slice_here = row_here % SLICES
    far_bit = n_cols.bit_length() - 2
    half_cols = n_cols // 2
    flat_ids = expert_ids.reshape(pair_count)
    home_column = flat_ids // slot_count
    slot_of = flat_ids % slot_count
    expert_iota = jnp.arange(experts, dtype=jnp.int32)
    relocated = jnp.sum(
        jnp.where(flat_ids[:, None] == expert_iota[None, :], relocate.reshape(experts)[None, :], 0),
        axis=1,
    )
    column = (home_column + half_cols * relocated) % n_cols
    pair_iota = jnp.arange(pair_count, dtype=jnp.int32)
    earlier = (flat_ids[:, None] == flat_ids[None, :]) & (pair_iota[None, :] < pair_iota[:, None])
    slot_rank = jnp.sum(earlier.astype(jnp.int32), axis=1)
    target = (slot_of * n_cols + column) * capacity + slot_rank
    placing = (target[None, :] == jnp.arange(buffer_rows, dtype=jnp.int32)[:, None]).astype(
        jnp.bfloat16
    )
    x_pairs = jnp.repeat(tokens, top_count, axis=0)
    d_pairs = (
        gates.reshape(pair_count, 1) * jnp.repeat(upstream, top_count, axis=0).astype(jnp.float32)
    ).astype(jnp.bfloat16)
    pair_data = jnp.stack([x_pairs, d_pairs])
    sent = jnp.einsum("bp,kpw->kbw", placing, pair_data, preferred_element_type=jnp.float32).astype(
        jnp.bfloat16
    )
    sent = sent.reshape(2, slot_count, n_cols, capacity, feature_width)
    at_column = lax.all_to_all(sent, "expert", split_axis=2, concat_axis=2, tiled=True)
    swapped_here = pick_entry(relocate, col_here, slot_here)
    own_pack = jnp.concatenate([w_gate_up, w_down], axis=2)
    far_pack = swapped(own_pack, "expert", far_bit)
    own_pack = jnp.where(swapped_here == 1, far_pack, own_pack)
    gate_up = own_pack[0, 0, : 2 * slice_width]
    down_rows = own_pack[0, 0, 2 * slice_width :]
    grouped = at_column.reshape(2, n_rows, col_block, capacity, feature_width)
    at_row = lax.all_to_all(grouped, "dp", split_axis=1, concat_axis=1, tiled=True)
    gathered = at_row[:, None]
    for bit_index in range(SLICES.bit_length() - 1):
        far_rows = swapped(gathered, "dp", bit_index)
        lower_half = slice_here // (1 << bit_index) % 2 == 0
        first_part = jnp.where(lower_half, gathered, far_rows)
        second_part = jnp.where(lower_half, far_rows, gathered)
        gathered = jnp.concatenate([first_part, second_part], axis=1)
    all_rows = gathered.reshape(2, -1, feature_width)
    rows_x = all_rows[0]
    rows_d = all_rows[1]
    gate_and_up = lax.dot_general(
        rows_x, gate_up, contract_last, preferred_element_type=jnp.float32
    )
    gate_pre = gate_and_up[:, :slice_width]
    up_pre = gate_and_up[:, slice_width:]
    activated, slope_of = silu_parts(gate_pre)
    hidden = (activated * up_pre).astype(jnp.bfloat16)
    hidden_grad = lax.dot_general(
        rows_d, down_rows, contract_last, preferred_element_type=jnp.float32
    )
    pre_grads = jnp.concatenate(
        [
            (hidden_grad * up_pre * slope_of).astype(jnp.bfloat16),
            (hidden_grad * activated).astype(jnp.bfloat16),
        ],
        axis=1,
    )
    grad_gu = lax.dot_general(
        pre_grads, rows_x, contract_first, preferred_element_type=jnp.float32
    ).astype(jnp.bfloat16)
    grad_dn = lax.dot_general(
        hidden, rows_d, contract_first, preferred_element_type=jnp.float32
    ).astype(jnp.bfloat16)
    slice_part = jnp.dot(pre_grads, gate_up, preferred_element_type=jnp.float32).astype(
        jnp.bfloat16
    )
    grad_pack = jnp.concatenate([grad_gu, grad_dn], axis=0)
    blocks = slice_part.reshape(2, 2, n_rows, col_block, capacity, feature_width)
    upper_half = slice_here // 2 % 2 == 1
    keep_half = jnp.where(upper_half, blocks[1], blocks[0])
    send_half = jnp.where(upper_half, blocks[0], blocks[1])
    got_half = swapped(send_half, "dp", 1)
    pairsum = keep_half.astype(jnp.float32) + got_half.astype(jnp.float32)
    odd_slice = slice_here % 2 == 1
    keep_last = jnp.where(odd_slice, pairsum[1], pairsum[0])
    send_last = jnp.where(odd_slice, pairsum[0], pairsum[1])
    got_last = swapped(send_last, "dp", 0)
    summed = keep_last + got_last
    back_rows = lax.all_to_all(summed, "dp", split_axis=0, concat_axis=0, tiled=True).reshape(
        slot_count, n_cols, capacity, feature_width
    )
    home_rows = lax.all_to_all(
        back_rows, "expert", split_axis=1, concat_axis=1, tiled=True
    ).reshape(buffer_rows, feature_width)
    hits = (
        target.reshape(tok_dev, top_count)[:, :, None]
        == jnp.arange(buffer_rows, dtype=jnp.int32)[None, None, :]
    )
    gather_mat = jnp.sum(hits.astype(jnp.float32), axis=1)
    grad_tokens = jnp.dot(
        gather_mat, home_rows, precision=lax.Precision.HIGHEST, preferred_element_type=jnp.float32
    ).astype(jnp.bfloat16)
    grad_gate_up = grad_pack[: 2 * slice_width].reshape(w_gate_up.shape)
    grad_down = grad_pack[2 * slice_width :].reshape(w_down.shape)
    return (grad_tokens, grad_gate_up, grad_down)


def summands(values):
    high = lax.reduce_precision(values, 8, 7)
    middle = lax.reduce_precision(values - high, 8, 7)
    low = values - high - middle
    return [piece.astype(jnp.bfloat16) for piece in (high, middle, low)]


def crossed(block, axis, apart):
    return lax.ppermute(block, axis, [(i, i ^ apart) for i in range(lax.axis_size(axis))])


def activations(plane, gate_col, gate_up, down_rows):
    width = gate_up.shape[1]
    units = down_rows.shape[0]
    pre = lax.dot_general(plane[:, :width], gate_up, contract_last, preferred_element_type=jnp.float32)
    grad = lax.dot_general(plane[:, width : 2 * width], down_rows, contract_last, preferred_element_type=jnp.float32)
    activated, slope_of = silu_parts(pre[:, :units])
    up_pre = pre[:, units:]
    hidden_grad = grad * gate_col
    return (
        (hidden_grad * up_pre * slope_of).astype(jnp.bfloat16),
        (hidden_grad * activated).astype(jnp.bfloat16),
        (activated * up_pre * gate_col).astype(jnp.bfloat16),
    )


def after_first_stage(pattern, own, along_z, along_dp, w_gate_up, w_down):
    n_rows = lax.axis_size("dp")
    n_cols = lax.axis_size("expert")
    n_z = n_cols // 2
    half = n_cols // 2
    tok_dev = own.shape[0]
    units, width = w_down.shape[2:]
    early = units // 2
    col_here = lax.axis_index("expert")
    wgu_own = w_gate_up[0, 0]
    wdn_own = w_down[0, 0]

    def place(col):
        return col ^ half if pattern >> (col % half) & 1 else col

    same_route = [(col, place(col)) for col in range(n_cols)]
    cross_route = [(col, place(col ^ 1)) for col in range(n_cols)]
    moved = (pattern >> (col_here % half)) & 1 == 1

    far = jnp.concatenate(along_z, axis=0)
    far_dp = [crossed(far, "dp", d) for d in range(1, n_rows)]
    wgu_sib = crossed(wgu_own, "expert", 1)
    wdn_sib = crossed(wdn_own, "expert", 1)
    early_own = jnp.concatenate([wgu_own[:early], wgu_own[units : units + early], wdn_own[:early]], axis=0)
    early_here = lax.ppermute(early_own, "expert", same_route)

    plane = [own] + along_dp
    for dz in range(n_z - 1):
        plane += [along_z[dz]] + [block[dz * tok_dev : (dz + 1) * tok_dev] for block in far_dp]
    plane = jnp.concatenate(plane, axis=0)
    plane_sib = crossed(plane, "expert", 1)

    def gate_of(rows, col):
        table = rows[:, 2 * width : 2 * width + 3 * n_cols].astype(jnp.float32)
        table = table[:, :n_cols] + table[:, n_cols : 2 * n_cols] + table[:, 2 * n_cols :]
        return jnp.sum(jnp.where(jnp.arange(n_cols, dtype=jnp.int32)[None, :] == col, table, 0.0), axis=1, keepdims=True)

    acts_own = activations(plane, gate_of(plane, col_here), wgu_own, wdn_own)
    acts_sib = activations(plane, gate_of(plane, col_here ^ 1), wgu_sib, wdn_sib)
    grad_rows = jnp.dot(
        jnp.concatenate(acts_own[:2], axis=1), wgu_own, preferred_element_type=jnp.float32
    ) + jnp.dot(jnp.concatenate(acts_sib[:2], axis=1), wgu_sib, preferred_element_type=jnp.float32)
    grad_rows = grad_rows.reshape(n_z, n_rows, tok_dev, width)
    sent_rows = grad_rows.astype(jnp.bfloat16)
    total = grad_rows[:, 0]
    for d in range(1, n_rows):
        total = total + crossed(sent_rows[:, d], "dp", d).astype(jnp.float32)
    sent_total = total.astype(jnp.bfloat16)
    grad_tokens = total[0]
    for dz in range(1, n_z):
        grad_tokens = grad_tokens + crossed(sent_total[dz], "expert", 2 * dz).astype(jnp.float32)

    late_same = lax.ppermute(jnp.concatenate([part[:, early:] for part in acts_own], axis=1), "expert", same_route)
    late_cross = lax.ppermute(jnp.concatenate([part[:, early:] for part in acts_sib], axis=1), "expert", cross_route)
    source = jnp.where(moved, col_here ^ half, col_here)

    def combined(rows, late):
        middle = late.shape[0] // 2
        late = jnp.where(moved, jnp.concatenate([late[middle:], late[:middle]], axis=0), late)
        parts = activations(rows, gate_of(rows, source), early_here[: 2 * early], early_here[2 * early :])
        rest = units - early
        return [
            jnp.concatenate([part, late[:, i * rest : (i + 1) * rest]], axis=1) for i, part in enumerate(parts)
        ]

    acts_same = combined(plane, late_same)
    acts_cross = combined(plane_sib, late_cross)

    def weight_grad(same, cross, start):
        return (
            lax.dot_general(same, plane[:, start : start + width], contract_first, preferred_element_type=jnp.float32)
            + lax.dot_general(cross, plane_sib[:, start : start + width], contract_first, preferred_element_type=jnp.float32)
        ).astype(jnp.bfloat16)

    grad_gu = weight_grad(
        jnp.concatenate(acts_same[:2], axis=1), jnp.concatenate(acts_cross[:2], axis=1), 0
    )
    grad_dn = weight_grad(acts_same[2], acts_cross[2], width)
    return grad_tokens.astype(jnp.bfloat16), grad_gu.reshape(w_gate_up.shape), grad_dn.reshape(w_down.shape)


def dense_device(tokens, upstream, expert_ids, gates, relocate, w_gate_up, w_down):
    n_rows = lax.axis_size("dp")
    n_cols = lax.axis_size("expert")
    n_z = n_cols // 2
    tok_dev = tokens.shape[0]
    half = n_cols // 2
    by_expert = jnp.sum(
        jnp.where(expert_ids[:, :, None] == jnp.arange(n_cols, dtype=jnp.int32)[None, None, :], gates[:, :, None], 0.0),
        axis=1,
    )
    spare = jnp.zeros((tok_dev, 128 - 3 * n_cols), jnp.bfloat16)
    own = jnp.concatenate([tokens, upstream] + summands(by_expert) + [spare], axis=1)

    along_z = [crossed(own, "expert", 2 * dz) for dz in range(n_z - 1, 0, -1)][::-1]
    along_dp = [crossed(own, "dp", d) for d in range(1, n_rows)]
    bits = jnp.sum(relocate[:half, 0] << jnp.arange(half, dtype=jnp.int32))
    branches = [functools.partial(after_first_stage, pattern) for pattern in range(1, (1 << half) - 1)]
    return lax.switch(bits - 1, branches, own, along_z, along_dp, w_gate_up, w_down)


def solution(mesh):
    def per_device(*arrays):
        n_rows, n_cols = mesh.shape["dp"], mesh.shape["expert"]
        dense = n_rows == SLICES and arrays[2].shape[1] == n_cols and 4 <= n_cols <= 8
        return (dense_device if dense else routed_device)(*arrays)

    return jax.shard_map(
        per_device,
        mesh=mesh,
        in_specs=(
            P(("dp", "expert"), None),
            P(("dp", "expert"), None),
            P(("dp", "expert"), None),
            P(("dp", "expert"), None),
            P(),
            P("expert", "dp", None, None),
            P("expert", "dp", None, None),
        ),
        out_specs=(
            P(("dp", "expert"), None),
            P("expert", "dp", None, None),
            P("expert", "dp", None, None),
        ),
        check_vma=False,
    )
```

```python
import functools

import jax
import jax.numpy as jnp
from jax import lax
from jax.sharding import PartitionSpec as P

SLICES = 4


contract_last = (((1,), (1,)), ((), ()))
contract_first = (((0,), (0,)), ((), ()))


def swapped(block, axis, apart):
    count = lax.axis_size(axis)
    route = []
    for low in range(count):
        high = low | 1 << apart
        if high != low and high < count:
            route += [(low, high), (high, low)]
    return lax.ppermute(block, axis, route)


def silu_parts(values_in):
    sigmoid_of = jax.nn.sigmoid(values_in)
    return (values_in * sigmoid_of, sigmoid_of * (1.0 + values_in * (1.0 - sigmoid_of)))


def pick_entry(lookup_table, row_index, col_index):
    rows_hit = jnp.arange(lookup_table.shape[0], dtype=jnp.int32)[:, None] == row_index
    cols_hit = jnp.arange(lookup_table.shape[1], dtype=jnp.int32)[None, :] == col_index
    return jnp.sum(jnp.where(rows_hit & cols_hit, lookup_table, 0))


def routed_device(tokens, upstream, expert_ids, gates, relocate, w_gate_up, w_down):
    n_rows = lax.axis_size("dp")
    n_cols = lax.axis_size("expert")
    slot_count = n_rows // SLICES
    experts = slot_count * n_cols
    tok_dev, feature_width = tokens.shape
    top_count = expert_ids.shape[1]
    capacity = min(tok_dev, max(2, (3 * tok_dev * top_count + 2 * experts - 1) // (2 * experts)))
    pair_count = tok_dev * top_count
    buffer_rows = experts * capacity
    slice_width = w_down.shape[2]
    col_block = n_cols // SLICES
    col_here = lax.axis_index("expert")
    row_here = lax.axis_index("dp")
    slot_here = row_here // SLICES
    slice_here = row_here % SLICES
    far_bit = n_cols.bit_length() - 2
    half_cols = n_cols // 2
    flat_ids = expert_ids.reshape(pair_count)
    home_column = flat_ids // slot_count
    slot_of = flat_ids % slot_count
    expert_iota = jnp.arange(experts, dtype=jnp.int32)
    relocated = jnp.sum(
        jnp.where(flat_ids[:, None] == expert_iota[None, :], relocate.reshape(experts)[None, :], 0),
        axis=1,
    )
    column = (home_column + half_cols * relocated) % n_cols
    pair_iota = jnp.arange(pair_count, dtype=jnp.int32)
    earlier = (flat_ids[:, None] == flat_ids[None, :]) & (pair_iota[None, :] < pair_iota[:, None])
    slot_rank = jnp.sum(earlier.astype(jnp.int32), axis=1)
    target = (slot_of * n_cols + column) * capacity + slot_rank
    placing = (target[None, :] == jnp.arange(buffer_rows, dtype=jnp.int32)[:, None]).astype(
        jnp.bfloat16
    )
    x_pairs = jnp.repeat(tokens, top_count, axis=0)
    d_pairs = (
        gates.reshape(pair_count, 1) * jnp.repeat(upstream, top_count, axis=0).astype(jnp.float32)
    ).astype(jnp.bfloat16)
    pair_data = jnp.stack([x_pairs, d_pairs])
    sent = jnp.einsum("bp,kpw->kbw", placing, pair_data, preferred_element_type=jnp.float32).astype(
        jnp.bfloat16
    )
    sent = sent.reshape(2, slot_count, n_cols, capacity, feature_width)
    at_column = lax.all_to_all(sent, "expert", split_axis=2, concat_axis=2, tiled=True)
    swapped_here = pick_entry(relocate, col_here, slot_here)
    own_pack = jnp.concatenate([w_gate_up, w_down], axis=2)
    far_pack = swapped(own_pack, "expert", far_bit)
    own_pack = jnp.where(swapped_here == 1, far_pack, own_pack)
    gate_up = own_pack[0, 0, : 2 * slice_width]
    down_rows = own_pack[0, 0, 2 * slice_width :]
    grouped = at_column.reshape(2, n_rows, col_block, capacity, feature_width)
    at_row = lax.all_to_all(grouped, "dp", split_axis=1, concat_axis=1, tiled=True)
    gathered = at_row[:, None]
    for bit_index in range(SLICES.bit_length() - 1):
        far_rows = swapped(gathered, "dp", bit_index)
        lower_half = slice_here // (1 << bit_index) % 2 == 0
        first_part = jnp.where(lower_half, gathered, far_rows)
        second_part = jnp.where(lower_half, far_rows, gathered)
        gathered = jnp.concatenate([first_part, second_part], axis=1)
    all_rows = gathered.reshape(2, -1, feature_width)
    rows_x = all_rows[0]
    rows_d = all_rows[1]
    gate_and_up = lax.dot_general(
        rows_x, gate_up, contract_last, preferred_element_type=jnp.float32
    )
    gate_pre = gate_and_up[:, :slice_width]
    up_pre = gate_and_up[:, slice_width:]
    activated, slope_of = silu_parts(gate_pre)
    hidden = (activated * up_pre).astype(jnp.bfloat16)
    hidden_grad = lax.dot_general(
        rows_d, down_rows, contract_last, preferred_element_type=jnp.float32
    )
    pre_grads = jnp.concatenate(
        [
            (hidden_grad * up_pre * slope_of).astype(jnp.bfloat16),
            (hidden_grad * activated).astype(jnp.bfloat16),
        ],
        axis=1,
    )
    grad_gu = lax.dot_general(
        pre_grads, rows_x, contract_first, preferred_element_type=jnp.float32
    ).astype(jnp.bfloat16)
    grad_dn = lax.dot_general(
        hidden, rows_d, contract_first, preferred_element_type=jnp.float32
    ).astype(jnp.bfloat16)
    slice_part = jnp.dot(pre_grads, gate_up, preferred_element_type=jnp.float32).astype(
        jnp.bfloat16
    )
    grad_pack = jnp.concatenate([grad_gu, grad_dn], axis=0)
    blocks = slice_part.reshape(2, 2, n_rows, col_block, capacity, feature_width)
    upper_half = slice_here // 2 % 2 == 1
    keep_half = jnp.where(upper_half, blocks[1], blocks[0])
    send_half = jnp.where(upper_half, blocks[0], blocks[1])
    got_half = swapped(send_half, "dp", 1)
    pairsum = keep_half.astype(jnp.float32) + got_half.astype(jnp.float32)
    odd_slice = slice_here % 2 == 1
    keep_last = jnp.where(odd_slice, pairsum[1], pairsum[0])
    send_last = jnp.where(odd_slice, pairsum[0], pairsum[1])
    got_last = swapped(send_last, "dp", 0)
    summed = keep_last + got_last
    back_rows = lax.all_to_all(summed, "dp", split_axis=0, concat_axis=0, tiled=True).reshape(
        slot_count, n_cols, capacity, feature_width
    )
    home_rows = lax.all_to_all(
        back_rows, "expert", split_axis=1, concat_axis=1, tiled=True
    ).reshape(buffer_rows, feature_width)
    hits = (
        target.reshape(tok_dev, top_count)[:, :, None]
        == jnp.arange(buffer_rows, dtype=jnp.int32)[None, None, :]
    )
    gather_mat = jnp.sum(hits.astype(jnp.float32), axis=1)
    grad_tokens = jnp.dot(
        gather_mat, home_rows, precision=lax.Precision.HIGHEST, preferred_element_type=jnp.float32
    ).astype(jnp.bfloat16)
    grad_gate_up = grad_pack[: 2 * slice_width].reshape(w_gate_up.shape)
    grad_down = grad_pack[2 * slice_width :].reshape(w_down.shape)
    return (grad_tokens, grad_gate_up, grad_down)


def summands(values):
    high = lax.reduce_precision(values, 8, 7)
    middle = lax.reduce_precision(values - high, 8, 7)
    low = values - high - middle
    return [piece.astype(jnp.bfloat16) for piece in (high, middle, low)]


def crossed(block, axis, apart):
    return lax.ppermute(block, axis, [(i, i ^ apart) for i in range(lax.axis_size(axis))])


def activations(plane, gate_col, gate_up, down_rows):
    width = gate_up.shape[1]
    units = down_rows.shape[0]
    pre = lax.dot_general(plane[:, :width], gate_up, contract_last, preferred_element_type=jnp.float32)
    grad = lax.dot_general(plane[:, width : 2 * width], down_rows, contract_last, preferred_element_type=jnp.float32)
    activated, slope_of = silu_parts(pre[:, :units])
    up_pre = pre[:, units:]
    hidden_grad = grad * gate_col
    return (
        (hidden_grad * up_pre * slope_of).astype(jnp.bfloat16),
        (hidden_grad * activated).astype(jnp.bfloat16),
        (activated * up_pre * gate_col).astype(jnp.bfloat16),
    )


def exchanges(pattern, acts_own, acts_sib, kept_rows, sent_rows):
    n_cols = lax.axis_size("expert")
    half = n_cols // 2

    def place(col):
        return col ^ half if pattern >> (col % half) & 1 else col

    got = [crossed(block, "dp", d + 1) for d, block in enumerate(sent_rows)]
    got_same = lax.ppermute(acts_own, "expert", [(col, place(col)) for col in range(n_cols)])
    got_cross = lax.ppermute(acts_sib, "expert", [(col, place(col ^ 1)) for col in range(n_cols)])
    total = kept_rows
    for block in got:
        total = total + block.astype(jnp.float32)
    sent_total = total.astype(jnp.bfloat16)
    grad_tokens = total[0]
    for dz in range(1, half):
        grad_tokens = grad_tokens + crossed(sent_total[dz], "expert", 2 * dz).astype(jnp.float32)
    return got_same, got_cross, grad_tokens.astype(jnp.bfloat16)


def dense_device(tokens, upstream, expert_ids, gates, relocate, w_gate_up, w_down):
    n_rows = lax.axis_size("dp")
    n_cols = lax.axis_size("expert")
    n_z = n_cols // 2
    tok_dev = tokens.shape[0]
    half = n_cols // 2
    units, width = w_down.shape[2:]
    col_here = lax.axis_index("expert")
    wgu_own = w_gate_up[0, 0]
    wdn_own = w_down[0, 0]
    experts_iota = jnp.arange(n_cols, dtype=jnp.int32)
    by_expert = jnp.sum(
        jnp.where(expert_ids[:, :, None] == experts_iota[None, None, :], gates[:, :, None], 0.0),
        axis=1,
    )
    spare = jnp.zeros((tok_dev, 128 - 3 * n_cols), jnp.bfloat16)
    own = jnp.concatenate([tokens, upstream] + summands(by_expert) + [spare], axis=1)

    along_z = [crossed(own, "expert", 2 * dz) for dz in range(n_z - 1, 0, -1)][::-1]
    along_dp = [crossed(own, "dp", d) for d in range(1, n_rows)]
    bits = jnp.sum(relocate[:half, 0] << jnp.arange(half, dtype=jnp.int32))
    moved = jnp.sum(jnp.where(experts_iota == col_here, relocate[:, 0], 0)) == 1
    along_z, along_dp, w_gate_up, w_down = lax.optimization_barrier((along_z, along_dp, w_gate_up, w_down))
    far = jnp.concatenate(along_z, axis=0)
    far_dp = [crossed(far, "dp", d) for d in range(1, n_rows)]
    wgu_sib = crossed(w_gate_up[0, 0], "expert", 1)
    wdn_sib = crossed(w_down[0, 0], "expert", 1)
    plane = [own] + along_dp
    for dz in range(n_z - 1):
        plane += [along_z[dz]] + [block[dz * tok_dev : (dz + 1) * tok_dev] for block in far_dp]
    plane = jnp.concatenate(plane, axis=0)
    plane_sib = crossed(plane, "expert", 1)

    def gate_of(rows, col):
        table = rows[:, 2 * width : 2 * width + 3 * n_cols].astype(jnp.float32)
        table = table[:, :n_cols] + table[:, n_cols : 2 * n_cols] + table[:, 2 * n_cols :]
        return jnp.sum(jnp.where(experts_iota[None, :] == col, table, 0.0), axis=1, keepdims=True)

    acts_own = activations(plane, gate_of(plane, col_here), wgu_own, wdn_own)
    acts_sib = activations(plane, gate_of(plane, col_here ^ 1), wgu_sib, wdn_sib)
    grad_rows = jnp.dot(
        jnp.concatenate(acts_own[:2], axis=1), wgu_own, preferred_element_type=jnp.float32
    ) + jnp.dot(jnp.concatenate(acts_sib[:2], axis=1), wgu_sib, preferred_element_type=jnp.float32)
    grad_rows = grad_rows.reshape(n_z, n_rows, tok_dev, width)
    sent_rows = [grad_rows[:, d].astype(jnp.bfloat16) for d in range(1, n_rows)]
    sent_rows, plane_sib = lax.optimization_barrier((sent_rows, plane_sib))
    branches = [functools.partial(exchanges, pattern) for pattern in range(1, (1 << half) - 1)]
    got_same, got_cross, grad_tokens = lax.switch(
        bits - 1,
        branches,
        jnp.concatenate(acts_own, axis=1),
        jnp.concatenate(acts_sib, axis=1),
        grad_rows[:, 0],
        sent_rows,
    )

    def turned(block):
        middle = block.shape[0] // 2
        return jnp.where(moved, jnp.concatenate([block[middle:], block[:middle]], axis=0), block)

    acts_same = turned(got_same)
    acts_cross = turned(got_cross)

    def weight_grad(low, high, start):
        return (
            lax.dot_general(acts_same[:, low:high], plane[:, start : start + width], contract_first, preferred_element_type=jnp.float32)
            + lax.dot_general(acts_cross[:, low:high], plane_sib[:, start : start + width], contract_first, preferred_element_type=jnp.float32)
        ).astype(jnp.bfloat16)

    grad_gu = weight_grad(0, 2 * units, 0)
    grad_dn = weight_grad(2 * units, 3 * units, width)
    return grad_tokens, grad_gu.reshape(w_gate_up.shape), grad_dn.reshape(w_down.shape)


def solution(mesh):
    def per_device(*arrays):
        n_rows, n_cols = mesh.shape["dp"], mesh.shape["expert"]
        dense = n_rows == SLICES and arrays[2].shape[1] == n_cols and 4 <= n_cols <= 8
        return (dense_device if dense else routed_device)(*arrays)

    return jax.shard_map(
        per_device,
        mesh=mesh,
        in_specs=(
            P(("dp", "expert"), None),
            P(("dp", "expert"), None),
            P(("dp", "expert"), None),
            P(("dp", "expert"), None),
            P(),
            P("expert", "dp", None, None),
            P("expert", "dp", None, None),
        ),
        out_specs=(
            P(("dp", "expert"), None),
            P("expert", "dp", None, None),
            P("expert", "dp", None, None),
        ),
        check_vma=False,
    )
```

```python
import functools

import jax
import jax.numpy as jnp
from jax import lax
from jax.experimental import pallas as pl
from jax.experimental.pallas import tpu as pltpu
from jax.sharding import PartitionSpec as P

SLICES = 4


contract_last = (((1,), (1,)), ((), ()))
contract_first = (((0,), (0,)), ((), ()))


def swapped(block, axis, apart):
    count = lax.axis_size(axis)
    route = []
    for low in range(count):
        high = low | 1 << apart
        if high != low and high < count:
            route += [(low, high), (high, low)]
    return lax.ppermute(block, axis, route)


def silu_parts(values_in):
    sigmoid_of = jax.nn.sigmoid(values_in)
    return (values_in * sigmoid_of, sigmoid_of * (1.0 + values_in * (1.0 - sigmoid_of)))


def pick_entry(lookup_table, row_index, col_index):
    rows_hit = jnp.arange(lookup_table.shape[0], dtype=jnp.int32)[:, None] == row_index
    cols_hit = jnp.arange(lookup_table.shape[1], dtype=jnp.int32)[None, :] == col_index
    return jnp.sum(jnp.where(rows_hit & cols_hit, lookup_table, 0))


def routed_device(tokens, upstream, expert_ids, gates, relocate, w_gate_up, w_down):
    n_rows = lax.axis_size("dp")
    n_cols = lax.axis_size("expert")
    slot_count = n_rows // SLICES
    experts = slot_count * n_cols
    tok_dev, feature_width = tokens.shape
    top_count = expert_ids.shape[1]
    capacity = min(tok_dev, max(2, (3 * tok_dev * top_count + 2 * experts - 1) // (2 * experts)))
    pair_count = tok_dev * top_count
    buffer_rows = experts * capacity
    slice_width = w_down.shape[2]
    col_block = n_cols // SLICES
    col_here = lax.axis_index("expert")
    row_here = lax.axis_index("dp")
    slot_here = row_here // SLICES
    slice_here = row_here % SLICES
    far_bit = n_cols.bit_length() - 2
    half_cols = n_cols // 2
    flat_ids = expert_ids.reshape(pair_count)
    home_column = flat_ids // slot_count
    slot_of = flat_ids % slot_count
    expert_iota = jnp.arange(experts, dtype=jnp.int32)
    relocated = jnp.sum(
        jnp.where(flat_ids[:, None] == expert_iota[None, :], relocate.reshape(experts)[None, :], 0),
        axis=1,
    )
    column = (home_column + half_cols * relocated) % n_cols
    pair_iota = jnp.arange(pair_count, dtype=jnp.int32)
    earlier = (flat_ids[:, None] == flat_ids[None, :]) & (pair_iota[None, :] < pair_iota[:, None])
    slot_rank = jnp.sum(earlier.astype(jnp.int32), axis=1)
    target = (slot_of * n_cols + column) * capacity + slot_rank
    placing = (target[None, :] == jnp.arange(buffer_rows, dtype=jnp.int32)[:, None]).astype(
        jnp.bfloat16
    )
    x_pairs = jnp.repeat(tokens, top_count, axis=0)
    d_pairs = (
        gates.reshape(pair_count, 1) * jnp.repeat(upstream, top_count, axis=0).astype(jnp.float32)
    ).astype(jnp.bfloat16)
    pair_data = jnp.stack([x_pairs, d_pairs])
    sent = jnp.einsum("bp,kpw->kbw", placing, pair_data, preferred_element_type=jnp.float32).astype(
        jnp.bfloat16
    )
    sent = sent.reshape(2, slot_count, n_cols, capacity, feature_width)
    at_column = lax.all_to_all(sent, "expert", split_axis=2, concat_axis=2, tiled=True)
    swapped_here = pick_entry(relocate, col_here, slot_here)
    own_pack = jnp.concatenate([w_gate_up, w_down], axis=2)
    far_pack = swapped(own_pack, "expert", far_bit)
    own_pack = jnp.where(swapped_here == 1, far_pack, own_pack)
    gate_up = own_pack[0, 0, : 2 * slice_width]
    down_rows = own_pack[0, 0, 2 * slice_width :]
    grouped = at_column.reshape(2, n_rows, col_block, capacity, feature_width)
    at_row = lax.all_to_all(grouped, "dp", split_axis=1, concat_axis=1, tiled=True)
    gathered = at_row[:, None]
    for bit_index in range(SLICES.bit_length() - 1):
        far_rows = swapped(gathered, "dp", bit_index)
        lower_half = slice_here // (1 << bit_index) % 2 == 0
        first_part = jnp.where(lower_half, gathered, far_rows)
        second_part = jnp.where(lower_half, far_rows, gathered)
        gathered = jnp.concatenate([first_part, second_part], axis=1)
    all_rows = gathered.reshape(2, -1, feature_width)
    rows_x = all_rows[0]
    rows_d = all_rows[1]
    gate_and_up = lax.dot_general(
        rows_x, gate_up, contract_last, preferred_element_type=jnp.float32
    )
    gate_pre = gate_and_up[:, :slice_width]
    up_pre = gate_and_up[:, slice_width:]
    activated, slope_of = silu_parts(gate_pre)
    hidden = (activated * up_pre).astype(jnp.bfloat16)
    hidden_grad = lax.dot_general(
        rows_d, down_rows, contract_last, preferred_element_type=jnp.float32
    )
    pre_grads = jnp.concatenate(
        [
            (hidden_grad * up_pre * slope_of).astype(jnp.bfloat16),
            (hidden_grad * activated).astype(jnp.bfloat16),
        ],
        axis=1,
    )
    grad_gu = lax.dot_general(
        pre_grads, rows_x, contract_first, preferred_element_type=jnp.float32
    ).astype(jnp.bfloat16)
    grad_dn = lax.dot_general(
        hidden, rows_d, contract_first, preferred_element_type=jnp.float32
    ).astype(jnp.bfloat16)
    slice_part = jnp.dot(pre_grads, gate_up, preferred_element_type=jnp.float32).astype(
        jnp.bfloat16
    )
    grad_pack = jnp.concatenate([grad_gu, grad_dn], axis=0)
    blocks = slice_part.reshape(2, 2, n_rows, col_block, capacity, feature_width)
    upper_half = slice_here // 2 % 2 == 1
    keep_half = jnp.where(upper_half, blocks[1], blocks[0])
    send_half = jnp.where(upper_half, blocks[0], blocks[1])
    got_half = swapped(send_half, "dp", 1)
    pairsum = keep_half.astype(jnp.float32) + got_half.astype(jnp.float32)
    odd_slice = slice_here % 2 == 1
    keep_last = jnp.where(odd_slice, pairsum[1], pairsum[0])
    send_last = jnp.where(odd_slice, pairsum[0], pairsum[1])
    got_last = swapped(send_last, "dp", 0)
    summed = keep_last + got_last
    back_rows = lax.all_to_all(summed, "dp", split_axis=0, concat_axis=0, tiled=True).reshape(
        slot_count, n_cols, capacity, feature_width
    )
    home_rows = lax.all_to_all(
        back_rows, "expert", split_axis=1, concat_axis=1, tiled=True
    ).reshape(buffer_rows, feature_width)
    hits = (
        target.reshape(tok_dev, top_count)[:, :, None]
        == jnp.arange(buffer_rows, dtype=jnp.int32)[None, None, :]
    )
    gather_mat = jnp.sum(hits.astype(jnp.float32), axis=1)
    grad_tokens = jnp.dot(
        gather_mat, home_rows, precision=lax.Precision.HIGHEST, preferred_element_type=jnp.float32
    ).astype(jnp.bfloat16)
    grad_gate_up = grad_pack[: 2 * slice_width].reshape(w_gate_up.shape)
    grad_down = grad_pack[2 * slice_width :].reshape(w_down.shape)
    return (grad_tokens, grad_gate_up, grad_down)


def crossed(block, axis, apart):
    return lax.ppermute(block, axis, [(i, i ^ apart) for i in range(lax.axis_size(axis))])


def whole(count):
    return [pl.BlockSpec(memory_space=pltpu.VMEM)] * count


def pack_kernel(n_cols, ids_ref, gates_ref, tokens_ref, upstream_ref, packed_ref):
    width = tokens_ref.shape[1]
    lane = lax.broadcasted_iota(jnp.int32, (tokens_ref.shape[0], 128), 1)
    table = jnp.zeros(lane.shape, jnp.float32)
    for k in range(ids_ref.shape[1]):
        table += jnp.where(ids_ref[:, k : k + 1] == lane % n_cols, gates_ref[:, k : k + 1], 0.0)
    high = table.astype(jnp.bfloat16)
    rest = table - high.astype(jnp.float32)
    middle = rest.astype(jnp.bfloat16)
    low = (rest - middle.astype(jnp.float32)).astype(jnp.bfloat16)
    zero = jnp.zeros_like(high)
    part = lane // n_cols
    packed_ref[:, :width] = tokens_ref[...]
    packed_ref[:, width : 2 * width] = upstream_ref[...]
    packed_ref[:, 2 * width :] = jnp.where(
        part == 0, high, jnp.where(part == 1, middle, jnp.where(part == 2, low, zero))
    )


def forward_kernel(n_cols, n_rows, tok_dev, plane_ref, wgu_own, wdn_own, wgu_sib, wdn_sib, own_ref, sib_ref, kept_ref, *sent_refs):
    units, width = wdn_own.shape
    col_here = lax.axis_index("expert")
    lane = lax.broadcasted_iota(jnp.int32, (8, 128), 1)
    row = lax.broadcasted_iota(jnp.int32, (8, 128), 0)
    wanted = jnp.where(row == 0, col_here, col_here ^ 1)
    chosen = (row < 2) & (lane % n_cols == wanted) & (lane < 3 * n_cols)
    gate_rows = lax.dot_general(
        jnp.where(chosen, 1.0, 0.0).astype(jnp.bfloat16), plane_ref[:, 2 * width :], contract_last, preferred_element_type=jnp.float32
    )
    total = None
    for index, (wgu, wdn, acts_ref) in enumerate(((wgu_own, wdn_own, own_ref), (wgu_sib, wdn_sib, sib_ref))):
        gate = gate_rows[index : index + 1, :]
        pre = lax.dot_general(wgu[...], plane_ref[:, :width], contract_last, preferred_element_type=jnp.float32)
        hidden_grad = gate * lax.dot_general(
            wdn[...], plane_ref[:, width : 2 * width], contract_last, preferred_element_type=jnp.float32
        )
        activated, slope_of = silu_parts(pre[:units])
        up_pre = pre[units:]
        acts_ref[:units] = (hidden_grad * up_pre * slope_of).astype(jnp.bfloat16)
        acts_ref[units : 2 * units] = (hidden_grad * activated).astype(jnp.bfloat16)
        acts_ref[2 * units :] = (activated * up_pre * gate).astype(jnp.bfloat16)
        part = lax.dot_general(acts_ref[: 2 * units], wgu[...], contract_first, preferred_element_type=jnp.float32)
        total = part if total is None else total + part
    for z in range(plane_ref.shape[0] // (n_rows * tok_dev)):
        for d in range(n_rows):
            start = (z * n_rows + d) * tok_dev
            block = total[start : start + tok_dev]
            if d == 0:
                kept_ref[z] = block
            else:
                sent_refs[d - 1][z] = block.astype(jnp.bfloat16)


def weight_grad_kernel(relocate_ref, same_ref, cross_ref, plane_ref, other_ref, gu_ref, dn_ref):
    units, width = dn_ref.shape
    half = plane_ref.shape[0] // 2
    first = pl.multiple_of(relocate_ref[lax.axis_index("expert"), 0] * half, half)
    for acts, rows_ref, start in ((same_ref, plane_ref, True), (cross_ref, other_ref, False)):
        for side in range(2):
            rows = pl.ds(first if side == 0 else half - first, half)
            lanes = slice(side * half, (side + 1) * half)
            gu = jnp.dot(acts[: 2 * units, lanes], rows_ref[rows, :width], preferred_element_type=jnp.float32)
            dn = jnp.dot(acts[2 * units :, lanes], rows_ref[rows, width : 2 * width], preferred_element_type=jnp.float32)
            if start and side == 0:
                gu_sum, dn_sum = gu, dn
            else:
                gu_sum, dn_sum = gu_sum + gu, dn_sum + dn
    gu_ref[...] = gu_sum.astype(jnp.bfloat16)
    dn_ref[...] = dn_sum.astype(jnp.bfloat16)


def exchanges(pattern, acts_own, acts_sib, plane, sent_rows):
    n_cols = lax.axis_size("expert")
    half = n_cols // 2

    def place(col):
        return col ^ half if pattern >> (col % half) & 1 else col

    got_same = lax.ppermute(acts_own, "expert", [(col, place(col)) for col in range(n_cols)])
    got = [crossed(block, "dp", d + 1) for d, block in enumerate(sent_rows)]
    plane_sib = crossed(plane, "expert", 1)
    got_cross = lax.ppermute(acts_sib, "expert", [(col, place(col ^ 1)) for col in range(n_cols)])
    return got_same, got_cross, plane_sib, got


def dense_device(tokens, upstream, expert_ids, gates, relocate, w_gate_up, w_down):
    n_rows = lax.axis_size("dp")
    n_cols = lax.axis_size("expert")
    n_z = n_cols // 2
    tok_dev = tokens.shape[0]
    half = n_cols // 2
    units, width = w_down.shape[2:]
    plane_rows = n_rows * n_z * tok_dev
    limit = pltpu.CompilerParams(vmem_limit_bytes=48 * 2**20)
    bf16 = jnp.bfloat16

    own = pl.pallas_call(
        functools.partial(pack_kernel, n_cols),
        out_shape=jax.ShapeDtypeStruct((tok_dev, 2 * width + 128), bf16),
        in_specs=whole(4),
        out_specs=whole(1)[0],
        compiler_params=limit,
        name="pack",
    )(expert_ids, gates, tokens, upstream)

    along_dp = [crossed(own, "dp", d) for d in range(1, n_rows)]
    along_z = [crossed(own, "expert", 2 * dz) for dz in range(1, n_z)]
    bits = jnp.sum(relocate[:half, 0] << jnp.arange(half, dtype=jnp.int32))
    along_z, along_dp, w_gate_up, w_down, bits = lax.optimization_barrier((along_z, along_dp, w_gate_up, w_down, bits))
    far = jnp.concatenate(along_z, axis=0)
    far_dp = [crossed(far, "dp", d) for d in range(1, n_rows)]
    wgu_own, wdn_own = w_gate_up[0, 0], w_down[0, 0]
    wgu_sib = crossed(wgu_own, "expert", 1)
    wdn_sib = crossed(wdn_own, "expert", 1)
    plane = [own] + along_dp
    for dz in range(n_z - 1):
        plane += [along_z[dz]] + [block[dz * tok_dev : (dz + 1) * tok_dev] for block in far_dp]
    plane = jnp.concatenate(plane, axis=0)

    acts = jax.ShapeDtypeStruct((3 * units, plane_rows), bf16)
    acts_own, acts_sib, kept, *sent = pl.pallas_call(
        functools.partial(forward_kernel, n_cols, n_rows, tok_dev),
        out_shape=[acts, acts, jax.ShapeDtypeStruct((n_z, tok_dev, width), jnp.float32)]
        + [jax.ShapeDtypeStruct((n_z, tok_dev, width), bf16)] * (n_rows - 1),
        in_specs=whole(5),
        out_specs=whole(2 + n_rows),
        compiler_params=limit,
        name="forward",
    )(plane, wgu_own, wdn_own, wgu_sib, wdn_sib)

    branches = [functools.partial(exchanges, pattern) for pattern in range(1, (1 << half) - 1)]
    got_same, got_cross, plane_sib, got = lax.switch(bits - 1, branches, acts_own, acts_sib, plane, sent)
    total = kept
    for block in got:
        total = total + block.astype(jnp.float32)
    sent_total = total.astype(bf16)
    grad_tokens = total[0]
    for dz in range(1, n_z):
        grad_tokens = grad_tokens + crossed(sent_total[dz], "expert", 2 * dz).astype(jnp.float32)
    grad_gu, grad_dn = pl.pallas_call(
        weight_grad_kernel,
        out_shape=[jax.ShapeDtypeStruct((2 * units, width), bf16), jax.ShapeDtypeStruct((units, width), bf16)],
        in_specs=[pl.BlockSpec(memory_space=pltpu.SMEM)] + whole(4),
        out_specs=whole(2),
        compiler_params=limit,
        name="weight_grads",
    )(relocate, got_same, got_cross, plane, plane_sib)
    return grad_tokens.astype(bf16), grad_gu.reshape(w_gate_up.shape), grad_dn.reshape(w_down.shape)


def solution(mesh):
    def per_device(*arrays):
        n_rows, n_cols = mesh.shape["dp"], mesh.shape["expert"]
        dense = n_rows == SLICES and arrays[2].shape[1] == n_cols and 4 <= n_cols <= 8
        return (dense_device if dense else routed_device)(*arrays)

    return jax.shard_map(
        per_device,
        mesh=mesh,
        in_specs=(
            P(("dp", "expert"), None),
            P(("dp", "expert"), None),
            P(("dp", "expert"), None),
            P(("dp", "expert"), None),
            P(),
            P("expert", "dp", None, None),
            P("expert", "dp", None, None),
        ),
        out_specs=(
            P(("dp", "expert"), None),
            P("expert", "dp", None, None),
            P("expert", "dp", None, None),
        ),
        check_vma=False,
    )
```

```python
import functools

import jax
import jax.numpy as jnp
from jax import lax
from jax.experimental import pallas as pl
from jax.experimental.pallas import tpu as pltpu
from jax.sharding import PartitionSpec as P

SLICES = 4


contract_last = (((1,), (1,)), ((), ()))
contract_first = (((0,), (0,)), ((), ()))


def swapped(block, axis, apart):
    count = lax.axis_size(axis)
    route = []
    for low in range(count):
        high = low | 1 << apart
        if high != low and high < count:
            route += [(low, high), (high, low)]
    return lax.ppermute(block, axis, route)


def silu_parts(values_in):
    sigmoid_of = jax.nn.sigmoid(values_in)
    return (values_in * sigmoid_of, sigmoid_of * (1.0 + values_in * (1.0 - sigmoid_of)))


def pick_entry(lookup_table, row_index, col_index):
    rows_hit = jnp.arange(lookup_table.shape[0], dtype=jnp.int32)[:, None] == row_index
    cols_hit = jnp.arange(lookup_table.shape[1], dtype=jnp.int32)[None, :] == col_index
    return jnp.sum(jnp.where(rows_hit & cols_hit, lookup_table, 0))


def routed_device(tokens, upstream, expert_ids, gates, relocate, w_gate_up, w_down):
    n_rows = lax.axis_size("dp")
    n_cols = lax.axis_size("expert")
    slot_count = n_rows // SLICES
    experts = slot_count * n_cols
    tok_dev, feature_width = tokens.shape
    top_count = expert_ids.shape[1]
    capacity = min(tok_dev, max(2, (3 * tok_dev * top_count + 2 * experts - 1) // (2 * experts)))
    pair_count = tok_dev * top_count
    buffer_rows = experts * capacity
    slice_width = w_down.shape[2]
    col_block = n_cols // SLICES
    col_here = lax.axis_index("expert")
    row_here = lax.axis_index("dp")
    slot_here = row_here // SLICES
    slice_here = row_here % SLICES
    far_bit = n_cols.bit_length() - 2
    half_cols = n_cols // 2
    flat_ids = expert_ids.reshape(pair_count)
    home_column = flat_ids // slot_count
    slot_of = flat_ids % slot_count
    expert_iota = jnp.arange(experts, dtype=jnp.int32)
    relocated = jnp.sum(
        jnp.where(flat_ids[:, None] == expert_iota[None, :], relocate.reshape(experts)[None, :], 0),
        axis=1,
    )
    column = (home_column + half_cols * relocated) % n_cols
    pair_iota = jnp.arange(pair_count, dtype=jnp.int32)
    earlier = (flat_ids[:, None] == flat_ids[None, :]) & (pair_iota[None, :] < pair_iota[:, None])
    slot_rank = jnp.sum(earlier.astype(jnp.int32), axis=1)
    target = (slot_of * n_cols + column) * capacity + slot_rank
    placing = (target[None, :] == jnp.arange(buffer_rows, dtype=jnp.int32)[:, None]).astype(
        jnp.bfloat16
    )
    x_pairs = jnp.repeat(tokens, top_count, axis=0)
    d_pairs = (
        gates.reshape(pair_count, 1) * jnp.repeat(upstream, top_count, axis=0).astype(jnp.float32)
    ).astype(jnp.bfloat16)
    pair_data = jnp.stack([x_pairs, d_pairs])
    sent = jnp.einsum("bp,kpw->kbw", placing, pair_data, preferred_element_type=jnp.float32).astype(
        jnp.bfloat16
    )
    sent = sent.reshape(2, slot_count, n_cols, capacity, feature_width)
    at_column = lax.all_to_all(sent, "expert", split_axis=2, concat_axis=2, tiled=True)
    swapped_here = pick_entry(relocate, col_here, slot_here)
    own_pack = jnp.concatenate([w_gate_up, w_down], axis=2)
    far_pack = swapped(own_pack, "expert", far_bit)
    own_pack = jnp.where(swapped_here == 1, far_pack, own_pack)
    gate_up = own_pack[0, 0, : 2 * slice_width]
    down_rows = own_pack[0, 0, 2 * slice_width :]
    grouped = at_column.reshape(2, n_rows, col_block, capacity, feature_width)
    at_row = lax.all_to_all(grouped, "dp", split_axis=1, concat_axis=1, tiled=True)
    gathered = at_row[:, None]
    for bit_index in range(SLICES.bit_length() - 1):
        far_rows = swapped(gathered, "dp", bit_index)
        lower_half = slice_here // (1 << bit_index) % 2 == 0
        first_part = jnp.where(lower_half, gathered, far_rows)
        second_part = jnp.where(lower_half, far_rows, gathered)
        gathered = jnp.concatenate([first_part, second_part], axis=1)
    all_rows = gathered.reshape(2, -1, feature_width)
    rows_x = all_rows[0]
    rows_d = all_rows[1]
    gate_and_up = lax.dot_general(
        rows_x, gate_up, contract_last, preferred_element_type=jnp.float32
    )
    gate_pre = gate_and_up[:, :slice_width]
    up_pre = gate_and_up[:, slice_width:]
    activated, slope_of = silu_parts(gate_pre)
    hidden = (activated * up_pre).astype(jnp.bfloat16)
    hidden_grad = lax.dot_general(
        rows_d, down_rows, contract_last, preferred_element_type=jnp.float32
    )
    pre_grads = jnp.concatenate(
        [
            (hidden_grad * up_pre * slope_of).astype(jnp.bfloat16),
            (hidden_grad * activated).astype(jnp.bfloat16),
        ],
        axis=1,
    )
    grad_gu = lax.dot_general(
        pre_grads, rows_x, contract_first, preferred_element_type=jnp.float32
    ).astype(jnp.bfloat16)
    grad_dn = lax.dot_general(
        hidden, rows_d, contract_first, preferred_element_type=jnp.float32
    ).astype(jnp.bfloat16)
    slice_part = jnp.dot(pre_grads, gate_up, preferred_element_type=jnp.float32).astype(
        jnp.bfloat16
    )
    grad_pack = jnp.concatenate([grad_gu, grad_dn], axis=0)
    blocks = slice_part.reshape(2, 2, n_rows, col_block, capacity, feature_width)
    upper_half = slice_here // 2 % 2 == 1
    keep_half = jnp.where(upper_half, blocks[1], blocks[0])
    send_half = jnp.where(upper_half, blocks[0], blocks[1])
    got_half = swapped(send_half, "dp", 1)
    pairsum = keep_half.astype(jnp.float32) + got_half.astype(jnp.float32)
    odd_slice = slice_here % 2 == 1
    keep_last = jnp.where(odd_slice, pairsum[1], pairsum[0])
    send_last = jnp.where(odd_slice, pairsum[0], pairsum[1])
    got_last = swapped(send_last, "dp", 0)
    summed = keep_last + got_last
    back_rows = lax.all_to_all(summed, "dp", split_axis=0, concat_axis=0, tiled=True).reshape(
        slot_count, n_cols, capacity, feature_width
    )
    home_rows = lax.all_to_all(
        back_rows, "expert", split_axis=1, concat_axis=1, tiled=True
    ).reshape(buffer_rows, feature_width)
    hits = (
        target.reshape(tok_dev, top_count)[:, :, None]
        == jnp.arange(buffer_rows, dtype=jnp.int32)[None, None, :]
    )
    gather_mat = jnp.sum(hits.astype(jnp.float32), axis=1)
    grad_tokens = jnp.dot(
        gather_mat, home_rows, precision=lax.Precision.HIGHEST, preferred_element_type=jnp.float32
    ).astype(jnp.bfloat16)
    grad_gate_up = grad_pack[: 2 * slice_width].reshape(w_gate_up.shape)
    grad_down = grad_pack[2 * slice_width :].reshape(w_down.shape)
    return (grad_tokens, grad_gate_up, grad_down)


def crossed(block, axis, apart):
    return lax.ppermute(block, axis, [(i, i ^ apart) for i in range(lax.axis_size(axis))])


def whole(count):
    return [pl.BlockSpec(memory_space=pltpu.VMEM)] * count


def packed(tokens, upstream, expert_ids, gates, n_cols):
    tok_dev, width = tokens.shape
    column = jnp.arange(128, dtype=jnp.int32)[None, :]
    table = jnp.zeros((tok_dev, 128), jnp.float32)
    for k in range(expert_ids.shape[1]):
        table = table + jnp.where(expert_ids[:, k : k + 1] == column % n_cols, gates[:, k : k + 1], 0.0)
    high = lax.reduce_precision(table, 8, 7)
    middle = lax.reduce_precision(table - high, 8, 7)
    part = column // n_cols
    table = jnp.where(part == 0, high, jnp.where(part == 1, middle, jnp.where(part == 2, table - high - middle, 0.0)))
    return jnp.concatenate([tokens, upstream, table.astype(jnp.bfloat16)], axis=1)


def forward_kernel(n_cols, n_rows, n_z, *refs):
    near = refs[: n_rows + n_z - 1]
    far = refs[n_rows + n_z - 1 : 2 * n_rows + n_z - 2]
    wgu_own, wdn_own, wgu_sib, wdn_sib, plane_ref, own_ref, sib_ref, kept_ref, *sent_refs = refs[2 * n_rows + n_z - 2 :]
    tok_dev = near[0].shape[0]
    for z in range(n_z):
        for d in range(n_rows):
            start = (z * n_rows + d) * tok_dev
            if z == 0:
                block = near[d][...]
            elif d == 0:
                block = near[n_rows + z - 1][...]
            else:
                block = far[d - 1][(z - 1) * tok_dev : z * tok_dev]
            plane_ref[start : start + tok_dev] = block
    units, width = wdn_own.shape
    col_here = lax.axis_index("expert")
    lane = lax.broadcasted_iota(jnp.int32, (8, 128), 1)
    row = lax.broadcasted_iota(jnp.int32, (8, 128), 0)
    wanted = jnp.where(row == 0, col_here, col_here ^ 1)
    chosen = (row < 2) & (lane % n_cols == wanted) & (lane < 3 * n_cols)
    gate_rows = lax.dot_general(
        jnp.where(chosen, 1.0, 0.0).astype(jnp.bfloat16), plane_ref[:, 2 * width :], contract_last, preferred_element_type=jnp.float32
    )
    total = None
    for index, (wgu, wdn, acts_ref) in enumerate(((wgu_own, wdn_own, own_ref), (wgu_sib, wdn_sib, sib_ref))):
        gate = gate_rows[index : index + 1, :]
        pre = lax.dot_general(wgu[...], plane_ref[:, :width], contract_last, preferred_element_type=jnp.float32)
        hidden_grad = gate * lax.dot_general(
            wdn[...], plane_ref[:, width : 2 * width], contract_last, preferred_element_type=jnp.float32
        )
        activated, slope_of = silu_parts(pre[:units])
        up_pre = pre[units:]
        acts_ref[:units] = (hidden_grad * up_pre * slope_of).astype(jnp.bfloat16)
        acts_ref[units : 2 * units] = (hidden_grad * activated).astype(jnp.bfloat16)
        acts_ref[2 * units :] = (activated * up_pre * gate).astype(jnp.bfloat16)
        part = lax.dot_general(acts_ref[: 2 * units], wgu[...], contract_first, preferred_element_type=jnp.float32)
        total = part if total is None else total + part
    for z in range(n_z):
        for d in range(n_rows):
            start = (z * n_rows + d) * tok_dev
            block = total[start : start + tok_dev]
            if d == 0:
                kept_ref[z] = block
            else:
                sent_refs[d - 1][z] = block.astype(jnp.bfloat16)


def halves_swapped(acts):
    half = acts.shape[1] // 2
    return jnp.concatenate([acts[:, half:], acts[:, :half]], axis=1)


def weight_grad_kernel(relocate_ref, same_ref, cross_ref, plane_ref, other_ref, gu_ref, dn_ref):
    units, width = dn_ref.shape
    moved = relocate_ref[lax.axis_index("expert"), 0] == 1
    same = jnp.where(moved, halves_swapped(same_ref[...]), same_ref[...])
    cross = jnp.where(moved, halves_swapped(cross_ref[...]), cross_ref[...])
    for out, low, start in ((gu_ref, 0, 0), (dn_ref, 2 * units, width)):
        high = low + out.shape[0]
        out[...] = (
            jnp.dot(same[low:high], plane_ref[:, start : start + width], preferred_element_type=jnp.float32)
            + jnp.dot(cross[low:high], other_ref[:, start : start + width], preferred_element_type=jnp.float32)
        ).astype(jnp.bfloat16)


def exchanges(pattern, acts_own, acts_sib, plane, sent_rows):
    n_cols = lax.axis_size("expert")
    half = n_cols // 2

    def place(col):
        return col ^ half if pattern >> (col % half) & 1 else col

    got_same = lax.ppermute(acts_own, "expert", [(col, place(col)) for col in range(n_cols)])
    got = [crossed(block, "dp", d + 1) for d, block in enumerate(sent_rows)]
    got_same, acts_sib = lax.optimization_barrier((got_same, acts_sib))
    got_cross = lax.ppermute(acts_sib, "expert", [(col, place(col ^ 1)) for col in range(n_cols)])
    got_same, got, plane = lax.optimization_barrier((got_same, got, plane))
    plane_sib = crossed(plane, "expert", 1)
    return got_same, got_cross, plane_sib, got


def dense_device(tokens, upstream, expert_ids, gates, relocate, w_gate_up, w_down):
    n_rows = lax.axis_size("dp")
    n_cols = lax.axis_size("expert")
    n_z = n_cols // 2
    tok_dev = tokens.shape[0]
    half = n_cols // 2
    units, width = w_down.shape[2:]
    plane_rows = n_rows * n_z * tok_dev
    limit = pltpu.CompilerParams(vmem_limit_bytes=16 * 2**20)
    bf16 = jnp.bfloat16

    own = packed(tokens, upstream, expert_ids, gates, n_cols)

    along_dp = [crossed(own, "dp", d) for d in range(1, n_rows)]
    along_z = [crossed(own, "expert", 2 * dz) for dz in range(1, n_z)]
    bits = jnp.sum(relocate[:half, 0] << jnp.arange(half, dtype=jnp.int32))
    along_z, along_dp, w_gate_up, w_down, bits = lax.optimization_barrier((along_z, along_dp, w_gate_up, w_down, bits))
    far = jnp.concatenate(along_z, axis=0)
    far_dp = [crossed(far, "dp", d) for d in range(1, n_rows)]
    wgu_own, wdn_own = w_gate_up[0, 0], w_down[0, 0]
    wgu_sib = crossed(wgu_own, "expert", 1)
    wdn_sib = crossed(wdn_own, "expert", 1)
    acts = jax.ShapeDtypeStruct((3 * units, plane_rows), bf16)
    plane, acts_own, acts_sib, kept, *sent = pl.pallas_call(
        functools.partial(forward_kernel, n_cols, n_rows, n_z),
        out_shape=[jax.ShapeDtypeStruct((plane_rows, own.shape[1]), bf16), acts, acts, jax.ShapeDtypeStruct((n_z, tok_dev, width), jnp.float32)]
        + [jax.ShapeDtypeStruct((n_z, tok_dev, width), bf16)] * (n_rows - 1),
        in_specs=whole(2 * n_rows + n_z + 2),
        out_specs=whole(3 + n_rows),
        compiler_params=limit,
        name="forward",
    )(own, *along_dp, *along_z, *far_dp, wgu_own, wdn_own, wgu_sib, wdn_sib)

    branches = [functools.partial(exchanges, pattern) for pattern in range(1, (1 << half) - 1)]
    got_same, got_cross, plane_sib, got = lax.switch(bits - 1, branches, acts_own, acts_sib, plane, sent)
    total = kept
    for block in got:
        total = total + block.astype(jnp.float32)
    sent_total = total.astype(bf16)
    grad_tokens = total[0]
    for dz in range(1, n_z):
        grad_tokens = grad_tokens + crossed(sent_total[dz], "expert", 2 * dz).astype(jnp.float32)
    grad_gu, grad_dn = pl.pallas_call(
        weight_grad_kernel,
        out_shape=[jax.ShapeDtypeStruct((2 * units, width), bf16), jax.ShapeDtypeStruct((units, width), bf16)],
        in_specs=[pl.BlockSpec(memory_space=pltpu.SMEM)] + whole(4),
        out_specs=whole(2),
        compiler_params=limit,
        name="weight_grads",
    )(relocate, got_same, got_cross, plane, plane_sib)
    return grad_tokens.astype(bf16), grad_gu.reshape(w_gate_up.shape), grad_dn.reshape(w_down.shape)


def solution(mesh):
    def per_device(*arrays):
        n_rows, n_cols = mesh.shape["dp"], mesh.shape["expert"]
        dense = n_rows == SLICES and arrays[2].shape[1] == n_cols and 4 <= n_cols <= 8
        return (dense_device if dense else routed_device)(*arrays)

    return jax.shard_map(
        per_device,
        mesh=mesh,
        in_specs=(
            P(("dp", "expert"), None),
            P(("dp", "expert"), None),
            P(("dp", "expert"), None),
            P(("dp", "expert"), None),
            P(),
            P("expert", "dp", None, None),
            P("expert", "dp", None, None),
        ),
        out_specs=(
            P(("dp", "expert"), None),
            P("expert", "dp", None, None),
            P("expert", "dp", None, None),
        ),
        check_vma=False,
    )
```

```python
import functools

import jax
import jax.numpy as jnp
from jax import lax
from jax.experimental import pallas as pl
from jax.experimental.pallas import tpu as pltpu
from jax.sharding import PartitionSpec as P

SLICES = 4


contract_last = (((1,), (1,)), ((), ()))
contract_first = (((0,), (0,)), ((), ()))


def swapped(block, axis, apart):
    count = lax.axis_size(axis)
    route = []
    for low in range(count):
        high = low | 1 << apart
        if high != low and high < count:
            route += [(low, high), (high, low)]
    return lax.ppermute(block, axis, route)


def silu_parts(values_in):
    sigmoid_of = jax.nn.sigmoid(values_in)
    return (values_in * sigmoid_of, sigmoid_of * (1.0 + values_in * (1.0 - sigmoid_of)))


def pick_entry(lookup_table, row_index, col_index):
    rows_hit = jnp.arange(lookup_table.shape[0], dtype=jnp.int32)[:, None] == row_index
    cols_hit = jnp.arange(lookup_table.shape[1], dtype=jnp.int32)[None, :] == col_index
    return jnp.sum(jnp.where(rows_hit & cols_hit, lookup_table, 0))


def routed_device(tokens, upstream, expert_ids, gates, relocate, w_gate_up, w_down):
    n_rows = lax.axis_size("dp")
    n_cols = lax.axis_size("expert")
    slot_count = n_rows // SLICES
    experts = slot_count * n_cols
    tok_dev, feature_width = tokens.shape
    top_count = expert_ids.shape[1]
    capacity = min(tok_dev, max(2, (3 * tok_dev * top_count + 2 * experts - 1) // (2 * experts)))
    pair_count = tok_dev * top_count
    buffer_rows = experts * capacity
    slice_width = w_down.shape[2]
    col_block = n_cols // SLICES
    col_here = lax.axis_index("expert")
    row_here = lax.axis_index("dp")
    slot_here = row_here // SLICES
    slice_here = row_here % SLICES
    far_bit = n_cols.bit_length() - 2
    half_cols = n_cols // 2
    flat_ids = expert_ids.reshape(pair_count)
    home_column = flat_ids // slot_count
    slot_of = flat_ids % slot_count
    expert_iota = jnp.arange(experts, dtype=jnp.int32)
    relocated = jnp.sum(
        jnp.where(flat_ids[:, None] == expert_iota[None, :], relocate.reshape(experts)[None, :], 0),
        axis=1,
    )
    column = (home_column + half_cols * relocated) % n_cols
    pair_iota = jnp.arange(pair_count, dtype=jnp.int32)
    earlier = (flat_ids[:, None] == flat_ids[None, :]) & (pair_iota[None, :] < pair_iota[:, None])
    slot_rank = jnp.sum(earlier.astype(jnp.int32), axis=1)
    target = (slot_of * n_cols + column) * capacity + slot_rank
    placing = (target[None, :] == jnp.arange(buffer_rows, dtype=jnp.int32)[:, None]).astype(
        jnp.bfloat16
    )
    x_pairs = jnp.repeat(tokens, top_count, axis=0)
    d_pairs = (
        gates.reshape(pair_count, 1) * jnp.repeat(upstream, top_count, axis=0).astype(jnp.float32)
    ).astype(jnp.bfloat16)
    pair_data = jnp.stack([x_pairs, d_pairs])
    sent = jnp.einsum("bp,kpw->kbw", placing, pair_data, preferred_element_type=jnp.float32).astype(
        jnp.bfloat16
    )
    sent = sent.reshape(2, slot_count, n_cols, capacity, feature_width)
    at_column = lax.all_to_all(sent, "expert", split_axis=2, concat_axis=2, tiled=True)
    swapped_here = pick_entry(relocate, col_here, slot_here)
    own_pack = jnp.concatenate([w_gate_up, w_down], axis=2)
    far_pack = swapped(own_pack, "expert", far_bit)
    own_pack = jnp.where(swapped_here == 1, far_pack, own_pack)
    gate_up = own_pack[0, 0, : 2 * slice_width]
    down_rows = own_pack[0, 0, 2 * slice_width :]
    grouped = at_column.reshape(2, n_rows, col_block, capacity, feature_width)
    at_row = lax.all_to_all(grouped, "dp", split_axis=1, concat_axis=1, tiled=True)
    gathered = at_row[:, None]
    for bit_index in range(SLICES.bit_length() - 1):
        far_rows = swapped(gathered, "dp", bit_index)
        lower_half = slice_here // (1 << bit_index) % 2 == 0
        first_part = jnp.where(lower_half, gathered, far_rows)
        second_part = jnp.where(lower_half, far_rows, gathered)
        gathered = jnp.concatenate([first_part, second_part], axis=1)
    all_rows = gathered.reshape(2, -1, feature_width)
    rows_x = all_rows[0]
    rows_d = all_rows[1]
    gate_and_up = lax.dot_general(
        rows_x, gate_up, contract_last, preferred_element_type=jnp.float32
    )
    gate_pre = gate_and_up[:, :slice_width]
    up_pre = gate_and_up[:, slice_width:]
    activated, slope_of = silu_parts(gate_pre)
    hidden = (activated * up_pre).astype(jnp.bfloat16)
    hidden_grad = lax.dot_general(
        rows_d, down_rows, contract_last, preferred_element_type=jnp.float32
    )
    pre_grads = jnp.concatenate(
        [
            (hidden_grad * up_pre * slope_of).astype(jnp.bfloat16),
            (hidden_grad * activated).astype(jnp.bfloat16),
        ],
        axis=1,
    )
    grad_gu = lax.dot_general(
        pre_grads, rows_x, contract_first, preferred_element_type=jnp.float32
    ).astype(jnp.bfloat16)
    grad_dn = lax.dot_general(
        hidden, rows_d, contract_first, preferred_element_type=jnp.float32
    ).astype(jnp.bfloat16)
    slice_part = jnp.dot(pre_grads, gate_up, preferred_element_type=jnp.float32).astype(
        jnp.bfloat16
    )
    grad_pack = jnp.concatenate([grad_gu, grad_dn], axis=0)
    blocks = slice_part.reshape(2, 2, n_rows, col_block, capacity, feature_width)
    upper_half = slice_here // 2 % 2 == 1
    keep_half = jnp.where(upper_half, blocks[1], blocks[0])
    send_half = jnp.where(upper_half, blocks[0], blocks[1])
    got_half = swapped(send_half, "dp", 1)
    pairsum = keep_half.astype(jnp.float32) + got_half.astype(jnp.float32)
    odd_slice = slice_here % 2 == 1
    keep_last = jnp.where(odd_slice, pairsum[1], pairsum[0])
    send_last = jnp.where(odd_slice, pairsum[0], pairsum[1])
    got_last = swapped(send_last, "dp", 0)
    summed = keep_last + got_last
    back_rows = lax.all_to_all(summed, "dp", split_axis=0, concat_axis=0, tiled=True).reshape(
        slot_count, n_cols, capacity, feature_width
    )
    home_rows = lax.all_to_all(
        back_rows, "expert", split_axis=1, concat_axis=1, tiled=True
    ).reshape(buffer_rows, feature_width)
    hits = (
        target.reshape(tok_dev, top_count)[:, :, None]
        == jnp.arange(buffer_rows, dtype=jnp.int32)[None, None, :]
    )
    gather_mat = jnp.sum(hits.astype(jnp.float32), axis=1)
    grad_tokens = jnp.dot(
        gather_mat, home_rows, precision=lax.Precision.HIGHEST, preferred_element_type=jnp.float32
    ).astype(jnp.bfloat16)
    grad_gate_up = grad_pack[: 2 * slice_width].reshape(w_gate_up.shape)
    grad_down = grad_pack[2 * slice_width :].reshape(w_down.shape)
    return (grad_tokens, grad_gate_up, grad_down)


def crossed(block, axis, apart):
    return lax.ppermute(block, axis, [(i, i ^ apart) for i in range(lax.axis_size(axis))])


def whole(count):
    return [pl.BlockSpec(memory_space=pltpu.VMEM)] * count


def packed(tokens, upstream, expert_ids, gates, n_cols):
    tok_dev, width = tokens.shape
    column = jnp.arange(128, dtype=jnp.int32)[None, :]
    table = jnp.zeros((tok_dev, 128), jnp.float32)
    for k in range(expert_ids.shape[1]):
        table = table + jnp.where(expert_ids[:, k : k + 1] == column % n_cols, gates[:, k : k + 1], 0.0)
    high = lax.reduce_precision(table, 8, 7)
    middle = lax.reduce_precision(table - high, 8, 7)
    part = column // n_cols
    table = jnp.where(part == 0, high, jnp.where(part == 1, middle, jnp.where(part == 2, table - high - middle, 0.0)))
    return jnp.concatenate([tokens, upstream, table.astype(jnp.bfloat16)], axis=1)


def gate_rows_of(plane, columns, n_cols, wanted):
    lane = lax.broadcasted_iota(jnp.int32, (8, 128), 1)
    row = lax.broadcasted_iota(jnp.int32, (8, 128), 0)
    chosen = jnp.zeros((8, 128), jnp.bool_)
    for index, expert in enumerate(wanted):
        chosen |= (row == index) & (lane % n_cols == expert) & (lane < 3 * n_cols)
    return lax.dot_general(
        jnp.where(chosen, 1.0, 0.0).astype(jnp.bfloat16), plane[:, columns:], contract_last, preferred_element_type=jnp.float32
    )


def activations(gate_weights, up_weights, down_weights, rows_x, rows_u, gate):
    gate_pre = lax.dot_general(gate_weights, rows_x, contract_last, preferred_element_type=jnp.float32)
    up_pre = lax.dot_general(up_weights, rows_x, contract_last, preferred_element_type=jnp.float32)
    hidden_grad = gate * lax.dot_general(down_weights, rows_u, contract_last, preferred_element_type=jnp.float32)
    activated, slope_of = silu_parts(gate_pre)
    return (
        (hidden_grad * up_pre * slope_of).astype(jnp.bfloat16),
        (hidden_grad * activated).astype(jnp.bfloat16),
        (activated * up_pre * gate).astype(jnp.bfloat16),
    )


def forward_kernel(n_cols, n_rows, n_z, early, *refs):
    near = refs[: n_rows + n_z - 1]
    far = refs[n_rows + n_z - 1 : 2 * n_rows + n_z - 2]
    wgu_hbm, wdn_hbm, wgu_sib, wdn_sib, plane_out, own_ref, sib_ref, kept_ref, *rest = refs[2 * n_rows + n_z - 2 :]
    sent_refs = rest[: n_rows - 1]
    plane_ref, wgu_own, wdn_own, acts_ref, sems = rest[n_rows - 1 :]
    loads = [
        pltpu.make_async_copy(wgu_hbm, wgu_own, sems.at[0]),
        pltpu.make_async_copy(wdn_hbm, wdn_own, sems.at[1]),
    ]
    for load in loads:
        load.start()
    tok_dev = near[0].shape[0]
    for z in range(n_z):
        for d in range(n_rows):
            start = (z * n_rows + d) * tok_dev
            if z == 0:
                block = near[d][...]
            elif d == 0:
                block = near[n_rows + z - 1][...]
            else:
                block = far[d - 1][(z - 1) * tok_dev : z * tok_dev]
            plane_ref[start : start + tok_dev] = block
    keep = pltpu.make_async_copy(plane_ref, plane_out, sems.at[2])
    keep.start()
    units, width = wdn_sib.shape
    col_here = lax.axis_index("expert")
    gate_rows = gate_rows_of(plane_ref, 2 * width, n_cols, (col_here ^ 1, col_here))
    rows_x = plane_ref[:, :width]
    rows_u = plane_ref[:, width : 2 * width]
    total = None
    for index, (wgu, wdn, late_ref) in enumerate(((wgu_sib, wdn_sib, sib_ref), (wgu_own, wdn_own, own_ref))):
        if index == 1:
            for load in loads:
                load.wait()
        parts = activations(wgu[:units], wgu[units:], wdn[...], rows_x, rows_u, gate_rows[index : index + 1, :])
        late = units - early
        for i, part in enumerate(parts):
            late_ref[i * late : (i + 1) * late] = part[early:]
        acts_ref[:units] = parts[0]
        acts_ref[units:] = parts[1]
        part = lax.dot_general(acts_ref[...], wgu[...], contract_first, preferred_element_type=jnp.float32)
        total = part if total is None else total + part
    for z in range(n_z):
        for d in range(n_rows):
            start = (z * n_rows + d) * tok_dev
            block = total[start : start + tok_dev]
            if d == 0:
                kept_ref[z] = block
            else:
                sent_refs[d - 1][z] = block.astype(jnp.bfloat16)
    keep.wait()


def weight_grad_kernel(
    n_cols, relocate_ref, same_ref, cross_ref, early_own, early_got, plane_ref, other_ref, gu_ref, dn_ref, weights, gate_acts, up_acts, down_acts
):
    units, width = dn_ref.shape
    early = early_own.shape[0] // 3
    late = units - early
    col_here = lax.axis_index("expert")
    moved = relocate_ref[col_here, 0] == 1
    weights[...] = jnp.where(moved, early_got[...], early_own[...])
    source = jnp.where(moved, col_here ^ (n_cols // 2), col_here)
    for side, (late_ref, rows) in enumerate(((same_ref, plane_ref), (cross_ref, other_ref))):
        gate = gate_rows_of(rows, 2 * width, n_cols, (source,))[:1, :]
        parts = activations(
            weights[:early], weights[early : 2 * early], weights[2 * early :], rows[:, :width], rows[:, width : 2 * width], gate
        )
        late_acts = jnp.where(moved, halves_swapped(late_ref[...]), late_ref[...])
        for i, acts in enumerate((gate_acts, up_acts, down_acts)):
            acts[side, :early] = parts[i]
            acts[side, early:] = late_acts[i * late : (i + 1) * late]
    for out, acts, start in ((gu_ref.at[:units], gate_acts, 0), (gu_ref.at[units:], up_acts, 0), (dn_ref, down_acts, width)):
        out[...] = (
            jnp.dot(acts[0], plane_ref[:, start : start + width], preferred_element_type=jnp.float32)
            + jnp.dot(acts[1], other_ref[:, start : start + width], preferred_element_type=jnp.float32)
        ).astype(jnp.bfloat16)


def halves_swapped(acts):
    half = acts.shape[1] // 2
    return jnp.concatenate([acts[:, half:], acts[:, :half]], axis=1)


def exchanges(pattern, acts_own, acts_sib, plane, sent_rows):
    n_cols = lax.axis_size("expert")
    half = n_cols // 2

    def place(col):
        return col ^ half if pattern >> (col % half) & 1 else col

    got_same = lax.ppermute(acts_own, "expert", [(col, place(col)) for col in range(n_cols)])
    got = [crossed(block, "dp", d + 1) for d, block in enumerate(sent_rows)]
    got_same, acts_sib = lax.optimization_barrier((got_same, acts_sib))
    got_cross = lax.ppermute(acts_sib, "expert", [(col, place(col ^ 1)) for col in range(n_cols)])
    got_same, got, plane = lax.optimization_barrier((got_same, got, plane))
    plane_sib = crossed(plane, "expert", 1)
    return got_same, got_cross, plane_sib, got


def dense_device(tokens, upstream, expert_ids, gates, relocate, w_gate_up, w_down):
    n_rows = lax.axis_size("dp")
    n_cols = lax.axis_size("expert")
    n_z = n_cols // 2
    tok_dev = tokens.shape[0]
    half = n_cols // 2
    units, width = w_down.shape[2:]
    plane_rows = n_rows * n_z * tok_dev
    limit = pltpu.CompilerParams(vmem_limit_bytes=16 * 2**20)
    bf16 = jnp.bfloat16

    early = units // 3 // 16 * 16
    wgu_own, wdn_own = w_gate_up[0, 0], w_down[0, 0]
    wgu_sib = crossed(wgu_own, "expert", 1)
    wdn_sib = crossed(wdn_own, "expert", 1)
    own = packed(tokens, upstream, expert_ids, gates, n_cols)
    own, wgu_sib, wdn_sib, w_gate_up, w_down = lax.optimization_barrier((own, wgu_sib, wdn_sib, w_gate_up, w_down))
    early_own = jnp.concatenate(
        [w_gate_up[0, 0, :early], w_gate_up[0, 0, units : units + early], w_down[0, 0, :early]], axis=0
    )

    along_dp = [crossed(own, "dp", d) for d in range(1, n_rows)]
    along_z = [crossed(own, "expert", 2 * dz) for dz in range(1, n_z)]
    bits = jnp.sum(relocate[:half, 0] << jnp.arange(half, dtype=jnp.int32))
    along_z, along_dp, early_own, bits = lax.optimization_barrier((along_z, along_dp, early_own, bits))
    far = jnp.concatenate(along_z, axis=0)
    far_dp = [crossed(far, "dp", d) for d in range(1, n_rows)]
    early_got = crossed(early_own, "expert", half)
    acts = jax.ShapeDtypeStruct((3 * (units - early), plane_rows), bf16)
    plane, acts_own, acts_sib, kept, *sent = pl.pallas_call(
        functools.partial(forward_kernel, n_cols, n_rows, n_z, early),
        out_shape=[jax.ShapeDtypeStruct((plane_rows, own.shape[1]), bf16), acts, acts, jax.ShapeDtypeStruct((n_z, tok_dev, width), jnp.float32)]
        + [jax.ShapeDtypeStruct((n_z, tok_dev, width), bf16)] * (n_rows - 1),
        in_specs=whole(2 * n_rows + n_z - 2) + [pl.BlockSpec(memory_space=pl.ANY)] * 2 + whole(2),
        out_specs=[pl.BlockSpec(memory_space=pl.ANY)] + whole(2 + n_rows),
        scratch_shapes=[
            pltpu.VMEM((plane_rows, own.shape[1]), bf16),
            pltpu.VMEM(wgu_own.shape, bf16),
            pltpu.VMEM(wdn_own.shape, bf16),
            pltpu.VMEM((2 * units, plane_rows), bf16),
            pltpu.SemaphoreType.DMA((3,)),
        ],
        compiler_params=limit,
        name="forward",
    )(own, *along_dp, *along_z, *far_dp, wgu_own, wdn_own, wgu_sib, wdn_sib)

    branches = [functools.partial(exchanges, pattern) for pattern in range(1, (1 << half) - 1)]
    got_same, got_cross, plane_sib, got = lax.switch(bits - 1, branches, acts_own, acts_sib, plane, sent)
    got, early_got = lax.optimization_barrier((got, early_got))
    total = kept
    for block in got:
        total = total + block.astype(jnp.float32)
    sent_total = total.astype(bf16)
    grad_tokens = total[0]
    for dz in range(1, n_z):
        grad_tokens = grad_tokens + crossed(sent_total[dz], "expert", 2 * dz).astype(jnp.float32)
    grad_gu, grad_dn = pl.pallas_call(
        functools.partial(weight_grad_kernel, n_cols),
        out_shape=[jax.ShapeDtypeStruct((2 * units, width), bf16), jax.ShapeDtypeStruct((units, width), bf16)],
        in_specs=[pl.BlockSpec(memory_space=pltpu.SMEM)] + whole(6),
        out_specs=whole(2),
        scratch_shapes=[pltpu.VMEM(early_own.shape, bf16)] + [pltpu.VMEM((2, units, plane_rows), bf16)] * 3,
        compiler_params=limit,
        name="weight_grads",
    )(relocate, got_same, got_cross, early_own, early_got, plane, plane_sib)
    return grad_tokens.astype(bf16), grad_gu.reshape(w_gate_up.shape), grad_dn.reshape(w_down.shape)


def solution(mesh):
    def per_device(*arrays):
        n_rows, n_cols = mesh.shape["dp"], mesh.shape["expert"]
        dense = n_rows == SLICES and arrays[2].shape[1] == n_cols and 4 <= n_cols <= 8
        return (dense_device if dense else routed_device)(*arrays)

    return jax.shard_map(
        per_device,
        mesh=mesh,
        in_specs=(
            P(("dp", "expert"), None),
            P(("dp", "expert"), None),
            P(("dp", "expert"), None),
            P(("dp", "expert"), None),
            P(),
            P("expert", "dp", None, None),
            P("expert", "dp", None, None),
        ),
        out_specs=(
            P(("dp", "expert"), None),
            P("expert", "dp", None, None),
            P("expert", "dp", None, None),
        ),
        check_vma=False,
    )
```

```python
import functools

import jax
import jax.numpy as jnp
from jax import lax
from jax.experimental import pallas as pl
from jax.experimental.pallas import tpu as pltpu
from jax.sharding import PartitionSpec as P

SLICES = 4


contract_last = (((1,), (1,)), ((), ()))
contract_first = (((0,), (0,)), ((), ()))


def swapped(block, axis, apart):
    count = lax.axis_size(axis)
    route = []
    for low in range(count):
        high = low | 1 << apart
        if high != low and high < count:
            route += [(low, high), (high, low)]
    return lax.ppermute(block, axis, route)


def silu_parts(values_in):
    sigmoid_of = jax.nn.sigmoid(values_in)
    return (values_in * sigmoid_of, sigmoid_of * (1.0 + values_in * (1.0 - sigmoid_of)))


def pick_entry(lookup_table, row_index, col_index):
    rows_hit = jnp.arange(lookup_table.shape[0], dtype=jnp.int32)[:, None] == row_index
    cols_hit = jnp.arange(lookup_table.shape[1], dtype=jnp.int32)[None, :] == col_index
    return jnp.sum(jnp.where(rows_hit & cols_hit, lookup_table, 0))


def routed_device(tokens, upstream, expert_ids, gates, relocate, w_gate_up, w_down):
    n_rows = lax.axis_size("dp")
    n_cols = lax.axis_size("expert")
    slot_count = n_rows // SLICES
    experts = slot_count * n_cols
    tok_dev, feature_width = tokens.shape
    top_count = expert_ids.shape[1]
    capacity = min(tok_dev, max(2, (3 * tok_dev * top_count + 2 * experts - 1) // (2 * experts)))
    pair_count = tok_dev * top_count
    buffer_rows = experts * capacity
    slice_width = w_down.shape[2]
    col_block = n_cols // SLICES
    col_here = lax.axis_index("expert")
    row_here = lax.axis_index("dp")
    slot_here = row_here // SLICES
    slice_here = row_here % SLICES
    far_bit = n_cols.bit_length() - 2
    half_cols = n_cols // 2
    flat_ids = expert_ids.reshape(pair_count)
    home_column = flat_ids // slot_count
    slot_of = flat_ids % slot_count
    expert_iota = jnp.arange(experts, dtype=jnp.int32)
    relocated = jnp.sum(
        jnp.where(flat_ids[:, None] == expert_iota[None, :], relocate.reshape(experts)[None, :], 0),
        axis=1,
    )
    column = (home_column + half_cols * relocated) % n_cols
    pair_iota = jnp.arange(pair_count, dtype=jnp.int32)
    earlier = (flat_ids[:, None] == flat_ids[None, :]) & (pair_iota[None, :] < pair_iota[:, None])
    slot_rank = jnp.sum(earlier.astype(jnp.int32), axis=1)
    target = (slot_of * n_cols + column) * capacity + slot_rank
    placing = (target[None, :] == jnp.arange(buffer_rows, dtype=jnp.int32)[:, None]).astype(
        jnp.bfloat16
    )
    x_pairs = jnp.repeat(tokens, top_count, axis=0)
    d_pairs = (
        gates.reshape(pair_count, 1) * jnp.repeat(upstream, top_count, axis=0).astype(jnp.float32)
    ).astype(jnp.bfloat16)
    pair_data = jnp.stack([x_pairs, d_pairs])
    sent = jnp.einsum("bp,kpw->kbw", placing, pair_data, preferred_element_type=jnp.float32).astype(
        jnp.bfloat16
    )
    sent = sent.reshape(2, slot_count, n_cols, capacity, feature_width)
    at_column = lax.all_to_all(sent, "expert", split_axis=2, concat_axis=2, tiled=True)
    swapped_here = pick_entry(relocate, col_here, slot_here)
    own_pack = jnp.concatenate([w_gate_up, w_down], axis=2)
    far_pack = swapped(own_pack, "expert", far_bit)
    own_pack = jnp.where(swapped_here == 1, far_pack, own_pack)
    gate_up = own_pack[0, 0, : 2 * slice_width]
    down_rows = own_pack[0, 0, 2 * slice_width :]
    grouped = at_column.reshape(2, n_rows, col_block, capacity, feature_width)
    at_row = lax.all_to_all(grouped, "dp", split_axis=1, concat_axis=1, tiled=True)
    gathered = at_row[:, None]
    for bit_index in range(SLICES.bit_length() - 1):
        far_rows = swapped(gathered, "dp", bit_index)
        lower_half = slice_here // (1 << bit_index) % 2 == 0
        first_part = jnp.where(lower_half, gathered, far_rows)
        second_part = jnp.where(lower_half, far_rows, gathered)
        gathered = jnp.concatenate([first_part, second_part], axis=1)
    all_rows = gathered.reshape(2, -1, feature_width)
    rows_x = all_rows[0]
    rows_d = all_rows[1]
    gate_and_up = lax.dot_general(
        rows_x, gate_up, contract_last, preferred_element_type=jnp.float32
    )
    gate_pre = gate_and_up[:, :slice_width]
    up_pre = gate_and_up[:, slice_width:]
    activated, slope_of = silu_parts(gate_pre)
    hidden = (activated * up_pre).astype(jnp.bfloat16)
    hidden_grad = lax.dot_general(
        rows_d, down_rows, contract_last, preferred_element_type=jnp.float32
    )
    pre_grads = jnp.concatenate(
        [
            (hidden_grad * up_pre * slope_of).astype(jnp.bfloat16),
            (hidden_grad * activated).astype(jnp.bfloat16),
        ],
        axis=1,
    )
    grad_gu = lax.dot_general(
        pre_grads, rows_x, contract_first, preferred_element_type=jnp.float32
    ).astype(jnp.bfloat16)
    grad_dn = lax.dot_general(
        hidden, rows_d, contract_first, preferred_element_type=jnp.float32
    ).astype(jnp.bfloat16)
    slice_part = jnp.dot(pre_grads, gate_up, preferred_element_type=jnp.float32).astype(
        jnp.bfloat16
    )
    grad_pack = jnp.concatenate([grad_gu, grad_dn], axis=0)
    blocks = slice_part.reshape(2, 2, n_rows, col_block, capacity, feature_width)
    upper_half = slice_here // 2 % 2 == 1
    keep_half = jnp.where(upper_half, blocks[1], blocks[0])
    send_half = jnp.where(upper_half, blocks[0], blocks[1])
    got_half = swapped(send_half, "dp", 1)
    pairsum = keep_half.astype(jnp.float32) + got_half.astype(jnp.float32)
    odd_slice = slice_here % 2 == 1
    keep_last = jnp.where(odd_slice, pairsum[1], pairsum[0])
    send_last = jnp.where(odd_slice, pairsum[0], pairsum[1])
    got_last = swapped(send_last, "dp", 0)
    summed = keep_last + got_last
    back_rows = lax.all_to_all(summed, "dp", split_axis=0, concat_axis=0, tiled=True).reshape(
        slot_count, n_cols, capacity, feature_width
    )
    home_rows = lax.all_to_all(
        back_rows, "expert", split_axis=1, concat_axis=1, tiled=True
    ).reshape(buffer_rows, feature_width)
    hits = (
        target.reshape(tok_dev, top_count)[:, :, None]
        == jnp.arange(buffer_rows, dtype=jnp.int32)[None, None, :]
    )
    gather_mat = jnp.sum(hits.astype(jnp.float32), axis=1)
    grad_tokens = jnp.dot(
        gather_mat, home_rows, precision=lax.Precision.HIGHEST, preferred_element_type=jnp.float32
    ).astype(jnp.bfloat16)
    grad_gate_up = grad_pack[: 2 * slice_width].reshape(w_gate_up.shape)
    grad_down = grad_pack[2 * slice_width :].reshape(w_down.shape)
    return (grad_tokens, grad_gate_up, grad_down)


def crossed(block, axis, apart):
    return lax.ppermute(block, axis, [(i, i ^ apart) for i in range(lax.axis_size(axis))])


def whole(count):
    return [pl.BlockSpec(memory_space=pltpu.VMEM)] * count


def packed(tokens, upstream, expert_ids, gates, n_cols):
    tok_dev, width = tokens.shape
    column = jnp.arange(128, dtype=jnp.int32)[None, :]
    table = jnp.zeros((tok_dev, 128), jnp.float32)
    for k in range(expert_ids.shape[1]):
        table = table + jnp.where(expert_ids[:, k : k + 1] == column % n_cols, gates[:, k : k + 1], 0.0)
    high = lax.reduce_precision(table, 8, 7)
    middle = lax.reduce_precision(table - high, 8, 7)
    part = column // n_cols
    table = jnp.where(part == 0, high, jnp.where(part == 1, middle, jnp.where(part == 2, table - high - middle, 0.0)))
    return jnp.concatenate([tokens, upstream, table.astype(jnp.bfloat16)], axis=1)


def gate_rows_of(plane, columns, n_cols, wanted):
    lane = lax.broadcasted_iota(jnp.int32, (8, 128), 1)
    row = lax.broadcasted_iota(jnp.int32, (8, 128), 0)
    chosen = jnp.zeros((8, 128), jnp.bool_)
    for index, expert in enumerate(wanted):
        chosen |= (row == index) & (lane % n_cols == expert) & (lane < 3 * n_cols)
    return lax.dot_general(
        jnp.where(chosen, 1.0, 0.0).astype(jnp.bfloat16), plane[:, columns:], contract_last, preferred_element_type=jnp.float32
    )


def weights_kernel(wgu_hbm, wdn_hbm, weights_ref, sems):
    split = wgu_hbm.shape[0]
    copies = [
        pltpu.make_async_copy(wgu_hbm, weights_ref.at[pl.ds(0, split)], sems.at[0]),
        pltpu.make_async_copy(wdn_hbm, weights_ref.at[pl.ds(split, wdn_hbm.shape[0])], sems.at[1]),
    ]
    for copy in copies:
        copy.start()
    for copy in copies:
        copy.wait()


def forward_kernel(n_cols, n_rows, n_z, relocate_ref, *refs):
    near = refs[: n_rows + n_z - 1]
    far = refs[n_rows + n_z - 1 : 2 * n_rows + n_z - 2]
    weights_own, wgu_sib, wdn_sib, plane_out, acts_ref, one_ref, kept_ref, *rest = refs[2 * n_rows + n_z - 2 :]
    sent_refs = rest[: n_rows - 1]
    plane_ref, sem = rest[n_rows - 1 :]
    tok_dev = near[0].shape[0]
    for z in range(n_z):
        for d in range(n_rows):
            start = (z * n_rows + d) * tok_dev
            if z == 0:
                block = near[d][...]
            elif d == 0:
                block = near[n_rows + z - 1][...]
            else:
                block = far[d - 1][(z - 1) * tok_dev : z * tok_dev]
            plane_ref[start : start + tok_dev] = block
    keep = pltpu.make_async_copy(plane_ref, plane_out, sem)
    keep.start()
    units, width = wdn_sib.shape
    split = wgu_sib.shape[0]
    col_here = lax.axis_index("expert")
    lane = lax.broadcasted_iota(jnp.int32, (8, 128), 1)
    row = lax.broadcasted_iota(jnp.int32, (8, 128), 0)
    wanted = jnp.where(row == 0, col_here, col_here ^ 1)
    chosen = (row < 2) & (lane % n_cols == wanted) & (lane < 3 * n_cols)
    gate_rows = lax.dot_general(
        jnp.where(chosen, 1.0, 0.0).astype(jnp.bfloat16),
        plane_ref[:, 2 * width :],
        contract_last,
        preferred_element_type=jnp.float32,
    )
    rows_x = plane_ref[:, :width]
    rows_u = plane_ref[:, width : 2 * width]
    total = None
    for index, (wgu, wdn) in enumerate(((weights_own[:split], weights_own[split:]), (wgu_sib[...], wdn_sib[...]))):
        gate = gate_rows[index : index + 1, :]
        pre = lax.dot_general(wgu, rows_x, contract_last, preferred_element_type=jnp.float32)
        hidden_grad = gate * lax.dot_general(wdn, rows_u, contract_last, preferred_element_type=jnp.float32)
        activated, slope_of = silu_parts(pre[:units])
        up_pre = pre[units:]
        base = index * 3 * units
        acts_ref[base : base + units] = (hidden_grad * up_pre * slope_of).astype(jnp.bfloat16)
        acts_ref[base + units : base + 2 * units] = (hidden_grad * activated).astype(jnp.bfloat16)
        acts_ref[base + 2 * units : base + 3 * units] = (activated * up_pre * gate).astype(jnp.bfloat16)
        part = lax.dot_general(acts_ref[base : base + 2 * units], wgu, contract_first, preferred_element_type=jnp.float32)
        total = part if total is None else total + part
    for z in range(n_z):
        for d in range(n_rows):
            start = (z * n_rows + d) * tok_dev
            block = total[start : start + tok_dev]
            if d == 0:
                kept_ref[z] = block
            else:
                sent_refs[d - 1][z] = block.astype(jnp.bfloat16)
    one_ref[...] = jnp.where(relocate_ref[col_here, 0] == 1, acts_ref[: 3 * units], acts_ref[3 * units :])
    keep.wait()


def weight_grad_kernel(same_ref, cross_ref, plane_ref, other_ref, gu_ref, dn_ref):
    units, width = dn_ref.shape
    for out, low, start in ((gu_ref, 0, 0), (dn_ref, 2 * units, width)):
        high = low + out.shape[0]
        out[...] = (
            jnp.dot(same_ref[low:high], plane_ref[:, start : start + width], preferred_element_type=jnp.float32)
            + jnp.dot(cross_ref[low:high], other_ref[:, start : start + width], preferred_element_type=jnp.float32)
        ).astype(jnp.bfloat16)


def halves_swapped(acts):
    half = acts.shape[1] // 2
    return jnp.concatenate([acts[:, half:], acts[:, :half]], axis=1)


def exchanges(moving, acts, one, plane, kept, sent_rows, own_moved, sib_moved):
    n_cols = lax.axis_size("expert")
    half = n_cols // 2
    pairs = half // 2
    rows = acts.shape[0] // 2

    def route(count):
        return [(col, col ^ half) for col in range(n_cols) if moving[col % half // 2] == count]

    from_one = lax.ppermute(one, "expert", route(1)) if 1 in moving else None
    from_both = lax.ppermute(acts, "expert", route(2)) if 2 in moving else None
    plane_sib = crossed(plane, "expert", 1)
    got = [crossed(block, "dp", d + 1) for d, block in enumerate(sent_rows)]
    total = kept
    for block in got:
        total = total + block.astype(jnp.float32)
    sent_total = total.astype(jnp.bfloat16)

    chip = lax.axis_index("expert") // 2 % pairs

    def placed(low, moved):
        here = acts[low : low + rows]
        if from_both is None:
            arrived = from_one
        elif from_one is None:
            arrived = from_both[low : low + rows]
        else:
            arrived = jnp.where(chip == moving.index(1), from_one, from_both[low : low + rows])
        return jnp.where(moved == 1, halves_swapped(arrived), here)

    parts = [sent_total[dz] for dz in range(1, half)]
    return lax.optimization_barrier((placed(0, own_moved), placed(rows, sib_moved), plane_sib, total[0], parts))


def dense_device(tokens, upstream, expert_ids, gates, relocate, w_gate_up, w_down):
    n_rows = lax.axis_size("dp")
    n_cols = lax.axis_size("expert")
    n_z = n_cols // 2
    tok_dev = tokens.shape[0]
    half = n_cols // 2
    units, width = w_down.shape[2:]
    plane_rows = n_rows * n_z * tok_dev
    limit = pltpu.CompilerParams(vmem_limit_bytes=16 * 2**20)
    bf16 = jnp.bfloat16

    wgu_own, wdn_own = w_gate_up[0, 0], w_down[0, 0]
    wgu_sib = crossed(wgu_own, "expert", 1)
    wdn_sib = crossed(wdn_own, "expert", 1)
    own = packed(tokens, upstream, expert_ids, gates, n_cols)
    own, wgu_sib, wdn_sib, wgu_own, wdn_own, flags = lax.optimization_barrier(
        (own, wgu_sib, wdn_sib, wgu_own, wdn_own, relocate[:, 0])
    )
    weights_own = pl.pallas_call(
        weights_kernel,
        out_shape=jax.ShapeDtypeStruct((3 * units, width), bf16),
        in_specs=[pl.BlockSpec(memory_space=pl.ANY)] * 2,
        out_specs=whole(1)[0],
        scratch_shapes=[pltpu.SemaphoreType.DMA((2,))],
        compiler_params=limit,
        name="weights",
    )(wgu_own, wdn_own)

    along_dp = [crossed(own, "dp", d) for d in range(1, n_rows)]
    along_z = [crossed(own, "expert", 2 * dz) for dz in range(1, n_z)]
    pairs = half // 2
    case = jnp.sum(flags[:half] * jnp.array([3 ** (pairs - 1 - col // 2) for col in range(half)], jnp.int32)) - 1
    columns = jnp.arange(n_cols, dtype=jnp.int32)
    col_here = lax.axis_index("expert")
    own_moved = jnp.sum(jnp.where(columns == col_here, flags, 0))
    sib_moved = jnp.sum(jnp.where(columns == col_here ^ 1, flags, 0))
    order = along_z[:0:-1] + along_dp[::-1] + along_z[:1]
    order, weights_own, case, own_moved, sib_moved = lax.optimization_barrier((order, weights_own, case, own_moved, sib_moved))
    along_z = [order[-1]] + order[: n_z - 2][::-1]
    along_dp = order[n_z - 2 : -1][::-1]
    far = jnp.concatenate(along_z, axis=0)
    far_dp = [crossed(far, "dp", d) for d in range(1, n_rows)]
    plane, acts, one, kept, *sent = pl.pallas_call(
        functools.partial(forward_kernel, n_cols, n_rows, n_z),
        out_shape=[
            jax.ShapeDtypeStruct((plane_rows, own.shape[1]), bf16),
            jax.ShapeDtypeStruct((6 * units, plane_rows), bf16),
            jax.ShapeDtypeStruct((3 * units, plane_rows), bf16),
            jax.ShapeDtypeStruct((n_z, tok_dev, width), jnp.float32),
        ]
        + [jax.ShapeDtypeStruct((n_z, tok_dev, width), bf16)] * (n_rows - 1),
        in_specs=[pl.BlockSpec(memory_space=pltpu.SMEM)] + whole(2 * n_rows + n_z + 1),
        out_specs=[pl.BlockSpec(memory_space=pltpu.HBM)] + whole(2 + n_rows),
        scratch_shapes=[pltpu.VMEM((plane_rows, own.shape[1]), bf16), pltpu.SemaphoreType.DMA],
        compiler_params=limit,
        name="forward",
    )(relocate, own, *along_dp, *along_z, *far_dp, weights_own, wgu_sib, wdn_sib)

    cases = [tuple(number // 3 ** (pairs - 1 - p) % 3 for p in range(pairs)) for number in range(1, 3**pairs - 1)]
    same, others, plane_sib, grad_tokens, parts = lax.switch(
        case, [functools.partial(exchanges, moving) for moving in cases], acts, one, plane, kept, sent, own_moved, sib_moved
    )
    cross = crossed(others, "expert", 1)
    for dz in range(1, n_z):
        grad_tokens = grad_tokens + crossed(parts[dz - 1], "expert", 2 * dz).astype(jnp.float32)
    grad_gu, grad_dn = pl.pallas_call(
        weight_grad_kernel,
        out_shape=[jax.ShapeDtypeStruct((2 * units, width), bf16), jax.ShapeDtypeStruct((units, width), bf16)],
        in_specs=whole(4),
        out_specs=whole(2),
        compiler_params=limit,
        name="weight_grads",
    )(same, cross, plane, plane_sib)
    return grad_tokens.astype(bf16), grad_gu.reshape(w_gate_up.shape), grad_dn.reshape(w_down.shape)


def solution(mesh):
    def per_device(*arrays):
        n_rows, n_cols = mesh.shape["dp"], mesh.shape["expert"]
        dense = n_rows == SLICES and arrays[2].shape[1] == n_cols and 4 <= n_cols <= 8
        return (dense_device if dense else routed_device)(*arrays)

    return jax.shard_map(
        per_device,
        mesh=mesh,
        in_specs=(
            P(("dp", "expert"), None),
            P(("dp", "expert"), None),
            P(("dp", "expert"), None),
            P(("dp", "expert"), None),
            P(),
            P("expert", "dp", None, None),
            P("expert", "dp", None, None),
        ),
        out_specs=(
            P(("dp", "expert"), None),
            P("expert", "dp", None, None),
            P("expert", "dp", None, None),
        ),
        check_vma=False,
    )
```

```python
import functools

import jax
import jax.numpy as jnp
from jax import lax
from jax.experimental import pallas as pl
from jax.experimental.pallas import tpu as pltpu
from jax.sharding import PartitionSpec as P

SLICES = 4


contract_last = (((1,), (1,)), ((), ()))
contract_first = (((0,), (0,)), ((), ()))


def swapped(block, axis, apart):
    count = lax.axis_size(axis)
    route = []
    for low in range(count):
        high = low | 1 << apart
        if high != low and high < count:
            route += [(low, high), (high, low)]
    return lax.ppermute(block, axis, route)


def silu_parts(values_in):
    sigmoid_of = jax.nn.sigmoid(values_in)
    return (values_in * sigmoid_of, sigmoid_of * (1.0 + values_in * (1.0 - sigmoid_of)))


def pick_entry(lookup_table, row_index, col_index):
    rows_hit = jnp.arange(lookup_table.shape[0], dtype=jnp.int32)[:, None] == row_index
    cols_hit = jnp.arange(lookup_table.shape[1], dtype=jnp.int32)[None, :] == col_index
    return jnp.sum(jnp.where(rows_hit & cols_hit, lookup_table, 0))


def routed_device(tokens, upstream, expert_ids, gates, relocate, w_gate_up, w_down):
    n_rows = lax.axis_size("dp")
    n_cols = lax.axis_size("expert")
    slot_count = n_rows // SLICES
    experts = slot_count * n_cols
    tok_dev, feature_width = tokens.shape
    top_count = expert_ids.shape[1]
    capacity = min(tok_dev, max(2, (3 * tok_dev * top_count + 2 * experts - 1) // (2 * experts)))
    pair_count = tok_dev * top_count
    buffer_rows = experts * capacity
    slice_width = w_down.shape[2]
    col_block = n_cols // SLICES
    col_here = lax.axis_index("expert")
    row_here = lax.axis_index("dp")
    slot_here = row_here // SLICES
    slice_here = row_here % SLICES
    far_bit = n_cols.bit_length() - 2
    half_cols = n_cols // 2
    flat_ids = expert_ids.reshape(pair_count)
    home_column = flat_ids // slot_count
    slot_of = flat_ids % slot_count
    expert_iota = jnp.arange(experts, dtype=jnp.int32)
    relocated = jnp.sum(
        jnp.where(flat_ids[:, None] == expert_iota[None, :], relocate.reshape(experts)[None, :], 0),
        axis=1,
    )
    column = (home_column + half_cols * relocated) % n_cols
    pair_iota = jnp.arange(pair_count, dtype=jnp.int32)
    earlier = (flat_ids[:, None] == flat_ids[None, :]) & (pair_iota[None, :] < pair_iota[:, None])
    slot_rank = jnp.sum(earlier.astype(jnp.int32), axis=1)
    target = (slot_of * n_cols + column) * capacity + slot_rank
    placing = (target[None, :] == jnp.arange(buffer_rows, dtype=jnp.int32)[:, None]).astype(
        jnp.bfloat16
    )
    x_pairs = jnp.repeat(tokens, top_count, axis=0)
    d_pairs = (
        gates.reshape(pair_count, 1) * jnp.repeat(upstream, top_count, axis=0).astype(jnp.float32)
    ).astype(jnp.bfloat16)
    pair_data = jnp.stack([x_pairs, d_pairs])
    sent = jnp.einsum("bp,kpw->kbw", placing, pair_data, preferred_element_type=jnp.float32).astype(
        jnp.bfloat16
    )
    sent = sent.reshape(2, slot_count, n_cols, capacity, feature_width)
    at_column = lax.all_to_all(sent, "expert", split_axis=2, concat_axis=2, tiled=True)
    swapped_here = pick_entry(relocate, col_here, slot_here)
    own_pack = jnp.concatenate([w_gate_up, w_down], axis=2)
    far_pack = swapped(own_pack, "expert", far_bit)
    own_pack = jnp.where(swapped_here == 1, far_pack, own_pack)
    gate_up = own_pack[0, 0, : 2 * slice_width]
    down_rows = own_pack[0, 0, 2 * slice_width :]
    grouped = at_column.reshape(2, n_rows, col_block, capacity, feature_width)
    at_row = lax.all_to_all(grouped, "dp", split_axis=1, concat_axis=1, tiled=True)
    gathered = at_row[:, None]
    for bit_index in range(SLICES.bit_length() - 1):
        far_rows = swapped(gathered, "dp", bit_index)
        lower_half = slice_here // (1 << bit_index) % 2 == 0
        first_part = jnp.where(lower_half, gathered, far_rows)
        second_part = jnp.where(lower_half, far_rows, gathered)
        gathered = jnp.concatenate([first_part, second_part], axis=1)
    all_rows = gathered.reshape(2, -1, feature_width)
    rows_x = all_rows[0]
    rows_d = all_rows[1]
    gate_and_up = lax.dot_general(
        rows_x, gate_up, contract_last, preferred_element_type=jnp.float32
    )
    gate_pre = gate_and_up[:, :slice_width]
    up_pre = gate_and_up[:, slice_width:]
    activated, slope_of = silu_parts(gate_pre)
    hidden = (activated * up_pre).astype(jnp.bfloat16)
    hidden_grad = lax.dot_general(
        rows_d, down_rows, contract_last, preferred_element_type=jnp.float32
    )
    pre_grads = jnp.concatenate(
        [
            (hidden_grad * up_pre * slope_of).astype(jnp.bfloat16),
            (hidden_grad * activated).astype(jnp.bfloat16),
        ],
        axis=1,
    )
    grad_gu = lax.dot_general(
        pre_grads, rows_x, contract_first, preferred_element_type=jnp.float32
    ).astype(jnp.bfloat16)
    grad_dn = lax.dot_general(
        hidden, rows_d, contract_first, preferred_element_type=jnp.float32
    ).astype(jnp.bfloat16)
    slice_part = jnp.dot(pre_grads, gate_up, preferred_element_type=jnp.float32).astype(
        jnp.bfloat16
    )
    grad_pack = jnp.concatenate([grad_gu, grad_dn], axis=0)
    blocks = slice_part.reshape(2, 2, n_rows, col_block, capacity, feature_width)
    upper_half = slice_here // 2 % 2 == 1
    keep_half = jnp.where(upper_half, blocks[1], blocks[0])
    send_half = jnp.where(upper_half, blocks[0], blocks[1])
    got_half = swapped(send_half, "dp", 1)
    pairsum = keep_half.astype(jnp.float32) + got_half.astype(jnp.float32)
    odd_slice = slice_here % 2 == 1
    keep_last = jnp.where(odd_slice, pairsum[1], pairsum[0])
    send_last = jnp.where(odd_slice, pairsum[0], pairsum[1])
    got_last = swapped(send_last, "dp", 0)
    summed = keep_last + got_last
    back_rows = lax.all_to_all(summed, "dp", split_axis=0, concat_axis=0, tiled=True).reshape(
        slot_count, n_cols, capacity, feature_width
    )
    home_rows = lax.all_to_all(
        back_rows, "expert", split_axis=1, concat_axis=1, tiled=True
    ).reshape(buffer_rows, feature_width)
    hits = (
        target.reshape(tok_dev, top_count)[:, :, None]
        == jnp.arange(buffer_rows, dtype=jnp.int32)[None, None, :]
    )
    gather_mat = jnp.sum(hits.astype(jnp.float32), axis=1)
    grad_tokens = jnp.dot(
        gather_mat, home_rows, precision=lax.Precision.HIGHEST, preferred_element_type=jnp.float32
    ).astype(jnp.bfloat16)
    grad_gate_up = grad_pack[: 2 * slice_width].reshape(w_gate_up.shape)
    grad_down = grad_pack[2 * slice_width :].reshape(w_down.shape)
    return (grad_tokens, grad_gate_up, grad_down)


def crossed(block, axis, apart):
    return lax.ppermute(block, axis, [(i, i ^ apart) for i in range(lax.axis_size(axis))])


def whole(count):
    return [pl.BlockSpec(memory_space=pltpu.VMEM)] * count


def packed(tokens, upstream, expert_ids, gates, n_cols):
    tok_dev, width = tokens.shape
    column = jnp.arange(128, dtype=jnp.int32)[None, :]
    table = jnp.zeros((tok_dev, 128), jnp.float32)
    for k in range(expert_ids.shape[1]):
        table = table + jnp.where(expert_ids[:, k : k + 1] == column % n_cols, gates[:, k : k + 1], 0.0)
    high = lax.reduce_precision(table, 8, 7)
    middle = lax.reduce_precision(table - high, 8, 7)
    part = column // n_cols
    table = jnp.where(part == 0, high, jnp.where(part == 1, middle, jnp.where(part == 2, table - high - middle, 0.0)))
    return jnp.concatenate([tokens, upstream, table.astype(jnp.bfloat16)], axis=1)


def gate_rows_of(plane, columns, n_cols, wanted):
    lane = lax.broadcasted_iota(jnp.int32, (8, 128), 1)
    row = lax.broadcasted_iota(jnp.int32, (8, 128), 0)
    chosen = jnp.zeros((8, 128), jnp.bool_)
    for index, expert in enumerate(wanted):
        chosen |= (row == index) & (lane % n_cols == expert) & (lane < 3 * n_cols)
    return lax.dot_general(
        jnp.where(chosen, 1.0, 0.0).astype(jnp.bfloat16), plane[:, columns:], contract_last, preferred_element_type=jnp.float32
    )


def weights_kernel(wgu_hbm, wdn_hbm, weights_ref, sems):
    split = wgu_hbm.shape[0]
    copies = [
        pltpu.make_async_copy(wgu_hbm, weights_ref.at[pl.ds(0, split)], sems.at[0]),
        pltpu.make_async_copy(wdn_hbm, weights_ref.at[pl.ds(split, wdn_hbm.shape[0])], sems.at[1]),
    ]
    for copy in copies:
        copy.start()
    for copy in copies:
        copy.wait()


def forward_kernel(n_cols, n_rows, n_z, relocate_ref, *refs):
    near = refs[: n_rows + n_z - 1]
    far = refs[n_rows + n_z - 1 : 2 * n_rows + n_z - 2]
    weights_own, wgu_sib, wdn_sib, plane_out, acts_ref, one_ref, kept_ref, *rest = refs[2 * n_rows + n_z - 2 :]
    sent_refs = rest[: n_rows - 1]
    plane_ref, sem = rest[n_rows - 1 :]
    tok_dev = near[0].shape[0]
    for z in range(n_z):
        for d in range(n_rows):
            start = (z * n_rows + d) * tok_dev
            if z == 0:
                block = near[d][...]
            elif d == 0:
                block = near[n_rows + z - 1][...]
            else:
                block = far[d - 1][(z - 1) * tok_dev : z * tok_dev]
            plane_ref[start : start + tok_dev] = block
    keep = pltpu.make_async_copy(plane_ref, plane_out, sem)
    keep.start()
    units, width = wdn_sib.shape
    split = wgu_sib.shape[0]
    col_here = lax.axis_index("expert")
    lane = lax.broadcasted_iota(jnp.int32, (8, 128), 1)
    row = lax.broadcasted_iota(jnp.int32, (8, 128), 0)
    wanted = jnp.where(row == 0, col_here, col_here ^ 1)
    chosen = (row < 2) & (lane % n_cols == wanted) & (lane < 3 * n_cols)
    gate_rows = lax.dot_general(
        jnp.where(chosen, 1.0, 0.0).astype(jnp.bfloat16),
        plane_ref[:, 2 * width :],
        contract_last,
        preferred_element_type=jnp.float32,
    )
    rows_x = plane_ref[:, :width]
    rows_u = plane_ref[:, width : 2 * width]
    total = None
    for index, (wgu, wdn) in enumerate(((weights_own[:split], weights_own[split:]), (wgu_sib[...], wdn_sib[...]))):
        gate = gate_rows[index : index + 1, :]
        pre = lax.dot_general(wgu, rows_x, contract_last, preferred_element_type=jnp.float32)
        hidden_grad = gate * lax.dot_general(wdn, rows_u, contract_last, preferred_element_type=jnp.float32)
        activated, slope_of = silu_parts(pre[:units])
        up_pre = pre[units:]
        base = index * 3 * units
        acts_ref[base : base + units] = (hidden_grad * up_pre * slope_of).astype(jnp.bfloat16)
        acts_ref[base + units : base + 2 * units] = (hidden_grad * activated).astype(jnp.bfloat16)
        acts_ref[base + 2 * units : base + 3 * units] = (activated * up_pre * gate).astype(jnp.bfloat16)
        part = lax.dot_general(acts_ref[base : base + 2 * units], wgu, contract_first, preferred_element_type=jnp.float32)
        total = part if total is None else total + part
    for z in range(n_z):
        for d in range(n_rows):
            start = (z * n_rows + d) * tok_dev
            block = total[start : start + tok_dev]
            if d == 0:
                kept_ref[z] = block
            else:
                sent_refs[d - 1][z] = block.astype(jnp.bfloat16)
    one_ref[...] = jnp.where(relocate_ref[col_here, 0] == 1, acts_ref[: 3 * units], acts_ref[3 * units :])
    keep.wait()


def weight_grad_kernel(same_ref, cross_ref, plane_ref, other_ref, gu_ref, dn_ref):
    units, width = dn_ref.shape
    for out, low, start in ((gu_ref, 0, 0), (dn_ref, 2 * units, width)):
        high = low + out.shape[0]
        out[...] = (
            jnp.dot(same_ref[low:high], plane_ref[:, start : start + width], preferred_element_type=jnp.float32)
            + jnp.dot(cross_ref[low:high], other_ref[:, start : start + width], preferred_element_type=jnp.float32)
        ).astype(jnp.bfloat16)


def join_kernel(*refs):
    joined_ref = refs[-1]
    start = 0
    for block in refs[:-1]:
        joined_ref[start : start + block.shape[0]] = block[...]
        start += block.shape[0]


def sum_kernel(kept_ref, *refs):
    n_z = kept_ref.shape[0]
    got, outs = refs[:-n_z], refs[-n_z:]
    for z, out in enumerate(outs):
        total = kept_ref[z]
        for block in got:
            total += block[z].astype(jnp.float32)
        out[...] = total.astype(out.dtype)


def final_kernel(kept_ref, *refs):
    total = kept_ref[...]
    for block in refs[:-1]:
        total += block[...].astype(jnp.float32)
    refs[-1][...] = total.astype(jnp.bfloat16)


def place_kernel(moving, relocate_ref, acts_ref, *refs):
    *arrived, same_ref, other_ref = refs
    rows, lanes = same_ref.shape
    half = lanes // 2
    col_here = lax.axis_index("expert")
    both = None if 2 not in moving else arrived[-1]
    one = None if 1 not in moving else arrived[0]
    for out, low, col in ((same_ref, 0, col_here), (other_ref, rows, col_here ^ 1)):
        if both is None:
            come = one[...]
        elif one is None:
            come = both[low : low + rows]
        else:
            chip = col_here // 2 % len(moving)
            come = jnp.where(chip == moving.index(1), one[...], both[low : low + rows])
        moved = relocate_ref[col, 0] == 1
        out[:, :half] = jnp.where(moved, come[:, half:], acts_ref[low : low + rows, :half])
        out[:, half:] = jnp.where(moved, come[:, :half], acts_ref[low : low + rows, half:])


def small(megabytes, flops=0, moved=0):
    return dict(
        compiler_params=pltpu.CompilerParams(vmem_limit_bytes=megabytes * 2**20),
        cost_estimate=pl.CostEstimate(flops=flops, bytes_accessed=moved, transcendentals=0),
    )


def exchanges(moving, relocate, acts, one, plane, kept, sent_rows):
    n_cols = lax.axis_size("expert")
    half = n_cols // 2
    placed = jax.ShapeDtypeStruct(one.shape, one.dtype)
    block = kept.shape[1:]

    def route(count):
        return [(col, col ^ half) for col in range(n_cols) if moving[col % half // 2] == count]

    arrived = []
    if 1 in moving:
        arrived.append(lax.ppermute(one, "expert", route(1)))
    if 2 in moving:
        arrived.append(lax.ppermute(acts, "expert", route(2)))
    plane_sib = crossed(plane, "expert", 1)
    got = [crossed(rows, "dp", d + 1) for d, rows in enumerate(sent_rows)]
    parts = pl.pallas_call(
        sum_kernel,
        out_shape=[jax.ShapeDtypeStruct(block, jnp.float32)] + [jax.ShapeDtypeStruct(block, jnp.bfloat16)] * (half - 1),
        in_specs=whole(1 + len(got)),
        out_specs=whole(half),
        name="sums",
        **small(4),
    )(kept, *got)
    same, others = pl.pallas_call(
        functools.partial(place_kernel, moving),
        out_shape=[placed, placed],
        in_specs=[pl.BlockSpec(memory_space=pltpu.SMEM)] + whole(1 + len(arrived)),
        out_specs=whole(2),
        name="place",
        **small(4),
    )(relocate, acts, *arrived)
    return same, others, plane_sib, parts


def dense_device(tokens, upstream, expert_ids, gates, relocate, w_gate_up, w_down):
    n_rows = lax.axis_size("dp")
    n_cols = lax.axis_size("expert")
    n_z = n_cols // 2
    tok_dev = tokens.shape[0]
    half = n_cols // 2
    units, width = w_down.shape[2:]
    plane_rows = n_rows * n_z * tok_dev
    bf16 = jnp.bfloat16

    wgu_own, wdn_own = w_gate_up[0, 0], w_down[0, 0]
    wgu_sib = crossed(wgu_own, "expert", 1)
    wdn_sib = crossed(wdn_own, "expert", 1)
    own = packed(tokens, upstream, expert_ids, gates, n_cols)
    own, wgu_sib, wdn_sib, flags = lax.optimization_barrier((own, wgu_sib, wdn_sib, relocate[:, 0]))
    along_z = [crossed(own, "expert", 2 * dz) for dz in range(1, n_z)]
    along_dp = [crossed(own, "dp", d) for d in range(1, n_rows)]
    pairs = half // 2
    case = jnp.sum(flags[:half] * jnp.array([3 ** (pairs - 1 - col // 2) for col in range(half)], jnp.int32)) - 1
    order = along_z[:1] + along_dp[1:] + along_z[1:] + along_dp[:1]
    order, case, wgu_own, wdn_own = lax.optimization_barrier((order, case, wgu_own, wdn_own))
    along_z, along_dp = order[:1] + order[n_rows - 1 : -1], order[-1:] + order[1 : n_rows - 1]
    far = pl.pallas_call(
        join_kernel,
        out_shape=jax.ShapeDtypeStruct((tok_dev * (n_z - 1), own.shape[1]), bf16),
        in_specs=whole(n_z - 1),
        out_specs=whole(1)[0],
        name="join",
        **small(4),
    )(*along_z)
    weights_own = pl.pallas_call(
        weights_kernel,
        out_shape=jax.ShapeDtypeStruct((3 * units, width), bf16),
        in_specs=[pl.BlockSpec(memory_space=pl.ANY)] * 2,
        out_specs=whole(1)[0],
        scratch_shapes=[pltpu.SemaphoreType.DMA((2,))],
        name="weights",
        **small(4),
    )(wgu_own, wdn_own)
    far_dp = [crossed(far, "dp", d) for d in range(1, n_rows - 1)]
    far_last, weights_own = lax.optimization_barrier((far, weights_own))
    far_dp.append(crossed(far_last, "dp", n_rows - 1))
    plane, acts, one, kept, *sent = pl.pallas_call(
        functools.partial(forward_kernel, n_cols, n_rows, n_z),
        out_shape=[
            jax.ShapeDtypeStruct((plane_rows, own.shape[1]), bf16),
            jax.ShapeDtypeStruct((6 * units, plane_rows), bf16),
            jax.ShapeDtypeStruct((3 * units, plane_rows), bf16),
            jax.ShapeDtypeStruct((n_z, tok_dev, width), jnp.float32),
        ]
        + [jax.ShapeDtypeStruct((n_z, tok_dev, width), bf16)] * (n_rows - 1),
        in_specs=[pl.BlockSpec(memory_space=pltpu.SMEM)] + whole(2 * n_rows + n_z + 1),
        out_specs=[pl.BlockSpec(memory_space=pltpu.HBM)] + whole(2 + n_rows),
        scratch_shapes=[pltpu.VMEM((plane_rows, own.shape[1]), bf16), pltpu.SemaphoreType.DMA],
        name="forward",
        **small(16, flops=2 * 6 * units * 2 * width * plane_rows, moved=8 * 2**20),
    )(relocate, own, *along_dp, *along_z, *far_dp, weights_own, wgu_sib, wdn_sib)

    cases = [tuple(number // 3 ** (pairs - 1 - p) % 3 for p in range(pairs)) for number in range(1, 3**pairs - 1)]
    same, others, plane_sib, parts = lax.switch(
        case, [functools.partial(exchanges, moving) for moving in cases], relocate, acts, one, plane, kept, sent
    )
    cross = crossed(others, "expert", 1)
    got_z = [crossed(parts[dz], "expert", 2 * dz) for dz in range(1, n_z)]
    grad_gu, grad_dn = pl.pallas_call(
        weight_grad_kernel,
        out_shape=[jax.ShapeDtypeStruct((2 * units, width), bf16), jax.ShapeDtypeStruct((units, width), bf16)],
        in_specs=whole(4),
        out_specs=whole(2),
        name="weight_grads",
        **small(16, flops=2 * 3 * units * width * 2 * plane_rows * 8, moved=32 * 2**20),
    )(same, cross, plane, plane_sib)
    kept, grad_dn = lax.optimization_barrier((parts[0], grad_dn))
    grad_tokens = pl.pallas_call(
        final_kernel,
        out_shape=jax.ShapeDtypeStruct((tok_dev, width), bf16),
        in_specs=whole(n_z),
        out_specs=whole(1)[0],
        name="grad_tokens",
        **small(4),
    )(kept, *got_z)
    return grad_tokens, grad_gu.reshape(w_gate_up.shape), grad_dn.reshape(w_down.shape)


def solution(mesh):
    def per_device(*arrays):
        n_rows, n_cols = mesh.shape["dp"], mesh.shape["expert"]
        dense = n_rows == SLICES and arrays[2].shape[1] == n_cols and 4 <= n_cols <= 8
        return (dense_device if dense else routed_device)(*arrays)

    return jax.shard_map(
        per_device,
        mesh=mesh,
        in_specs=(
            P(("dp", "expert"), None),
            P(("dp", "expert"), None),
            P(("dp", "expert"), None),
            P(("dp", "expert"), None),
            P(),
            P("expert", "dp", None, None),
            P("expert", "dp", None, None),
        ),
        out_specs=(
            P(("dp", "expert"), None),
            P("expert", "dp", None, None),
            P("expert", "dp", None, None),
        ),
        check_vma=False,
    )
```

```python
import functools

import jax
import jax.numpy as jnp
from jax import lax
from jax.experimental import pallas as pl
from jax.experimental.pallas import tpu as pltpu
from jax.sharding import PartitionSpec as P

SLICES = 4


contract_last = (((1,), (1,)), ((), ()))
contract_first = (((0,), (0,)), ((), ()))


def swapped(block, axis, apart):
    count = lax.axis_size(axis)
    route = []
    for low in range(count):
        high = low | 1 << apart
        if high != low and high < count:
            route += [(low, high), (high, low)]
    return lax.ppermute(block, axis, route)


def silu_parts(values_in):
    sigmoid_of = jax.nn.sigmoid(values_in)
    return (values_in * sigmoid_of, sigmoid_of * (1.0 + values_in * (1.0 - sigmoid_of)))


def pick_entry(lookup_table, row_index, col_index):
    rows_hit = jnp.arange(lookup_table.shape[0], dtype=jnp.int32)[:, None] == row_index
    cols_hit = jnp.arange(lookup_table.shape[1], dtype=jnp.int32)[None, :] == col_index
    return jnp.sum(jnp.where(rows_hit & cols_hit, lookup_table, 0))


def routed_device(tokens, upstream, expert_ids, gates, relocate, w_gate_up, w_down):
    n_rows = lax.axis_size("dp")
    n_cols = lax.axis_size("expert")
    slot_count = n_rows // SLICES
    experts = slot_count * n_cols
    tok_dev, feature_width = tokens.shape
    top_count = expert_ids.shape[1]
    capacity = min(tok_dev, max(2, (3 * tok_dev * top_count + 2 * experts - 1) // (2 * experts)))
    pair_count = tok_dev * top_count
    buffer_rows = experts * capacity
    slice_width = w_down.shape[2]
    col_block = n_cols // SLICES
    col_here = lax.axis_index("expert")
    row_here = lax.axis_index("dp")
    slot_here = row_here // SLICES
    slice_here = row_here % SLICES
    far_bit = n_cols.bit_length() - 2
    half_cols = n_cols // 2
    flat_ids = expert_ids.reshape(pair_count)
    home_column = flat_ids // slot_count
    slot_of = flat_ids % slot_count
    expert_iota = jnp.arange(experts, dtype=jnp.int32)
    relocated = jnp.sum(
        jnp.where(flat_ids[:, None] == expert_iota[None, :], relocate.reshape(experts)[None, :], 0),
        axis=1,
    )
    column = (home_column + half_cols * relocated) % n_cols
    pair_iota = jnp.arange(pair_count, dtype=jnp.int32)
    earlier = (flat_ids[:, None] == flat_ids[None, :]) & (pair_iota[None, :] < pair_iota[:, None])
    slot_rank = jnp.sum(earlier.astype(jnp.int32), axis=1)
    target = (slot_of * n_cols + column) * capacity + slot_rank
    placing = (target[None, :] == jnp.arange(buffer_rows, dtype=jnp.int32)[:, None]).astype(
        jnp.bfloat16
    )
    x_pairs = jnp.repeat(tokens, top_count, axis=0)
    d_pairs = (
        gates.reshape(pair_count, 1) * jnp.repeat(upstream, top_count, axis=0).astype(jnp.float32)
    ).astype(jnp.bfloat16)
    pair_data = jnp.stack([x_pairs, d_pairs])
    sent = jnp.einsum("bp,kpw->kbw", placing, pair_data, preferred_element_type=jnp.float32).astype(
        jnp.bfloat16
    )
    sent = sent.reshape(2, slot_count, n_cols, capacity, feature_width)
    at_column = lax.all_to_all(sent, "expert", split_axis=2, concat_axis=2, tiled=True)
    swapped_here = pick_entry(relocate, col_here, slot_here)
    own_pack = jnp.concatenate([w_gate_up, w_down], axis=2)
    far_pack = swapped(own_pack, "expert", far_bit)
    own_pack = jnp.where(swapped_here == 1, far_pack, own_pack)
    gate_up = own_pack[0, 0, : 2 * slice_width]
    down_rows = own_pack[0, 0, 2 * slice_width :]
    grouped = at_column.reshape(2, n_rows, col_block, capacity, feature_width)
    at_row = lax.all_to_all(grouped, "dp", split_axis=1, concat_axis=1, tiled=True)
    gathered = at_row[:, None]
    for bit_index in range(SLICES.bit_length() - 1):
        far_rows = swapped(gathered, "dp", bit_index)
        lower_half = slice_here // (1 << bit_index) % 2 == 0
        first_part = jnp.where(lower_half, gathered, far_rows)
        second_part = jnp.where(lower_half, far_rows, gathered)
        gathered = jnp.concatenate([first_part, second_part], axis=1)
    all_rows = gathered.reshape(2, -1, feature_width)
    rows_x = all_rows[0]
    rows_d = all_rows[1]
    gate_and_up = lax.dot_general(
        rows_x, gate_up, contract_last, preferred_element_type=jnp.float32
    )
    gate_pre = gate_and_up[:, :slice_width]
    up_pre = gate_and_up[:, slice_width:]
    activated, slope_of = silu_parts(gate_pre)
    hidden = (activated * up_pre).astype(jnp.bfloat16)
    hidden_grad = lax.dot_general(
        rows_d, down_rows, contract_last, preferred_element_type=jnp.float32
    )
    pre_grads = jnp.concatenate(
        [
            (hidden_grad * up_pre * slope_of).astype(jnp.bfloat16),
            (hidden_grad * activated).astype(jnp.bfloat16),
        ],
        axis=1,
    )
    grad_gu = lax.dot_general(
        pre_grads, rows_x, contract_first, preferred_element_type=jnp.float32
    ).astype(jnp.bfloat16)
    grad_dn = lax.dot_general(
        hidden, rows_d, contract_first, preferred_element_type=jnp.float32
    ).astype(jnp.bfloat16)
    slice_part = jnp.dot(pre_grads, gate_up, preferred_element_type=jnp.float32).astype(
        jnp.bfloat16
    )
    grad_pack = jnp.concatenate([grad_gu, grad_dn], axis=0)
    blocks = slice_part.reshape(2, 2, n_rows, col_block, capacity, feature_width)
    upper_half = slice_here // 2 % 2 == 1
    keep_half = jnp.where(upper_half, blocks[1], blocks[0])
    send_half = jnp.where(upper_half, blocks[0], blocks[1])
    got_half = swapped(send_half, "dp", 1)
    pairsum = keep_half.astype(jnp.float32) + got_half.astype(jnp.float32)
    odd_slice = slice_here % 2 == 1
    keep_last = jnp.where(odd_slice, pairsum[1], pairsum[0])
    send_last = jnp.where(odd_slice, pairsum[0], pairsum[1])
    got_last = swapped(send_last, "dp", 0)
    summed = keep_last + got_last
    back_rows = lax.all_to_all(summed, "dp", split_axis=0, concat_axis=0, tiled=True).reshape(
        slot_count, n_cols, capacity, feature_width
    )
    home_rows = lax.all_to_all(
        back_rows, "expert", split_axis=1, concat_axis=1, tiled=True
    ).reshape(buffer_rows, feature_width)
    hits = (
        target.reshape(tok_dev, top_count)[:, :, None]
        == jnp.arange(buffer_rows, dtype=jnp.int32)[None, None, :]
    )
    gather_mat = jnp.sum(hits.astype(jnp.float32), axis=1)
    grad_tokens = jnp.dot(
        gather_mat, home_rows, precision=lax.Precision.HIGHEST, preferred_element_type=jnp.float32
    ).astype(jnp.bfloat16)
    grad_gate_up = grad_pack[: 2 * slice_width].reshape(w_gate_up.shape)
    grad_down = grad_pack[2 * slice_width :].reshape(w_down.shape)
    return (grad_tokens, grad_gate_up, grad_down)


def crossed(block, axis, apart):
    return lax.ppermute(block, axis, [(i, i ^ apart) for i in range(lax.axis_size(axis))])


def whole(count):
    return [pl.BlockSpec(memory_space=pltpu.VMEM)] * count


def packed(tokens, upstream, expert_ids, gates, n_cols):
    experts = jnp.arange(n_cols, dtype=jnp.int32)[None, None, :]
    by_expert = jnp.sum(jnp.where(expert_ids[:, :, None] == experts, gates[:, :, None], 0.0), axis=1)
    high = lax.reduce_precision(by_expert, 8, 7)
    middle = lax.reduce_precision(by_expert - high, 8, 7)
    low = by_expert - high - middle
    spare = jnp.zeros((tokens.shape[0], 128 - 3 * n_cols), jnp.bfloat16)
    summands = [part.astype(jnp.bfloat16) for part in (high, middle, low)]
    return jnp.concatenate([tokens, upstream] + summands + [spare], axis=1)


def weights_kernel(wgu_hbm, wdn_hbm, weights_ref, sems):
    split = wgu_hbm.shape[0]
    copies = [
        pltpu.make_async_copy(wgu_hbm, weights_ref.at[pl.ds(0, split)], sems.at[0]),
        pltpu.make_async_copy(wdn_hbm, weights_ref.at[pl.ds(split, wdn_hbm.shape[0])], sems.at[1]),
    ]
    for copy in copies:
        copy.start()
    for copy in copies:
        copy.wait()


def forward_kernel(n_cols, n_rows, n_z, relocate_ref, *refs):
    near = refs[:n_rows]
    far = refs[n_rows : 2 * n_rows]
    weights_own, wgu_sib, wdn_sib, case_ref, plane_out, acts_ref, one_ref, kept_ref, *rest = refs[2 * n_rows :]
    sent_refs = rest[: n_rows - 1]
    plane_ref, sem = rest[n_rows - 1 :]
    tok_dev = near[0].shape[0]
    pairs = n_cols // 4
    case_ref[0] = sum(relocate_ref[col] * 3 ** (pairs - 1 - col // 2) for col in range(n_cols // 2)) - 1
    for z in range(n_z):
        for d in range(n_rows):
            start = (z * n_rows + d) * tok_dev
            if z == 0:
                block = near[d][...]
            else:
                block = far[d][(z - 1) * tok_dev : z * tok_dev]
            plane_ref[start : start + tok_dev] = block
    keep = pltpu.make_async_copy(plane_ref, plane_out, sem)
    keep.start()
    units, width = wdn_sib.shape
    split = wgu_sib.shape[0]
    col_here = lax.axis_index("expert")
    lane = lax.broadcasted_iota(jnp.int32, (8, 128), 1)
    row = lax.broadcasted_iota(jnp.int32, (8, 128), 0)
    wanted = jnp.where(row == 0, col_here, col_here ^ 1)
    chosen = (row < 2) & (lane % n_cols == wanted) & (lane < 3 * n_cols)
    gate_rows = lax.dot_general(
        jnp.where(chosen, 1.0, 0.0).astype(jnp.bfloat16),
        plane_ref[:, 2 * width :],
        contract_last,
        preferred_element_type=jnp.float32,
    )
    rows_x = plane_ref[:, :width]
    rows_u = plane_ref[:, width : 2 * width]
    total = None
    for index, (wgu, wdn) in enumerate(((weights_own[:split], weights_own[split:]), (wgu_sib[...], wdn_sib[...]))):
        gate = gate_rows[index : index + 1, :]
        pre = lax.dot_general(wgu, rows_x, contract_last, preferred_element_type=jnp.float32)
        hidden_grad = gate * lax.dot_general(wdn, rows_u, contract_last, preferred_element_type=jnp.float32)
        activated, slope_of = silu_parts(pre[:units])
        up_pre = pre[units:]
        base = index * 3 * units
        acts_ref[base : base + units] = (hidden_grad * up_pre * slope_of).astype(jnp.bfloat16)
        acts_ref[base + units : base + 2 * units] = (hidden_grad * activated).astype(jnp.bfloat16)
        acts_ref[base + 2 * units : base + 3 * units] = (activated * up_pre * gate).astype(jnp.bfloat16)
        part = lax.dot_general(acts_ref[base : base + 2 * units], wgu, contract_first, preferred_element_type=jnp.float32)
        total = part if total is None else total + part
    for z in range(n_z):
        for d in range(n_rows):
            start = (z * n_rows + d) * tok_dev
            block = total[start : start + tok_dev]
            if d == 0:
                kept_ref[z] = block
            else:
                sent_refs[d - 1][z] = block.astype(jnp.bfloat16)
    one_ref[...] = jnp.where(relocate_ref[col_here] == 1, acts_ref[: 3 * units], acts_ref[3 * units :])
    keep.wait()


def weight_grad_kernel(same_ref, cross_ref, plane_ref, other_ref, gu_ref, dn_ref):
    units, width = dn_ref.shape
    for out, low, start in ((gu_ref, 0, 0), (dn_ref, 2 * units, width)):
        high = low + out.shape[0]
        out[...] = (
            jnp.dot(same_ref[low:high], plane_ref[:, start : start + width], preferred_element_type=jnp.float32)
            + jnp.dot(cross_ref[low:high], other_ref[:, start : start + width], preferred_element_type=jnp.float32)
        ).astype(jnp.bfloat16)


def join_kernel(*refs):
    joined_ref = refs[-1]
    start = 0
    for block in refs[:-1]:
        joined_ref[start : start + block.shape[0]] = block[...]
        start += block.shape[0]


def sum_kernel(kept_ref, *refs):
    n_z = kept_ref.shape[0]
    got, outs = refs[:-n_z], refs[-n_z:]
    for z, out in enumerate(outs):
        total = kept_ref[z]
        for block in got:
            total += block[z].astype(jnp.float32)
        out[...] = total.astype(out.dtype)


def final_kernel(kept_ref, *refs):
    total = kept_ref[...]
    for block in refs[:-1]:
        total += block[...].astype(jnp.float32)
    refs[-1][...] = total.astype(jnp.bfloat16)


def place_kernel(moving, relocate_ref, acts_ref, *refs):
    *arrived, same_ref, other_ref = refs
    rows, lanes = same_ref.shape
    half = lanes // 2
    col_here = lax.axis_index("expert")
    both = None if 2 not in moving else arrived[-1]
    one = None if 1 not in moving else arrived[0]
    for out, low, col in ((same_ref, 0, col_here), (other_ref, rows, col_here ^ 1)):
        if both is None:
            come = one[...]
        elif one is None:
            come = both[low : low + rows]
        else:
            chip = col_here // 2 % len(moving)
            come = jnp.where(chip == moving.index(1), one[...], both[low : low + rows])
        moved = relocate_ref[col] == 1
        out[:, :half] = jnp.where(moved, come[:, half:], acts_ref[low : low + rows, :half])
        out[:, half:] = jnp.where(moved, come[:, :half], acts_ref[low : low + rows, half:])


def small(megabytes, flops=0, moved=0):
    return dict(
        compiler_params=pltpu.CompilerParams(vmem_limit_bytes=megabytes * 2**20),
        cost_estimate=pl.CostEstimate(flops=flops, bytes_accessed=moved, transcendentals=0),
    )


def exchanges(moving, relocate, acts, one, kept, sent_rows):
    n_cols = lax.axis_size("expert")
    half = n_cols // 2
    placed = jax.ShapeDtypeStruct(one.shape, one.dtype)
    block = kept.shape[1:]

    def route(count):
        return [(col, col ^ half) for col in range(n_cols) if moving[col % half // 2] == count]

    arrived = []
    if 1 in moving:
        arrived.append(lax.ppermute(one, "expert", route(1)))
    if 2 in moving:
        arrived.append(lax.ppermute(acts, "expert", route(2)))
    got = [crossed(rows, "dp", d + 1) for d, rows in enumerate(sent_rows)]
    parts = pl.pallas_call(
        sum_kernel,
        out_shape=[jax.ShapeDtypeStruct(block, jnp.float32)] + [jax.ShapeDtypeStruct(block, jnp.bfloat16)] * (half - 1),
        in_specs=whole(1 + len(got)),
        out_specs=whole(half),
        name="sums",
        **small(4),
    )(kept, *got)
    same, others = pl.pallas_call(
        functools.partial(place_kernel, moving),
        out_shape=[placed, placed],
        in_specs=[pl.BlockSpec(memory_space=pltpu.SMEM)] + whole(1 + len(arrived)),
        out_specs=whole(2),
        name="place",
        **small(4),
    )(relocate, acts, *arrived)
    return same, others, parts


def dense_device(tokens, upstream, expert_ids, gates, relocate, w_gate_up, w_down):
    n_rows = lax.axis_size("dp")
    n_cols = lax.axis_size("expert")
    n_z = n_cols // 2
    tok_dev = tokens.shape[0]
    half = n_cols // 2
    units, width = w_down.shape[2:]
    plane_rows = n_rows * n_z * tok_dev
    bf16 = jnp.bfloat16

    wgu_own, wdn_own = w_gate_up[0, 0], w_down[0, 0]
    wgu_sib = crossed(wgu_own, "expert", 1)
    wdn_sib = crossed(wdn_own, "expert", 1)
    own = packed(tokens, upstream, expert_ids, gates, n_cols)
    own, wgu_sib, wdn_sib = lax.optimization_barrier((own, wgu_sib, wdn_sib))
    along_z = [crossed(own, "expert", 2 * dz) for dz in range(1, n_z)]
    along_dp = [crossed(own, "dp", d) for d in range(1, n_rows)]
    pairs = half // 2
    order = along_z[:1] + along_dp[1:] + along_z[1:] + along_dp[:1]
    order, wgu_own, wdn_own = lax.optimization_barrier((order, wgu_own, wdn_own))
    along_z, along_dp = order[:1] + order[n_rows - 1 : -1], order[-1:] + order[1 : n_rows - 1]
    far = pl.pallas_call(
        join_kernel,
        out_shape=jax.ShapeDtypeStruct((tok_dev * (n_z - 1), own.shape[1]), bf16),
        in_specs=whole(n_z - 1),
        out_specs=whole(1)[0],
        name="join",
        **small(4),
    )(*along_z)
    weights_own = pl.pallas_call(
        weights_kernel,
        out_shape=jax.ShapeDtypeStruct((3 * units, width), bf16),
        in_specs=[pl.BlockSpec(memory_space=pl.ANY)] * 2,
        out_specs=whole(1)[0],
        scratch_shapes=[pltpu.SemaphoreType.DMA((2,))],
        name="weights",
        **small(4),
    )(wgu_own, wdn_own)
    far_dp = [crossed(far, "dp", d) for d in range(1, n_rows - 1)]
    far_last, weights_own = lax.optimization_barrier((far, weights_own))
    far_dp.append(crossed(far_last, "dp", n_rows - 1))
    case, plane, acts, one, kept, *sent = pl.pallas_call(
        functools.partial(forward_kernel, n_cols, n_rows, n_z),
        out_shape=[
            jax.ShapeDtypeStruct((1,), jnp.int32),
            jax.ShapeDtypeStruct((plane_rows, own.shape[1]), bf16),
            jax.ShapeDtypeStruct((6 * units, plane_rows), bf16),
            jax.ShapeDtypeStruct((3 * units, plane_rows), bf16),
            jax.ShapeDtypeStruct((n_z, tok_dev, width), jnp.float32),
        ]
        + [jax.ShapeDtypeStruct((n_z, tok_dev, width), bf16)] * (n_rows - 1),
        in_specs=[pl.BlockSpec(memory_space=pltpu.SMEM)] + whole(2 * n_rows + 3),
        out_specs=[pl.BlockSpec(memory_space=pltpu.SMEM), pl.BlockSpec(memory_space=pltpu.HBM)] + whole(2 + n_rows),
        scratch_shapes=[pltpu.VMEM((plane_rows, own.shape[1]), bf16), pltpu.SemaphoreType.DMA],
        name="forward",
        **small(16, flops=2 * 6 * units * 2 * width * plane_rows, moved=8 * 2**20),
    )(relocate[:, 0], own, *along_dp, far, *far_dp, weights_own, wgu_sib, wdn_sib)

    plane_sib = crossed(plane, "expert", 1)
    cases = [tuple(number // 3 ** (pairs - 1 - p) % 3 for p in range(pairs)) for number in range(1, 3**pairs - 1)]
    same, others, parts = lax.switch(
        case[0], [functools.partial(exchanges, moving) for moving in cases], relocate[:, 0], acts, one, kept, sent
    )
    cross = crossed(others, "expert", 1)
    got_z = [crossed(parts[dz], "expert", 2 * dz) for dz in range(1, n_z)]
    grad_gu, grad_dn = pl.pallas_call(
        weight_grad_kernel,
        out_shape=[jax.ShapeDtypeStruct((2 * units, width), bf16), jax.ShapeDtypeStruct((units, width), bf16)],
        in_specs=whole(4),
        out_specs=whole(2),
        name="weight_grads",
        **small(16, flops=2 * 3 * units * width * 2 * plane_rows * 8, moved=32 * 2**20),
    )(same, cross, plane, plane_sib)
    kept, grad_dn = lax.optimization_barrier((parts[0], grad_dn))
    grad_tokens = pl.pallas_call(
        final_kernel,
        out_shape=jax.ShapeDtypeStruct((tok_dev, width), bf16),
        in_specs=whole(n_z),
        out_specs=whole(1)[0],
        name="grad_tokens",
        **small(4),
    )(kept, *got_z)
    return grad_tokens, grad_gu.reshape(w_gate_up.shape), grad_dn.reshape(w_down.shape)


def solution(mesh):
    def per_device(*arrays):
        n_rows, n_cols = mesh.shape["dp"], mesh.shape["expert"]
        dense = n_rows == SLICES and arrays[2].shape[1] == n_cols and 4 <= n_cols <= 8
        return (dense_device if dense else routed_device)(*arrays)

    return jax.shard_map(
        per_device,
        mesh=mesh,
        in_specs=(
            P(("dp", "expert"), None),
            P(("dp", "expert"), None),
            P(("dp", "expert"), None),
            P(("dp", "expert"), None),
            P(),
            P("expert", "dp", None, None),
            P("expert", "dp", None, None),
        ),
        out_specs=(
            P(("dp", "expert"), None),
            P("expert", "dp", None, None),
            P("expert", "dp", None, None),
        ),
        check_vma=False,
    )
```

```python
import functools

import jax
import jax.numpy as jnp
from jax import lax
from jax.experimental import pallas as pl
from jax.experimental.pallas import tpu as pltpu
from jax.sharding import PartitionSpec as P

SLICES = 4


contract_last = (((1,), (1,)), ((), ()))
contract_first = (((0,), (0,)), ((), ()))


def swapped(block, axis, apart):
    count = lax.axis_size(axis)
    route = []
    for low in range(count):
        high = low | 1 << apart
        if high != low and high < count:
            route += [(low, high), (high, low)]
    return lax.ppermute(block, axis, route)


def silu_parts(values_in):
    sigmoid_of = jax.nn.sigmoid(values_in)
    return (values_in * sigmoid_of, sigmoid_of * (1.0 + values_in * (1.0 - sigmoid_of)))


def pick_entry(lookup_table, row_index, col_index):
    rows_hit = jnp.arange(lookup_table.shape[0], dtype=jnp.int32)[:, None] == row_index
    cols_hit = jnp.arange(lookup_table.shape[1], dtype=jnp.int32)[None, :] == col_index
    return jnp.sum(jnp.where(rows_hit & cols_hit, lookup_table, 0))


def routed_device(tokens, upstream, expert_ids, gates, relocate, w_gate_up, w_down):
    n_rows = lax.axis_size("dp")
    n_cols = lax.axis_size("expert")
    slot_count = n_rows // SLICES
    experts = slot_count * n_cols
    tok_dev, feature_width = tokens.shape
    top_count = expert_ids.shape[1]
    capacity = min(tok_dev, max(2, (3 * tok_dev * top_count + 2 * experts - 1) // (2 * experts)))
    pair_count = tok_dev * top_count
    buffer_rows = experts * capacity
    slice_width = w_down.shape[2]
    col_block = n_cols // SLICES
    col_here = lax.axis_index("expert")
    row_here = lax.axis_index("dp")
    slot_here = row_here // SLICES
    slice_here = row_here % SLICES
    far_bit = n_cols.bit_length() - 2
    half_cols = n_cols // 2
    flat_ids = expert_ids.reshape(pair_count)
    home_column = flat_ids // slot_count
    slot_of = flat_ids % slot_count
    expert_iota = jnp.arange(experts, dtype=jnp.int32)
    relocated = jnp.sum(
        jnp.where(flat_ids[:, None] == expert_iota[None, :], relocate.reshape(experts)[None, :], 0),
        axis=1,
    )
    column = (home_column + half_cols * relocated) % n_cols
    pair_iota = jnp.arange(pair_count, dtype=jnp.int32)
    earlier = (flat_ids[:, None] == flat_ids[None, :]) & (pair_iota[None, :] < pair_iota[:, None])
    slot_rank = jnp.sum(earlier.astype(jnp.int32), axis=1)
    target = (slot_of * n_cols + column) * capacity + slot_rank
    placing = (target[None, :] == jnp.arange(buffer_rows, dtype=jnp.int32)[:, None]).astype(
        jnp.bfloat16
    )
    x_pairs = jnp.repeat(tokens, top_count, axis=0)
    d_pairs = (
        gates.reshape(pair_count, 1) * jnp.repeat(upstream, top_count, axis=0).astype(jnp.float32)
    ).astype(jnp.bfloat16)
    pair_data = jnp.stack([x_pairs, d_pairs])
    sent = jnp.einsum("bp,kpw->kbw", placing, pair_data, preferred_element_type=jnp.float32).astype(
        jnp.bfloat16
    )
    sent = sent.reshape(2, slot_count, n_cols, capacity, feature_width)
    at_column = lax.all_to_all(sent, "expert", split_axis=2, concat_axis=2, tiled=True)
    swapped_here = pick_entry(relocate, col_here, slot_here)
    own_pack = jnp.concatenate([w_gate_up, w_down], axis=2)
    far_pack = swapped(own_pack, "expert", far_bit)
    own_pack = jnp.where(swapped_here == 1, far_pack, own_pack)
    gate_up = own_pack[0, 0, : 2 * slice_width]
    down_rows = own_pack[0, 0, 2 * slice_width :]
    grouped = at_column.reshape(2, n_rows, col_block, capacity, feature_width)
    at_row = lax.all_to_all(grouped, "dp", split_axis=1, concat_axis=1, tiled=True)
    gathered = at_row[:, None]
    for bit_index in range(SLICES.bit_length() - 1):
        far_rows = swapped(gathered, "dp", bit_index)
        lower_half = slice_here // (1 << bit_index) % 2 == 0
        first_part = jnp.where(lower_half, gathered, far_rows)
        second_part = jnp.where(lower_half, far_rows, gathered)
        gathered = jnp.concatenate([first_part, second_part], axis=1)
    all_rows = gathered.reshape(2, -1, feature_width)
    rows_x = all_rows[0]
    rows_d = all_rows[1]
    gate_and_up = lax.dot_general(
        rows_x, gate_up, contract_last, preferred_element_type=jnp.float32
    )
    gate_pre = gate_and_up[:, :slice_width]
    up_pre = gate_and_up[:, slice_width:]
    activated, slope_of = silu_parts(gate_pre)
    hidden = (activated * up_pre).astype(jnp.bfloat16)
    hidden_grad = lax.dot_general(
        rows_d, down_rows, contract_last, preferred_element_type=jnp.float32
    )
    pre_grads = jnp.concatenate(
        [
            (hidden_grad * up_pre * slope_of).astype(jnp.bfloat16),
            (hidden_grad * activated).astype(jnp.bfloat16),
        ],
        axis=1,
    )
    grad_gu = lax.dot_general(
        pre_grads, rows_x, contract_first, preferred_element_type=jnp.float32
    ).astype(jnp.bfloat16)
    grad_dn = lax.dot_general(
        hidden, rows_d, contract_first, preferred_element_type=jnp.float32
    ).astype(jnp.bfloat16)
    slice_part = jnp.dot(pre_grads, gate_up, preferred_element_type=jnp.float32).astype(
        jnp.bfloat16
    )
    grad_pack = jnp.concatenate([grad_gu, grad_dn], axis=0)
    blocks = slice_part.reshape(2, 2, n_rows, col_block, capacity, feature_width)
    upper_half = slice_here // 2 % 2 == 1
    keep_half = jnp.where(upper_half, blocks[1], blocks[0])
    send_half = jnp.where(upper_half, blocks[0], blocks[1])
    got_half = swapped(send_half, "dp", 1)
    pairsum = keep_half.astype(jnp.float32) + got_half.astype(jnp.float32)
    odd_slice = slice_here % 2 == 1
    keep_last = jnp.where(odd_slice, pairsum[1], pairsum[0])
    send_last = jnp.where(odd_slice, pairsum[0], pairsum[1])
    got_last = swapped(send_last, "dp", 0)
    summed = keep_last + got_last
    back_rows = lax.all_to_all(summed, "dp", split_axis=0, concat_axis=0, tiled=True).reshape(
        slot_count, n_cols, capacity, feature_width
    )
    home_rows = lax.all_to_all(
        back_rows, "expert", split_axis=1, concat_axis=1, tiled=True
    ).reshape(buffer_rows, feature_width)
    hits = (
        target.reshape(tok_dev, top_count)[:, :, None]
        == jnp.arange(buffer_rows, dtype=jnp.int32)[None, None, :]
    )
    gather_mat = jnp.sum(hits.astype(jnp.float32), axis=1)
    grad_tokens = jnp.dot(
        gather_mat, home_rows, precision=lax.Precision.HIGHEST, preferred_element_type=jnp.float32
    ).astype(jnp.bfloat16)
    grad_gate_up = grad_pack[: 2 * slice_width].reshape(w_gate_up.shape)
    grad_down = grad_pack[2 * slice_width :].reshape(w_down.shape)
    return (grad_tokens, grad_gate_up, grad_down)


def crossed(block, axis, apart):
    return lax.ppermute(block, axis, [(i, i ^ apart) for i in range(lax.axis_size(axis))])


def whole(count):
    return [pl.BlockSpec(memory_space=pltpu.VMEM)] * count


def packed(tokens, upstream, expert_ids, gates, n_cols):
    experts = jnp.arange(n_cols, dtype=jnp.int32)[None, None, :]
    by_expert = jnp.sum(jnp.where(expert_ids[:, :, None] == experts, gates[:, :, None], 0.0), axis=1)
    high = lax.reduce_precision(by_expert, 8, 7)
    middle = lax.reduce_precision(by_expert - high, 8, 7)
    low = by_expert - high - middle
    spare = jnp.zeros((tokens.shape[0], 128 - 3 * n_cols), jnp.bfloat16)
    summands = [part.astype(jnp.bfloat16) for part in (high, middle, low)]
    return jnp.concatenate([tokens, upstream] + summands + [spare], axis=1)


def weights_kernel(wgu_hbm, wdn_hbm, weights_ref, sems):
    split = wgu_hbm.shape[0]
    copies = [
        pltpu.make_async_copy(wgu_hbm, weights_ref.at[pl.ds(0, split)], sems.at[0]),
        pltpu.make_async_copy(wdn_hbm, weights_ref.at[pl.ds(split, wdn_hbm.shape[0])], sems.at[1]),
    ]
    for copy in copies:
        copy.start()
    for copy in copies:
        copy.wait()


def forward_kernel(n_cols, n_rows, n_z, relocate_ref, *refs):
    near = refs[:n_rows]
    far = refs[n_rows : 2 * n_rows]
    weights_own, wgu_sib, wdn_sib, case_ref, plane_ref, acts_ref, one_ref, kept_ref, *sent_refs = refs[2 * n_rows :]
    tok_dev = near[0].shape[0]
    pairs = n_cols // 4
    case_ref[0] = sum(relocate_ref[col] * 3 ** (pairs - 1 - col // 2) for col in range(n_cols // 2)) - 1
    for z in range(n_z):
        for d in range(n_rows):
            start = (z * n_rows + d) * tok_dev
            if z == 0:
                block = near[d][...]
            else:
                block = far[d][(z - 1) * tok_dev : z * tok_dev]
            plane_ref[start : start + tok_dev] = block
    units, width = wdn_sib.shape
    split = wgu_sib.shape[0]
    col_here = lax.axis_index("expert")
    lane = lax.broadcasted_iota(jnp.int32, (8, 128), 1)
    row = lax.broadcasted_iota(jnp.int32, (8, 128), 0)
    wanted = jnp.where(row == 0, col_here, col_here ^ 1)
    chosen = (row < 2) & (lane % n_cols == wanted) & (lane < 3 * n_cols)
    gate_rows = lax.dot_general(
        jnp.where(chosen, 1.0, 0.0).astype(jnp.bfloat16),
        plane_ref[:, 2 * width :],
        contract_last,
        preferred_element_type=jnp.float32,
    )
    rows_x = plane_ref[:, :width]
    rows_u = plane_ref[:, width : 2 * width]
    total = None
    for index, (wgu, wdn) in enumerate(((weights_own[:split], weights_own[split:]), (wgu_sib[...], wdn_sib[...]))):
        gate = gate_rows[index : index + 1, :]
        pre = lax.dot_general(wgu, rows_x, contract_last, preferred_element_type=jnp.float32)
        hidden_grad = gate * lax.dot_general(wdn, rows_u, contract_last, preferred_element_type=jnp.float32)
        activated, slope_of = silu_parts(pre[:units])
        up_pre = pre[units:]
        base = index * 3 * units
        acts_ref[base : base + units] = (hidden_grad * up_pre * slope_of).astype(jnp.bfloat16)
        acts_ref[base + units : base + 2 * units] = (hidden_grad * activated).astype(jnp.bfloat16)
        acts_ref[base + 2 * units : base + 3 * units] = (activated * up_pre * gate).astype(jnp.bfloat16)
        part = lax.dot_general(acts_ref[base : base + 2 * units], wgu, contract_first, preferred_element_type=jnp.float32)
        total = part if total is None else total + part
    for z in range(n_z):
        for d in range(n_rows):
            start = (z * n_rows + d) * tok_dev
            block = total[start : start + tok_dev]
            if d == 0:
                kept_ref[z] = block
            else:
                sent_refs[d - 1][z] = block.astype(jnp.bfloat16)
    one_ref[...] = jnp.where(relocate_ref[col_here] == 1, acts_ref[: 3 * units], acts_ref[3 * units :])


def weight_grad_kernel(same_ref, cross_ref, plane_ref, other_ref, gu_ref, dn_ref):
    units, width = dn_ref.shape
    for out, low, start in ((gu_ref, 0, 0), (dn_ref, 2 * units, width)):
        high = low + out.shape[0]
        out[...] = (
            jnp.dot(same_ref[low:high], plane_ref[:, start : start + width], preferred_element_type=jnp.float32)
            + jnp.dot(cross_ref[low:high], other_ref[:, start : start + width], preferred_element_type=jnp.float32)
        ).astype(jnp.bfloat16)


def join_kernel(*refs):
    joined_ref = refs[-1]
    start = 0
    for block in refs[:-1]:
        joined_ref[start : start + block.shape[0]] = block[...]
        start += block.shape[0]


def sum_kernel(kept_ref, *refs):
    n_z = kept_ref.shape[0]
    got, outs = refs[:-n_z], refs[-n_z:]
    for z, out in enumerate(outs):
        total = kept_ref[z]
        for block in got:
            total += block[z].astype(jnp.float32)
        out[...] = total.astype(out.dtype)


def final_kernel(kept_ref, *refs):
    total = kept_ref[...]
    for block in refs[:-1]:
        total += block[...].astype(jnp.float32)
    refs[-1][...] = total.astype(jnp.bfloat16)


def place_kernel(moving, relocate_ref, acts_ref, *refs):
    *arrived, same_ref, other_ref = refs
    rows, lanes = same_ref.shape
    half = lanes // 2
    col_here = lax.axis_index("expert")
    both = None if 2 not in moving else arrived[-1]
    one = None if 1 not in moving else arrived[0]
    for out, low, col in ((same_ref, 0, col_here), (other_ref, rows, col_here ^ 1)):
        if both is None:
            come = one[...]
        elif one is None:
            come = both[low : low + rows]
        else:
            chip = col_here // 2 % len(moving)
            come = jnp.where(chip == moving.index(1), one[...], both[low : low + rows])
        moved = relocate_ref[col] == 1
        out[:, :half] = jnp.where(moved, come[:, half:], acts_ref[low : low + rows, :half])
        out[:, half:] = jnp.where(moved, come[:, :half], acts_ref[low : low + rows, half:])


def small(megabytes, flops=0, moved=0):
    return dict(
        compiler_params=pltpu.CompilerParams(vmem_limit_bytes=megabytes * 2**20),
        cost_estimate=pl.CostEstimate(flops=flops, bytes_accessed=moved, transcendentals=0),
    )


def exchanges(moving, relocate, acts, one, kept, sent_rows):
    n_cols = lax.axis_size("expert")
    half = n_cols // 2
    placed = jax.ShapeDtypeStruct(one.shape, one.dtype)
    block = kept.shape[1:]

    def route(count):
        return [(col, col ^ half) for col in range(n_cols) if moving[col % half // 2] == count]

    arrived = []
    if 1 in moving:
        arrived.append(lax.ppermute(one, "expert", route(1)))
    if 2 in moving:
        arrived.append(lax.ppermute(acts, "expert", route(2)))
    got = [crossed(rows, "dp", d + 1) for d, rows in enumerate(sent_rows)]
    parts = pl.pallas_call(
        sum_kernel,
        out_shape=[jax.ShapeDtypeStruct(block, jnp.float32)] + [jax.ShapeDtypeStruct(block, jnp.bfloat16)] * (half - 1),
        in_specs=whole(1 + len(got)),
        out_specs=whole(half),
        name="sums",
        **small(4),
    )(kept, *got)
    same, others = pl.pallas_call(
        functools.partial(place_kernel, moving),
        out_shape=[placed, placed],
        in_specs=[pl.BlockSpec(memory_space=pltpu.SMEM)] + whole(1 + len(arrived)),
        out_specs=whole(2),
        name="place",
        **small(4),
    )(relocate, acts, *arrived)
    return same, others, parts


def dense_device(tokens, upstream, expert_ids, gates, relocate, w_gate_up, w_down):
    n_rows = lax.axis_size("dp")
    n_cols = lax.axis_size("expert")
    n_z = n_cols // 2
    tok_dev = tokens.shape[0]
    half = n_cols // 2
    units, width = w_down.shape[2:]
    plane_rows = n_rows * n_z * tok_dev
    bf16 = jnp.bfloat16

    own = packed(tokens, upstream, expert_ids, gates, n_cols)

    along_z = [crossed(own, "expert", 2 * dz) for dz in range(1, n_z)]
    along_dp = [crossed(own, "dp", d) for d in range(1, n_rows)]
    pairs = half // 2
    order = along_z[:1] + along_dp[1:] + along_z[1:] + along_dp[:1]
    order = lax.optimization_barrier(order)
    along_z, along_dp = order[:1] + order[n_rows - 1 : -1], order[-1:] + order[1 : n_rows - 1]
    far = pl.pallas_call(
        join_kernel,
        out_shape=jax.ShapeDtypeStruct((tok_dev * (n_z - 1), own.shape[1]), bf16),
        in_specs=whole(n_z - 1),
        out_specs=whole(1)[0],
        name="join",
        **small(4),
    )(*along_z)
    far, wgu_early, wdn_early = lax.optimization_barrier((far, w_gate_up[0, 0], w_down[0, 0]))
    far_dp = [crossed(far, "dp", d) for d in range(1, n_rows)]
    wgu_sib = crossed(wgu_early, "expert", 1)
    wdn_sib = crossed(wdn_early, "expert", 1)
    far_dp[0], wgu_own, wdn_own = lax.optimization_barrier((far_dp[0], w_gate_up[0, 0], w_down[0, 0]))
    weights_own = pl.pallas_call(
        weights_kernel,
        out_shape=jax.ShapeDtypeStruct((3 * units, width), bf16),
        in_specs=[pl.BlockSpec(memory_space=pl.ANY)] * 2,
        out_specs=whole(1)[0],
        scratch_shapes=[pltpu.SemaphoreType.DMA((2,))],
        name="weights",
        **small(4),
    )(wgu_own, wdn_own)

    case, plane, acts, one, kept, *sent = pl.pallas_call(
        functools.partial(forward_kernel, n_cols, n_rows, n_z),
        out_shape=[
            jax.ShapeDtypeStruct((1,), jnp.int32),
            jax.ShapeDtypeStruct((plane_rows, own.shape[1]), bf16),
            jax.ShapeDtypeStruct((6 * units, plane_rows), bf16),
            jax.ShapeDtypeStruct((3 * units, plane_rows), bf16),
            jax.ShapeDtypeStruct((n_z, tok_dev, width), jnp.float32),
        ]
        + [jax.ShapeDtypeStruct((n_z, tok_dev, width), bf16)] * (n_rows - 1),
        in_specs=[pl.BlockSpec(memory_space=pltpu.SMEM)] + whole(2 * n_rows + 3),
        out_specs=[pl.BlockSpec(memory_space=pltpu.SMEM)] + whole(3 + n_rows),
        name="forward",
        **small(16, flops=2 * 6 * units * 2 * width * plane_rows, moved=8 * 2**20),
    )(relocate[:, 0], own, *along_dp, far, *far_dp, weights_own, wgu_sib, wdn_sib)

    plane_sib = crossed(plane, "expert", 1)
    cases = [tuple(number // 3 ** (pairs - 1 - p) % 3 for p in range(pairs)) for number in range(1, 3**pairs - 1)]
    same, others, parts = lax.switch(
        case[0], [functools.partial(exchanges, moving) for moving in cases], relocate[:, 0], acts, one, kept, sent
    )
    cross = crossed(others, "expert", 1)
    got_z = [crossed(parts[dz], "expert", 2 * dz) for dz in range(1, n_z)]
    grad_gu, grad_dn = pl.pallas_call(
        weight_grad_kernel,
        out_shape=[jax.ShapeDtypeStruct((2 * units, width), bf16), jax.ShapeDtypeStruct((units, width), bf16)],
        in_specs=whole(4),
        out_specs=whole(2),
        name="weight_grads",
        **small(16, flops=2 * 3 * units * width * 2 * plane_rows * 8, moved=32 * 2**20),
    )(same, cross, plane, plane_sib)
    kept, grad_dn = lax.optimization_barrier((parts[0], grad_dn))
    grad_tokens = pl.pallas_call(
        final_kernel,
        out_shape=jax.ShapeDtypeStruct((tok_dev, width), bf16),
        in_specs=whole(n_z),
        out_specs=whole(1)[0],
        name="grad_tokens",
        **small(4),
    )(kept, *got_z)
    return grad_tokens, grad_gu.reshape(w_gate_up.shape), grad_dn.reshape(w_down.shape)


def solution(mesh):
    def per_device(*arrays):
        n_rows, n_cols = mesh.shape["dp"], mesh.shape["expert"]
        dense = n_rows == SLICES and arrays[2].shape[1] == n_cols and 4 <= n_cols <= 8
        return (dense_device if dense else routed_device)(*arrays)

    return jax.shard_map(
        per_device,
        mesh=mesh,
        in_specs=(
            P(("dp", "expert"), None),
            P(("dp", "expert"), None),
            P(("dp", "expert"), None),
            P(("dp", "expert"), None),
            P(),
            P("expert", "dp", None, None),
            P("expert", "dp", None, None),
        ),
        out_specs=(
            P(("dp", "expert"), None),
            P("expert", "dp", None, None),
            P("expert", "dp", None, None),
        ),
        check_vma=False,
    )
```

```python
import functools

import jax
import jax.numpy as jnp
from jax import lax
from jax.experimental import pallas as pl
from jax.experimental.pallas import tpu as pltpu
from jax.sharding import PartitionSpec as P

SLICES = 4


contract_last = (((1,), (1,)), ((), ()))
contract_first = (((0,), (0,)), ((), ()))


def swapped(block, axis, apart):
    count = lax.axis_size(axis)
    route = []
    for low in range(count):
        high = low | 1 << apart
        if high != low and high < count:
            route += [(low, high), (high, low)]
    return lax.ppermute(block, axis, route)


def silu_parts(values_in):
    sigmoid_of = jax.nn.sigmoid(values_in)
    return (values_in * sigmoid_of, sigmoid_of * (1.0 + values_in * (1.0 - sigmoid_of)))


def pick_entry(lookup_table, row_index, col_index):
    rows_hit = jnp.arange(lookup_table.shape[0], dtype=jnp.int32)[:, None] == row_index
    cols_hit = jnp.arange(lookup_table.shape[1], dtype=jnp.int32)[None, :] == col_index
    return jnp.sum(jnp.where(rows_hit & cols_hit, lookup_table, 0))


def routed_device(tokens, upstream, expert_ids, gates, relocate, w_gate_up, w_down):
    n_rows = lax.axis_size("dp")
    n_cols = lax.axis_size("expert")
    slot_count = n_rows // SLICES
    experts = slot_count * n_cols
    tok_dev, feature_width = tokens.shape
    top_count = expert_ids.shape[1]
    capacity = min(tok_dev, max(2, (3 * tok_dev * top_count + 2 * experts - 1) // (2 * experts)))
    pair_count = tok_dev * top_count
    buffer_rows = experts * capacity
    slice_width = w_down.shape[2]
    col_block = n_cols // SLICES
    col_here = lax.axis_index("expert")
    row_here = lax.axis_index("dp")
    slot_here = row_here // SLICES
    slice_here = row_here % SLICES
    far_bit = n_cols.bit_length() - 2
    half_cols = n_cols // 2
    flat_ids = expert_ids.reshape(pair_count)
    home_column = flat_ids // slot_count
    slot_of = flat_ids % slot_count
    expert_iota = jnp.arange(experts, dtype=jnp.int32)
    relocated = jnp.sum(
        jnp.where(flat_ids[:, None] == expert_iota[None, :], relocate.reshape(experts)[None, :], 0),
        axis=1,
    )
    column = (home_column + half_cols * relocated) % n_cols
    pair_iota = jnp.arange(pair_count, dtype=jnp.int32)
    earlier = (flat_ids[:, None] == flat_ids[None, :]) & (pair_iota[None, :] < pair_iota[:, None])
    slot_rank = jnp.sum(earlier.astype(jnp.int32), axis=1)
    target = (slot_of * n_cols + column) * capacity + slot_rank
    placing = (target[None, :] == jnp.arange(buffer_rows, dtype=jnp.int32)[:, None]).astype(
        jnp.bfloat16
    )
    x_pairs = jnp.repeat(tokens, top_count, axis=0)
    d_pairs = (
        gates.reshape(pair_count, 1) * jnp.repeat(upstream, top_count, axis=0).astype(jnp.float32)
    ).astype(jnp.bfloat16)
    pair_data = jnp.stack([x_pairs, d_pairs])
    sent = jnp.einsum("bp,kpw->kbw", placing, pair_data, preferred_element_type=jnp.float32).astype(
        jnp.bfloat16
    )
    sent = sent.reshape(2, slot_count, n_cols, capacity, feature_width)
    at_column = lax.all_to_all(sent, "expert", split_axis=2, concat_axis=2, tiled=True)
    swapped_here = pick_entry(relocate, col_here, slot_here)
    own_pack = jnp.concatenate([w_gate_up, w_down], axis=2)
    far_pack = swapped(own_pack, "expert", far_bit)
    own_pack = jnp.where(swapped_here == 1, far_pack, own_pack)
    gate_up = own_pack[0, 0, : 2 * slice_width]
    down_rows = own_pack[0, 0, 2 * slice_width :]
    grouped = at_column.reshape(2, n_rows, col_block, capacity, feature_width)
    at_row = lax.all_to_all(grouped, "dp", split_axis=1, concat_axis=1, tiled=True)
    gathered = at_row[:, None]
    for bit_index in range(SLICES.bit_length() - 1):
        far_rows = swapped(gathered, "dp", bit_index)
        lower_half = slice_here // (1 << bit_index) % 2 == 0
        first_part = jnp.where(lower_half, gathered, far_rows)
        second_part = jnp.where(lower_half, far_rows, gathered)
        gathered = jnp.concatenate([first_part, second_part], axis=1)
    all_rows = gathered.reshape(2, -1, feature_width)
    rows_x = all_rows[0]
    rows_d = all_rows[1]
    gate_and_up = lax.dot_general(
        rows_x, gate_up, contract_last, preferred_element_type=jnp.float32
    )
    gate_pre = gate_and_up[:, :slice_width]
    up_pre = gate_and_up[:, slice_width:]
    activated, slope_of = silu_parts(gate_pre)
    hidden = (activated * up_pre).astype(jnp.bfloat16)
    hidden_grad = lax.dot_general(
        rows_d, down_rows, contract_last, preferred_element_type=jnp.float32
    )
    pre_grads = jnp.concatenate(
        [
            (hidden_grad * up_pre * slope_of).astype(jnp.bfloat16),
            (hidden_grad * activated).astype(jnp.bfloat16),
        ],
        axis=1,
    )
    grad_gu = lax.dot_general(
        pre_grads, rows_x, contract_first, preferred_element_type=jnp.float32
    ).astype(jnp.bfloat16)
    grad_dn = lax.dot_general(
        hidden, rows_d, contract_first, preferred_element_type=jnp.float32
    ).astype(jnp.bfloat16)
    slice_part = jnp.dot(pre_grads, gate_up, preferred_element_type=jnp.float32).astype(
        jnp.bfloat16
    )
    grad_pack = jnp.concatenate([grad_gu, grad_dn], axis=0)
    blocks = slice_part.reshape(2, 2, n_rows, col_block, capacity, feature_width)
    upper_half = slice_here // 2 % 2 == 1
    keep_half = jnp.where(upper_half, blocks[1], blocks[0])
    send_half = jnp.where(upper_half, blocks[0], blocks[1])
    got_half = swapped(send_half, "dp", 1)
    pairsum = keep_half.astype(jnp.float32) + got_half.astype(jnp.float32)
    odd_slice = slice_here % 2 == 1
    keep_last = jnp.where(odd_slice, pairsum[1], pairsum[0])
    send_last = jnp.where(odd_slice, pairsum[0], pairsum[1])
    got_last = swapped(send_last, "dp", 0)
    summed = keep_last + got_last
    back_rows = lax.all_to_all(summed, "dp", split_axis=0, concat_axis=0, tiled=True).reshape(
        slot_count, n_cols, capacity, feature_width
    )
    home_rows = lax.all_to_all(
        back_rows, "expert", split_axis=1, concat_axis=1, tiled=True
    ).reshape(buffer_rows, feature_width)
    hits = (
        target.reshape(tok_dev, top_count)[:, :, None]
        == jnp.arange(buffer_rows, dtype=jnp.int32)[None, None, :]
    )
    gather_mat = jnp.sum(hits.astype(jnp.float32), axis=1)
    grad_tokens = jnp.dot(
        gather_mat, home_rows, precision=lax.Precision.HIGHEST, preferred_element_type=jnp.float32
    ).astype(jnp.bfloat16)
    grad_gate_up = grad_pack[: 2 * slice_width].reshape(w_gate_up.shape)
    grad_down = grad_pack[2 * slice_width :].reshape(w_down.shape)
    return (grad_tokens, grad_gate_up, grad_down)


def crossed(block, axis, apart):
    return lax.ppermute(block, axis, [(i, i ^ apart) for i in range(lax.axis_size(axis))])


def whole(count):
    return [pl.BlockSpec(memory_space=pltpu.VMEM)] * count


def packed(tokens, upstream, expert_ids, gates, n_cols):
    experts = jnp.arange(n_cols, dtype=jnp.int32)[None, None, :]
    by_expert = jnp.sum(jnp.where(expert_ids[:, :, None] == experts, gates[:, :, None], 0.0), axis=1)
    high = lax.reduce_precision(by_expert, 8, 7)
    middle = lax.reduce_precision(by_expert - high, 8, 7)
    low = by_expert - high - middle
    spare = jnp.zeros((tokens.shape[0], 128 - 3 * n_cols), jnp.bfloat16)
    summands = [part.astype(jnp.bfloat16) for part in (high, middle, low)]
    return jnp.concatenate([tokens, upstream] + summands + [spare], axis=1)


def weights_kernel(wgu_hbm, wdn_hbm, weights_ref, sems):
    split = wgu_hbm.shape[0]
    copies = [
        pltpu.make_async_copy(wgu_hbm, weights_ref.at[pl.ds(0, split)], sems.at[0]),
        pltpu.make_async_copy(wdn_hbm, weights_ref.at[pl.ds(split, wdn_hbm.shape[0])], sems.at[1]),
    ]
    for copy in copies:
        copy.start()
    for copy in copies:
        copy.wait()


def forward_kernel(n_cols, n_rows, n_z, relocate_ref, *refs):
    near = refs[:n_rows]
    far = refs[n_rows : 2 * n_rows]
    weights_own, wgu_sib, wdn_sib, case_ref, plane_ref, acts_ref, one_ref, kept_ref, *sent_refs = refs[2 * n_rows :]
    tok_dev = near[0].shape[0]
    pairs = n_cols // 4
    case_ref[0] = sum(relocate_ref[col] * 3 ** (pairs - 1 - col // 2) for col in range(n_cols // 2)) - 1
    for z in range(n_z):
        for d in range(n_rows):
            start = (z * n_rows + d) * tok_dev
            if z == 0:
                block = near[d][...]
            else:
                block = far[d][(z - 1) * tok_dev : z * tok_dev]
            plane_ref[start : start + tok_dev] = block
    units, width = wdn_sib.shape
    split = wgu_sib.shape[0]
    col_here = lax.axis_index("expert")
    lane = lax.broadcasted_iota(jnp.int32, (8, 128), 1)
    row = lax.broadcasted_iota(jnp.int32, (8, 128), 0)
    wanted = jnp.where(row == 0, col_here, col_here ^ 1)
    chosen = (row < 2) & (lane % n_cols == wanted) & (lane < 3 * n_cols)
    gate_rows = lax.dot_general(
        jnp.where(chosen, 1.0, 0.0).astype(jnp.bfloat16),
        plane_ref[:, 2 * width :],
        contract_last,
        preferred_element_type=jnp.float32,
    )
    rows_x = plane_ref[:, :width]
    rows_u = plane_ref[:, width : 2 * width]
    total = None
    for index, (wgu, wdn) in enumerate(((weights_own[:split], weights_own[split:]), (wgu_sib[...], wdn_sib[...]))):
        gate = gate_rows[index : index + 1, :]
        pre = lax.dot_general(wgu, rows_x, contract_last, preferred_element_type=jnp.float32)
        hidden_grad = gate * lax.dot_general(wdn, rows_u, contract_last, preferred_element_type=jnp.float32)
        activated, slope_of = silu_parts(pre[:units])
        up_pre = pre[units:]
        base = index * 3 * units
        acts_ref[base : base + units] = (hidden_grad * up_pre * slope_of).astype(jnp.bfloat16)
        acts_ref[base + units : base + 2 * units] = (hidden_grad * activated).astype(jnp.bfloat16)
        acts_ref[base + 2 * units : base + 3 * units] = (activated * up_pre * gate).astype(jnp.bfloat16)
        part = lax.dot_general(acts_ref[base : base + 2 * units], wgu, contract_first, preferred_element_type=jnp.float32)
        total = part if total is None else total + part
    for z in range(n_z):
        for d in range(n_rows):
            start = (z * n_rows + d) * tok_dev
            block = total[start : start + tok_dev]
            if d == 0:
                kept_ref[z] = block
            else:
                sent_refs[d - 1][z] = block.astype(jnp.bfloat16)
    one_ref[...] = jnp.where(relocate_ref[col_here] == 1, acts_ref[: 3 * units], acts_ref[3 * units :])


def weight_grad_kernel(same_ref, cross_ref, plane_ref, other_ref, gu_ref, dn_ref):
    units, width = dn_ref.shape
    for out, low, start in ((gu_ref, 0, 0), (dn_ref, 2 * units, width)):
        high = low + out.shape[0]
        out[...] = (
            jnp.dot(same_ref[low:high], plane_ref[:, start : start + width], preferred_element_type=jnp.float32)
            + jnp.dot(cross_ref[low:high], other_ref[:, start : start + width], preferred_element_type=jnp.float32)
        ).astype(jnp.bfloat16)


def join_kernel(*refs):
    joined_ref = refs[-1]
    start = 0
    for block in refs[:-1]:
        joined_ref[start : start + block.shape[0]] = block[...]
        start += block.shape[0]


def sum_kernel(kept_ref, *refs):
    n_z = kept_ref.shape[0]
    got, outs = refs[:-n_z], refs[-n_z:]
    for z, out in enumerate(outs):
        total = kept_ref[z]
        for block in got:
            total += block[z].astype(jnp.float32)
        out[...] = total.astype(out.dtype)


def final_kernel(kept_ref, *refs):
    total = kept_ref[...]
    for block in refs[:-1]:
        total += block[...].astype(jnp.float32)
    refs[-1][...] = total.astype(jnp.bfloat16)


def place_kernel(moving, relocate_ref, acts_ref, *refs):
    *arrived, same_ref, other_ref = refs
    rows, lanes = same_ref.shape
    half = lanes // 2
    col_here = lax.axis_index("expert")
    both = None if 2 not in moving else arrived[-1]
    one = None if 1 not in moving else arrived[0]
    for out, low, col in ((same_ref, 0, col_here), (other_ref, rows, col_here ^ 1)):
        if both is None:
            come = one[...]
        elif one is None:
            come = both[low : low + rows]
        else:
            chip = col_here // 2 % len(moving)
            come = jnp.where(chip == moving.index(1), one[...], both[low : low + rows])
        moved = relocate_ref[col] == 1
        out[:, :half] = jnp.where(moved, come[:, half:], acts_ref[low : low + rows, :half])
        out[:, half:] = jnp.where(moved, come[:, :half], acts_ref[low : low + rows, half:])


def small(megabytes, flops=0, moved=0):
    return dict(
        compiler_params=pltpu.CompilerParams(vmem_limit_bytes=megabytes * 2**20),
        cost_estimate=pl.CostEstimate(flops=flops, bytes_accessed=moved, transcendentals=0),
    )


def exchanges(moving, relocate, acts, one, kept, sent_rows):
    n_cols = lax.axis_size("expert")
    half = n_cols // 2
    placed = jax.ShapeDtypeStruct(one.shape, one.dtype)
    block = kept.shape[1:]

    def route(count):
        return [(col, col ^ half) for col in range(n_cols) if moving[col % half // 2] == count]

    arrived = []
    if 1 in moving:
        arrived.append(lax.ppermute(one, "expert", route(1)))
    if 2 in moving:
        arrived.append(lax.ppermute(acts, "expert", route(2)))
    got = [crossed(rows, "dp", d + 1) for d, rows in enumerate(sent_rows)]
    parts = pl.pallas_call(
        sum_kernel,
        out_shape=[jax.ShapeDtypeStruct(block, jnp.float32)] + [jax.ShapeDtypeStruct(block, jnp.bfloat16)] * (half - 1),
        in_specs=whole(1 + len(got)),
        out_specs=whole(half),
        name="sums",
        **small(4),
    )(kept, *got)
    same, others = pl.pallas_call(
        functools.partial(place_kernel, moving),
        out_shape=[placed, placed],
        in_specs=[pl.BlockSpec(memory_space=pltpu.SMEM)] + whole(1 + len(arrived)),
        out_specs=whole(2),
        name="place",
        **small(4),
    )(relocate, acts, *arrived)
    return same, others, parts


def dense_device(tokens, upstream, expert_ids, gates, relocate, w_gate_up, w_down):
    n_rows = lax.axis_size("dp")
    n_cols = lax.axis_size("expert")
    n_z = n_cols // 2
    tok_dev = tokens.shape[0]
    half = n_cols // 2
    units, width = w_down.shape[2:]
    plane_rows = n_rows * n_z * tok_dev
    bf16 = jnp.bfloat16

    own = packed(tokens, upstream, expert_ids, gates, n_cols)

    along_z = [crossed(own, "expert", 2 * dz) for dz in range(1, n_z)]
    along_dp = [crossed(own, "dp", d) for d in range(1, n_rows)]
    pairs = half // 2
    order = lax.optimization_barrier([along_dp[1], along_dp[0], along_dp[2], along_z[1], along_z[2], along_z[0]])
    along_z, along_dp = [order[5], order[3], order[4]], [order[1], order[0], order[2]]
    far = pl.pallas_call(
        join_kernel,
        out_shape=jax.ShapeDtypeStruct((tok_dev * (n_z - 1), own.shape[1]), bf16),
        in_specs=whole(n_z - 1),
        out_specs=whole(1)[0],
        name="join",
        **small(4),
    )(*along_z)
    far, wgu_early, wdn_early = lax.optimization_barrier((far, w_gate_up[0, 0], w_down[0, 0]))
    far_dp = [crossed(far, "dp", d) for d in range(1, n_rows)]
    wgu_sib = crossed(wgu_early, "expert", 1)
    wdn_sib = crossed(wdn_early, "expert", 1)
    far_dp[0], wgu_own, wdn_own = lax.optimization_barrier((far_dp[0], w_gate_up[0, 0], w_down[0, 0]))
    weights_own = pl.pallas_call(
        weights_kernel,
        out_shape=jax.ShapeDtypeStruct((3 * units, width), bf16),
        in_specs=[pl.BlockSpec(memory_space=pl.ANY)] * 2,
        out_specs=whole(1)[0],
        scratch_shapes=[pltpu.SemaphoreType.DMA((2,))],
        name="weights",
        **small(4),
    )(wgu_own, wdn_own)

    case, plane, acts, one, kept, *sent = pl.pallas_call(
        functools.partial(forward_kernel, n_cols, n_rows, n_z),
        out_shape=[
            jax.ShapeDtypeStruct((1,), jnp.int32),
            jax.ShapeDtypeStruct((plane_rows, own.shape[1]), bf16),
            jax.ShapeDtypeStruct((6 * units, plane_rows), bf16),
            jax.ShapeDtypeStruct((3 * units, plane_rows), bf16),
            jax.ShapeDtypeStruct((n_z, tok_dev, width), jnp.float32),
        ]
        + [jax.ShapeDtypeStruct((n_z, tok_dev, width), bf16)] * (n_rows - 1),
        in_specs=[pl.BlockSpec(memory_space=pltpu.SMEM)] + whole(2 * n_rows + 3),
        out_specs=[pl.BlockSpec(memory_space=pltpu.SMEM)] + whole(3 + n_rows),
        name="forward",
        **small(16, flops=2 * 6 * units * 2 * width * plane_rows, moved=8 * 2**20),
    )(relocate[:, 0], own, *along_dp, far, *far_dp, weights_own, wgu_sib, wdn_sib)

    plane_sib = crossed(plane, "expert", 1)
    cases = [tuple(number // 3 ** (pairs - 1 - p) % 3 for p in range(pairs)) for number in range(1, 3**pairs - 1)]
    same, others, parts = lax.switch(
        case[0], [functools.partial(exchanges, moving) for moving in cases], relocate[:, 0], acts, one, kept, sent
    )
    cross = crossed(others, "expert", 1)
    got_z = [crossed(parts[dz], "expert", 2 * dz) for dz in range(1, n_z)]
    grad_gu, grad_dn = pl.pallas_call(
        weight_grad_kernel,
        out_shape=[jax.ShapeDtypeStruct((2 * units, width), bf16), jax.ShapeDtypeStruct((units, width), bf16)],
        in_specs=whole(4),
        out_specs=whole(2),
        name="weight_grads",
        **small(16, flops=2 * 3 * units * width * 2 * plane_rows * 8, moved=32 * 2**20),
    )(same, cross, plane, plane_sib)
    kept, grad_dn = lax.optimization_barrier((parts[0], grad_dn))
    grad_tokens = pl.pallas_call(
        final_kernel,
        out_shape=jax.ShapeDtypeStruct((tok_dev, width), bf16),
        in_specs=whole(n_z),
        out_specs=whole(1)[0],
        name="grad_tokens",
        **small(4),
    )(kept, *got_z[::-1])
    return grad_tokens, grad_gu.reshape(w_gate_up.shape), grad_dn.reshape(w_down.shape)


def solution(mesh):
    def per_device(*arrays):
        n_rows, n_cols = mesh.shape["dp"], mesh.shape["expert"]
        dense = n_rows == SLICES and arrays[2].shape[1] == n_cols and 4 <= n_cols <= 8
        return (dense_device if dense else routed_device)(*arrays)

    return jax.shard_map(
        per_device,
        mesh=mesh,
        in_specs=(
            P(("dp", "expert"), None),
            P(("dp", "expert"), None),
            P(("dp", "expert"), None),
            P(("dp", "expert"), None),
            P(),
            P("expert", "dp", None, None),
            P("expert", "dp", None, None),
        ),
        out_specs=(
            P(("dp", "expert"), None),
            P("expert", "dp", None, None),
            P("expert", "dp", None, None),
        ),
        check_vma=False,
    )
```

```python
import functools

import jax
import jax.numpy as jnp
from jax import lax
from jax.experimental import pallas as pl
from jax.experimental.pallas import tpu as pltpu
from jax.sharding import PartitionSpec as P

SLICES = 4


contract_last = (((1,), (1,)), ((), ()))
contract_first = (((0,), (0,)), ((), ()))


def swapped(block, axis, apart):
    count = lax.axis_size(axis)
    route = []
    for low in range(count):
        high = low | 1 << apart
        if high != low and high < count:
            route += [(low, high), (high, low)]
    return lax.ppermute(block, axis, route)


def silu_parts(values_in):
    sigmoid_of = jax.nn.sigmoid(values_in)
    return (values_in * sigmoid_of, sigmoid_of * (1.0 + values_in * (1.0 - sigmoid_of)))


def pick_entry(lookup_table, row_index, col_index):
    rows_hit = jnp.arange(lookup_table.shape[0], dtype=jnp.int32)[:, None] == row_index
    cols_hit = jnp.arange(lookup_table.shape[1], dtype=jnp.int32)[None, :] == col_index
    return jnp.sum(jnp.where(rows_hit & cols_hit, lookup_table, 0))


def routed_device(tokens, upstream, expert_ids, gates, relocate, w_gate_up, w_down):
    n_rows = lax.axis_size("dp")
    n_cols = lax.axis_size("expert")
    slot_count = n_rows // SLICES
    experts = slot_count * n_cols
    tok_dev, feature_width = tokens.shape
    top_count = expert_ids.shape[1]
    capacity = min(tok_dev, max(2, (3 * tok_dev * top_count + 2 * experts - 1) // (2 * experts)))
    pair_count = tok_dev * top_count
    buffer_rows = experts * capacity
    slice_width = w_down.shape[2]
    col_block = n_cols // SLICES
    col_here = lax.axis_index("expert")
    row_here = lax.axis_index("dp")
    slot_here = row_here // SLICES
    slice_here = row_here % SLICES
    far_bit = n_cols.bit_length() - 2
    half_cols = n_cols // 2
    flat_ids = expert_ids.reshape(pair_count)
    home_column = flat_ids // slot_count
    slot_of = flat_ids % slot_count
    expert_iota = jnp.arange(experts, dtype=jnp.int32)
    relocated = jnp.sum(
        jnp.where(flat_ids[:, None] == expert_iota[None, :], relocate.reshape(experts)[None, :], 0),
        axis=1,
    )
    column = (home_column + half_cols * relocated) % n_cols
    pair_iota = jnp.arange(pair_count, dtype=jnp.int32)
    earlier = (flat_ids[:, None] == flat_ids[None, :]) & (pair_iota[None, :] < pair_iota[:, None])
    slot_rank = jnp.sum(earlier.astype(jnp.int32), axis=1)
    target = (slot_of * n_cols + column) * capacity + slot_rank
    placing = (target[None, :] == jnp.arange(buffer_rows, dtype=jnp.int32)[:, None]).astype(
        jnp.bfloat16
    )
    x_pairs = jnp.repeat(tokens, top_count, axis=0)
    d_pairs = (
        gates.reshape(pair_count, 1) * jnp.repeat(upstream, top_count, axis=0).astype(jnp.float32)
    ).astype(jnp.bfloat16)
    pair_data = jnp.stack([x_pairs, d_pairs])
    sent = jnp.einsum("bp,kpw->kbw", placing, pair_data, preferred_element_type=jnp.float32).astype(
        jnp.bfloat16
    )
    sent = sent.reshape(2, slot_count, n_cols, capacity, feature_width)
    at_column = lax.all_to_all(sent, "expert", split_axis=2, concat_axis=2, tiled=True)
    swapped_here = pick_entry(relocate, col_here, slot_here)
    own_pack = jnp.concatenate([w_gate_up, w_down], axis=2)
    far_pack = swapped(own_pack, "expert", far_bit)
    own_pack = jnp.where(swapped_here == 1, far_pack, own_pack)
    gate_up = own_pack[0, 0, : 2 * slice_width]
    down_rows = own_pack[0, 0, 2 * slice_width :]
    grouped = at_column.reshape(2, n_rows, col_block, capacity, feature_width)
    at_row = lax.all_to_all(grouped, "dp", split_axis=1, concat_axis=1, tiled=True)
    gathered = at_row[:, None]
    for bit_index in range(SLICES.bit_length() - 1):
        far_rows = swapped(gathered, "dp", bit_index)
        lower_half = slice_here // (1 << bit_index) % 2 == 0
        first_part = jnp.where(lower_half, gathered, far_rows)
        second_part = jnp.where(lower_half, far_rows, gathered)
        gathered = jnp.concatenate([first_part, second_part], axis=1)
    all_rows = gathered.reshape(2, -1, feature_width)
    rows_x = all_rows[0]
    rows_d = all_rows[1]
    gate_and_up = lax.dot_general(
        rows_x, gate_up, contract_last, preferred_element_type=jnp.float32
    )
    gate_pre = gate_and_up[:, :slice_width]
    up_pre = gate_and_up[:, slice_width:]
    activated, slope_of = silu_parts(gate_pre)
    hidden = (activated * up_pre).astype(jnp.bfloat16)
    hidden_grad = lax.dot_general(
        rows_d, down_rows, contract_last, preferred_element_type=jnp.float32
    )
    pre_grads = jnp.concatenate(
        [
            (hidden_grad * up_pre * slope_of).astype(jnp.bfloat16),
            (hidden_grad * activated).astype(jnp.bfloat16),
        ],
        axis=1,
    )
    grad_gu = lax.dot_general(
        pre_grads, rows_x, contract_first, preferred_element_type=jnp.float32
    ).astype(jnp.bfloat16)
    grad_dn = lax.dot_general(
        hidden, rows_d, contract_first, preferred_element_type=jnp.float32
    ).astype(jnp.bfloat16)
    slice_part = jnp.dot(pre_grads, gate_up, preferred_element_type=jnp.float32).astype(
        jnp.bfloat16
    )
    grad_pack = jnp.concatenate([grad_gu, grad_dn], axis=0)
    blocks = slice_part.reshape(2, 2, n_rows, col_block, capacity, feature_width)
    upper_half = slice_here // 2 % 2 == 1
    keep_half = jnp.where(upper_half, blocks[1], blocks[0])
    send_half = jnp.where(upper_half, blocks[0], blocks[1])
    got_half = swapped(send_half, "dp", 1)
    pairsum = keep_half.astype(jnp.float32) + got_half.astype(jnp.float32)
    odd_slice = slice_here % 2 == 1
    keep_last = jnp.where(odd_slice, pairsum[1], pairsum[0])
    send_last = jnp.where(odd_slice, pairsum[0], pairsum[1])
    got_last = swapped(send_last, "dp", 0)
    summed = keep_last + got_last
    back_rows = lax.all_to_all(summed, "dp", split_axis=0, concat_axis=0, tiled=True).reshape(
        slot_count, n_cols, capacity, feature_width
    )
    home_rows = lax.all_to_all(
        back_rows, "expert", split_axis=1, concat_axis=1, tiled=True
    ).reshape(buffer_rows, feature_width)
    hits = (
        target.reshape(tok_dev, top_count)[:, :, None]
        == jnp.arange(buffer_rows, dtype=jnp.int32)[None, None, :]
    )
    gather_mat = jnp.sum(hits.astype(jnp.float32), axis=1)
    grad_tokens = jnp.dot(
        gather_mat, home_rows, precision=lax.Precision.HIGHEST, preferred_element_type=jnp.float32
    ).astype(jnp.bfloat16)
    grad_gate_up = grad_pack[: 2 * slice_width].reshape(w_gate_up.shape)
    grad_down = grad_pack[2 * slice_width :].reshape(w_down.shape)
    return (grad_tokens, grad_gate_up, grad_down)


def crossed(block, axis, apart):
    return lax.ppermute(block, axis, [(i, i ^ apart) for i in range(lax.axis_size(axis))])


def whole(count):
    return [pl.BlockSpec(memory_space=pltpu.VMEM)] * count


def packed(tokens, upstream, expert_ids, gates, n_cols):
    experts = jnp.arange(n_cols, dtype=jnp.int32)[None, None, :]
    by_expert = jnp.sum(jnp.where(expert_ids[:, :, None] == experts, gates[:, :, None], 0.0), axis=1)
    high = lax.reduce_precision(by_expert, 8, 7)
    middle = lax.reduce_precision(by_expert - high, 8, 7)
    low = by_expert - high - middle
    spare = jnp.zeros((tokens.shape[0], 128 - 3 * n_cols), jnp.bfloat16)
    summands = [part.astype(jnp.bfloat16) for part in (high, middle, low)]
    return jnp.concatenate([tokens, upstream] + summands + [spare], axis=1)


def weights_kernel(wgu_hbm, wdn_hbm, weights_ref, sems):
    split = wgu_hbm.shape[0]
    copies = [
        pltpu.make_async_copy(wgu_hbm, weights_ref.at[pl.ds(0, split)], sems.at[0]),
        pltpu.make_async_copy(wdn_hbm, weights_ref.at[pl.ds(split, wdn_hbm.shape[0])], sems.at[1]),
    ]
    for copy in copies:
        copy.start()
    for copy in copies:
        copy.wait()


def forward_kernel(n_cols, n_rows, n_z, relocate_ref, *refs):
    near = refs[:n_rows]
    far = refs[n_rows : 2 * n_rows - 1]
    diagonal = refs[2 * n_rows - 1 : 2 * n_rows + n_z - 2]
    weights_own, wgu_sib, wdn_sib, plane_ref, acts_ref, one_ref, kept_ref, *sent_refs = refs[2 * n_rows + n_z - 2 :]
    tok_dev = near[0].shape[0]
    for z in range(n_z):
        for d in range(n_rows):
            start = (z * n_rows + d) * tok_dev
            if z == 0:
                block = near[d][...]
            elif d < n_rows - 1:
                block = far[d][(z - 1) * tok_dev : z * tok_dev]
            else:
                block = diagonal[z - 1][...]
            plane_ref[start : start + tok_dev] = block
    units, width = wdn_sib.shape
    split = wgu_sib.shape[0]
    col_here = lax.axis_index("expert")
    lane = lax.broadcasted_iota(jnp.int32, (8, 128), 1)
    row = lax.broadcasted_iota(jnp.int32, (8, 128), 0)
    wanted = jnp.where(row == 0, col_here, col_here ^ 1)
    chosen = (row < 2) & (lane % n_cols == wanted) & (lane < 3 * n_cols)
    gate_rows = lax.dot_general(
        jnp.where(chosen, 1.0, 0.0).astype(jnp.bfloat16),
        plane_ref[:, 2 * width :],
        contract_last,
        preferred_element_type=jnp.float32,
    )
    rows_x = plane_ref[:, :width]
    rows_u = plane_ref[:, width : 2 * width]
    total = None
    for index, (wgu, wdn) in enumerate(((weights_own[:split], weights_own[split:]), (wgu_sib[...], wdn_sib[...]))):
        gate = gate_rows[index : index + 1, :]
        pre = lax.dot_general(wgu, rows_x, contract_last, preferred_element_type=jnp.float32)
        hidden_grad = gate * lax.dot_general(wdn, rows_u, contract_last, preferred_element_type=jnp.float32)
        activated, slope_of = silu_parts(pre[:units])
        up_pre = pre[units:]
        base = index * 3 * units
        acts_ref[base : base + units] = (hidden_grad * up_pre * slope_of).astype(jnp.bfloat16)
        acts_ref[base + units : base + 2 * units] = (hidden_grad * activated).astype(jnp.bfloat16)
        acts_ref[base + 2 * units : base + 3 * units] = (activated * up_pre * gate).astype(jnp.bfloat16)
        part = lax.dot_general(acts_ref[base : base + 2 * units], wgu, contract_first, preferred_element_type=jnp.float32)
        total = part if total is None else total + part
    for z in range(n_z):
        for d in range(n_rows):
            start = (z * n_rows + d) * tok_dev
            block = total[start : start + tok_dev]
            if d == 0:
                kept_ref[z] = block
            else:
                sent_refs[d - 1][z] = block.astype(jnp.bfloat16)
    one_ref[...] = jnp.where(relocate_ref[col_here] == 1, acts_ref[: 3 * units], acts_ref[3 * units :])


def weight_grad_kernel(same_ref, cross_ref, plane_ref, other_ref, gu_ref, dn_ref):
    units, width = dn_ref.shape
    for out, low, start in ((gu_ref, 0, 0), (dn_ref, 2 * units, width)):
        high = low + out.shape[0]
        out[...] = (
            jnp.dot(same_ref[low:high], plane_ref[:, start : start + width], preferred_element_type=jnp.float32)
            + jnp.dot(cross_ref[low:high], other_ref[:, start : start + width], preferred_element_type=jnp.float32)
        ).astype(jnp.bfloat16)


def join_kernel(*refs):
    joined_ref = refs[-1]
    start = 0
    for block in refs[:-1]:
        joined_ref[start : start + block.shape[0]] = block[...]
        start += block.shape[0]


def case_kernel(n_cols, relocate_ref, case_ref):
    pairs = n_cols // 4
    case_ref[0] = sum(relocate_ref[col] * 3 ** (pairs - 1 - col // 2) for col in range(n_cols // 2)) - 1


def sum_kernel(kept_ref, *refs):
    n_z = kept_ref.shape[0]
    got, outs = refs[:-n_z], refs[-n_z:]
    for z, out in enumerate(outs):
        total = kept_ref[z]
        for block in got:
            total += block[z].astype(jnp.float32)
        out[...] = total.astype(out.dtype)


def final_kernel(kept_ref, *refs):
    total = kept_ref[...]
    for block in refs[:-1]:
        total += block[...].astype(jnp.float32)
    refs[-1][...] = total.astype(jnp.bfloat16)


def place_kernel(moving, relocate_ref, acts_ref, *refs):
    *arrived, same_ref, other_ref = refs
    rows, lanes = same_ref.shape
    half = lanes // 2
    col_here = lax.axis_index("expert")
    both = None if 2 not in moving else arrived[-1]
    one = None if 1 not in moving else arrived[0]
    for out, low, col in ((same_ref, 0, col_here), (other_ref, rows, col_here ^ 1)):
        if both is None:
            come = one[...]
        elif one is None:
            come = both[low : low + rows]
        else:
            chip = col_here // 2 % len(moving)
            come = jnp.where(chip == moving.index(1), one[...], both[low : low + rows])
        moved = relocate_ref[col] == 1
        out[:, :half] = jnp.where(moved, come[:, half:], acts_ref[low : low + rows, :half])
        out[:, half:] = jnp.where(moved, come[:, :half], acts_ref[low : low + rows, half:])


def small(megabytes, flops=0, moved=0):
    return dict(
        compiler_params=pltpu.CompilerParams(vmem_limit_bytes=megabytes * 2**20),
        cost_estimate=pl.CostEstimate(flops=flops, bytes_accessed=moved, transcendentals=0),
    )


def exchanges(moving, relocate, acts, one, kept, sent_rows):
    n_cols = lax.axis_size("expert")
    half = n_cols // 2
    placed = jax.ShapeDtypeStruct(one.shape, one.dtype)
    block = kept.shape[1:]

    def route(count):
        return [(col, col ^ half) for col in range(n_cols) if moving[col % half // 2] == count]

    arrived = []
    if 1 in moving:
        arrived.append(lax.ppermute(one, "expert", route(1)))
    if 2 in moving:
        arrived.append(lax.ppermute(acts, "expert", route(2)))
    got = [crossed(rows, "dp", d + 1) for d, rows in enumerate(sent_rows)]
    parts = pl.pallas_call(
        sum_kernel,
        out_shape=[jax.ShapeDtypeStruct(block, jnp.float32)] + [jax.ShapeDtypeStruct(block, jnp.bfloat16)] * (half - 1),
        in_specs=whole(1 + len(got)),
        out_specs=whole(half),
        name="sums",
        **small(4),
    )(kept, *got)
    same, others = pl.pallas_call(
        functools.partial(place_kernel, moving),
        out_shape=[placed, placed],
        in_specs=[pl.BlockSpec(memory_space=pltpu.SMEM)] + whole(1 + len(arrived)),
        out_specs=whole(2),
        name="place",
        **small(4),
    )(relocate, acts, *arrived)
    return same, others, parts


def dense_device(tokens, upstream, expert_ids, gates, relocate, w_gate_up, w_down):
    n_rows = lax.axis_size("dp")
    n_cols = lax.axis_size("expert")
    n_z = n_cols // 2
    tok_dev = tokens.shape[0]
    half = n_cols // 2
    units, width = w_down.shape[2:]
    plane_rows = n_rows * n_z * tok_dev
    bf16 = jnp.bfloat16

    wgu_sib = crossed(w_gate_up[0, 0], "expert", 1)
    wdn_sib = crossed(w_down[0, 0], "expert", 1)
    own = packed(tokens, upstream, expert_ids, gates, n_cols)
    case = pl.pallas_call(
        functools.partial(case_kernel, n_cols),
        out_shape=jax.ShapeDtypeStruct((1,), jnp.int32),
        in_specs=[pl.BlockSpec(memory_space=pltpu.SMEM)],
        out_specs=pl.BlockSpec(memory_space=pltpu.SMEM),
        name="case",
        **small(4),
    )(relocate[:, 0])
    own, wgu_sib, wdn_sib, case = lax.optimization_barrier((own, wgu_sib, wdn_sib, case))

    along_z = [crossed(own, "expert", 2 * dz) for dz in range(1, n_z)]
    along_dp = [crossed(own, "dp", d) for d in range(1, n_rows)]
    pairs = half // 2
    order = lax.optimization_barrier([along_dp[1], along_dp[0], along_dp[2], along_z[1], along_z[2], along_z[0]])
    along_z, along_dp = [order[5], order[3], order[4]], [order[1], order[0], order[2]]
    far = pl.pallas_call(
        join_kernel,
        out_shape=jax.ShapeDtypeStruct((tok_dev * (n_z - 1), own.shape[1]), bf16),
        in_specs=whole(n_z - 1),
        out_specs=whole(1)[0],
        name="join",
        **small(4),
    )(*along_z)
    far_dp = [crossed(far, "dp", d) for d in range(1, n_rows - 1)]
    diagonal = [crossed(along_dp[-1], "expert", 2 * dz) for dz in range(1, n_z)]
    far_dp[0], wgu_own, wdn_own = lax.optimization_barrier((far_dp[0], w_gate_up[0, 0], w_down[0, 0]))
    weights_own = pl.pallas_call(
        weights_kernel,
        out_shape=jax.ShapeDtypeStruct((3 * units, width), bf16),
        in_specs=[pl.BlockSpec(memory_space=pl.ANY)] * 2,
        out_specs=whole(1)[0],
        scratch_shapes=[pltpu.SemaphoreType.DMA((2,))],
        name="weights",
        **small(4),
    )(wgu_own, wdn_own)

    plane, acts, one, kept, *sent = pl.pallas_call(
        functools.partial(forward_kernel, n_cols, n_rows, n_z),
        out_shape=[
            jax.ShapeDtypeStruct((plane_rows, own.shape[1]), bf16),
            jax.ShapeDtypeStruct((6 * units, plane_rows), bf16),
            jax.ShapeDtypeStruct((3 * units, plane_rows), bf16),
            jax.ShapeDtypeStruct((n_z, tok_dev, width), jnp.float32),
        ]
        + [jax.ShapeDtypeStruct((n_z, tok_dev, width), bf16)] * (n_rows - 1),
        in_specs=[pl.BlockSpec(memory_space=pltpu.SMEM)] + whole(2 * n_rows + n_z + 1),
        out_specs=whole(3 + n_rows),
        name="forward",
        **small(16, flops=2 * 6 * units * 2 * width * plane_rows, moved=8 * 2**20),
    )(relocate[:, 0], own, *along_dp, far, *far_dp, *diagonal, weights_own, wgu_sib, wdn_sib)

    plane_sib = crossed(plane, "expert", 1)
    cases = [tuple(number // 3 ** (pairs - 1 - p) % 3 for p in range(pairs)) for number in range(1, 3**pairs - 1)]
    same, others, parts = lax.switch(
        case[0], [functools.partial(exchanges, moving) for moving in cases], relocate[:, 0], acts, one, kept, sent
    )
    cross = crossed(others, "expert", 1)
    got_z = [crossed(parts[dz], "expert", 2 * dz) for dz in range(1, n_z)]
    grad_gu, grad_dn = pl.pallas_call(
        weight_grad_kernel,
        out_shape=[jax.ShapeDtypeStruct((2 * units, width), bf16), jax.ShapeDtypeStruct((units, width), bf16)],
        in_specs=whole(4),
        out_specs=whole(2),
        name="weight_grads",
        **small(16, flops=2 * 3 * units * width * 2 * plane_rows * 8, moved=32 * 2**20),
    )(same, cross, plane, plane_sib)
    kept, grad_dn = lax.optimization_barrier((parts[0], grad_dn))
    grad_tokens = pl.pallas_call(
        final_kernel,
        out_shape=jax.ShapeDtypeStruct((tok_dev, width), bf16),
        in_specs=whole(n_z),
        out_specs=whole(1)[0],
        name="grad_tokens",
        **small(4),
    )(kept, *got_z[::-1])
    return grad_tokens, grad_gu.reshape(w_gate_up.shape), grad_dn.reshape(w_down.shape)


def solution(mesh):
    def per_device(*arrays):
        n_rows, n_cols = mesh.shape["dp"], mesh.shape["expert"]
        dense = n_rows == SLICES and arrays[2].shape[1] == n_cols and 4 <= n_cols <= 8
        return (dense_device if dense else routed_device)(*arrays)

    return jax.shard_map(
        per_device,
        mesh=mesh,
        in_specs=(
            P(("dp", "expert"), None),
            P(("dp", "expert"), None),
            P(("dp", "expert"), None),
            P(("dp", "expert"), None),
            P(),
            P("expert", "dp", None, None),
            P("expert", "dp", None, None),
        ),
        out_specs=(
            P(("dp", "expert"), None),
            P("expert", "dp", None, None),
            P("expert", "dp", None, None),
        ),
        check_vma=False,
    )
```

```python
import functools

import jax
import jax.numpy as jnp
from jax import lax
from jax.experimental import pallas as pl
from jax.experimental.pallas import tpu as pltpu
from jax.sharding import PartitionSpec as P

SLICES = 4


contract_last = (((1,), (1,)), ((), ()))
contract_first = (((0,), (0,)), ((), ()))


def swapped(block, axis, apart):
    count = lax.axis_size(axis)
    route = []
    for low in range(count):
        high = low | 1 << apart
        if high != low and high < count:
            route += [(low, high), (high, low)]
    return lax.ppermute(block, axis, route)


def silu_parts(values_in):
    sigmoid_of = jax.nn.sigmoid(values_in)
    return (values_in * sigmoid_of, sigmoid_of * (1.0 + values_in * (1.0 - sigmoid_of)))


def pick_entry(lookup_table, row_index, col_index):
    rows_hit = jnp.arange(lookup_table.shape[0], dtype=jnp.int32)[:, None] == row_index
    cols_hit = jnp.arange(lookup_table.shape[1], dtype=jnp.int32)[None, :] == col_index
    return jnp.sum(jnp.where(rows_hit & cols_hit, lookup_table, 0))


def routed_device(tokens, upstream, expert_ids, gates, relocate, w_gate_up, w_down):
    n_rows = lax.axis_size("dp")
    n_cols = lax.axis_size("expert")
    slot_count = n_rows // SLICES
    experts = slot_count * n_cols
    tok_dev, feature_width = tokens.shape
    top_count = expert_ids.shape[1]
    capacity = min(tok_dev, max(2, (3 * tok_dev * top_count + 2 * experts - 1) // (2 * experts)))
    pair_count = tok_dev * top_count
    buffer_rows = experts * capacity
    slice_width = w_down.shape[2]
    col_block = n_cols // SLICES
    col_here = lax.axis_index("expert")
    row_here = lax.axis_index("dp")
    slot_here = row_here // SLICES
    slice_here = row_here % SLICES
    far_bit = n_cols.bit_length() - 2
    half_cols = n_cols // 2
    flat_ids = expert_ids.reshape(pair_count)
    home_column = flat_ids // slot_count
    slot_of = flat_ids % slot_count
    expert_iota = jnp.arange(experts, dtype=jnp.int32)
    relocated = jnp.sum(
        jnp.where(flat_ids[:, None] == expert_iota[None, :], relocate.reshape(experts)[None, :], 0),
        axis=1,
    )
    column = (home_column + half_cols * relocated) % n_cols
    pair_iota = jnp.arange(pair_count, dtype=jnp.int32)
    earlier = (flat_ids[:, None] == flat_ids[None, :]) & (pair_iota[None, :] < pair_iota[:, None])
    slot_rank = jnp.sum(earlier.astype(jnp.int32), axis=1)
    target = (slot_of * n_cols + column) * capacity + slot_rank
    placing = (target[None, :] == jnp.arange(buffer_rows, dtype=jnp.int32)[:, None]).astype(
        jnp.bfloat16
    )
    x_pairs = jnp.repeat(tokens, top_count, axis=0)
    d_pairs = (
        gates.reshape(pair_count, 1) * jnp.repeat(upstream, top_count, axis=0).astype(jnp.float32)
    ).astype(jnp.bfloat16)
    pair_data = jnp.stack([x_pairs, d_pairs])
    sent = jnp.einsum("bp,kpw->kbw", placing, pair_data, preferred_element_type=jnp.float32).astype(
        jnp.bfloat16
    )
    sent = sent.reshape(2, slot_count, n_cols, capacity, feature_width)
    at_column = lax.all_to_all(sent, "expert", split_axis=2, concat_axis=2, tiled=True)
    swapped_here = pick_entry(relocate, col_here, slot_here)
    own_pack = jnp.concatenate([w_gate_up, w_down], axis=2)
    far_pack = swapped(own_pack, "expert", far_bit)
    own_pack = jnp.where(swapped_here == 1, far_pack, own_pack)
    gate_up = own_pack[0, 0, : 2 * slice_width]
    down_rows = own_pack[0, 0, 2 * slice_width :]
    grouped = at_column.reshape(2, n_rows, col_block, capacity, feature_width)
    at_row = lax.all_to_all(grouped, "dp", split_axis=1, concat_axis=1, tiled=True)
    gathered = at_row[:, None]
    for bit_index in range(SLICES.bit_length() - 1):
        far_rows = swapped(gathered, "dp", bit_index)
        lower_half = slice_here // (1 << bit_index) % 2 == 0
        first_part = jnp.where(lower_half, gathered, far_rows)
        second_part = jnp.where(lower_half, far_rows, gathered)
        gathered = jnp.concatenate([first_part, second_part], axis=1)
    all_rows = gathered.reshape(2, -1, feature_width)
    rows_x = all_rows[0]
    rows_d = all_rows[1]
    gate_and_up = lax.dot_general(
        rows_x, gate_up, contract_last, preferred_element_type=jnp.float32
    )
    gate_pre = gate_and_up[:, :slice_width]
    up_pre = gate_and_up[:, slice_width:]
    activated, slope_of = silu_parts(gate_pre)
    hidden = (activated * up_pre).astype(jnp.bfloat16)
    hidden_grad = lax.dot_general(
        rows_d, down_rows, contract_last, preferred_element_type=jnp.float32
    )
    pre_grads = jnp.concatenate(
        [
            (hidden_grad * up_pre * slope_of).astype(jnp.bfloat16),
            (hidden_grad * activated).astype(jnp.bfloat16),
        ],
        axis=1,
    )
    grad_gu = lax.dot_general(
        pre_grads, rows_x, contract_first, preferred_element_type=jnp.float32
    ).astype(jnp.bfloat16)
    grad_dn = lax.dot_general(
        hidden, rows_d, contract_first, preferred_element_type=jnp.float32
    ).astype(jnp.bfloat16)
    slice_part = jnp.dot(pre_grads, gate_up, preferred_element_type=jnp.float32).astype(
        jnp.bfloat16
    )
    grad_pack = jnp.concatenate([grad_gu, grad_dn], axis=0)
    blocks = slice_part.reshape(2, 2, n_rows, col_block, capacity, feature_width)
    upper_half = slice_here // 2 % 2 == 1
    keep_half = jnp.where(upper_half, blocks[1], blocks[0])
    send_half = jnp.where(upper_half, blocks[0], blocks[1])
    got_half = swapped(send_half, "dp", 1)
    pairsum = keep_half.astype(jnp.float32) + got_half.astype(jnp.float32)
    odd_slice = slice_here % 2 == 1
    keep_last = jnp.where(odd_slice, pairsum[1], pairsum[0])
    send_last = jnp.where(odd_slice, pairsum[0], pairsum[1])
    got_last = swapped(send_last, "dp", 0)
    summed = keep_last + got_last
    back_rows = lax.all_to_all(summed, "dp", split_axis=0, concat_axis=0, tiled=True).reshape(
        slot_count, n_cols, capacity, feature_width
    )
    home_rows = lax.all_to_all(
        back_rows, "expert", split_axis=1, concat_axis=1, tiled=True
    ).reshape(buffer_rows, feature_width)
    hits = (
        target.reshape(tok_dev, top_count)[:, :, None]
        == jnp.arange(buffer_rows, dtype=jnp.int32)[None, None, :]
    )
    gather_mat = jnp.sum(hits.astype(jnp.float32), axis=1)
    grad_tokens = jnp.dot(
        gather_mat, home_rows, precision=lax.Precision.HIGHEST, preferred_element_type=jnp.float32
    ).astype(jnp.bfloat16)
    grad_gate_up = grad_pack[: 2 * slice_width].reshape(w_gate_up.shape)
    grad_down = grad_pack[2 * slice_width :].reshape(w_down.shape)
    return (grad_tokens, grad_gate_up, grad_down)


def crossed(block, axis, apart):
    return lax.ppermute(block, axis, [(i, i ^ apart) for i in range(lax.axis_size(axis))])


def whole(count):
    return [pl.BlockSpec(memory_space=pltpu.VMEM)] * count


def packed(tokens, upstream, expert_ids, gates, n_cols):
    experts = jnp.arange(n_cols, dtype=jnp.int32)[None, None, :]
    by_expert = jnp.sum(jnp.where(expert_ids[:, :, None] == experts, gates[:, :, None], 0.0), axis=1)
    high = lax.reduce_precision(by_expert, 8, 7)
    middle = lax.reduce_precision(by_expert - high, 8, 7)
    low = by_expert - high - middle
    spare = jnp.zeros((tokens.shape[0], 128 - 3 * n_cols), jnp.bfloat16)
    summands = [part.astype(jnp.bfloat16) for part in (high, middle, low)]
    return jnp.concatenate([tokens, upstream] + summands + [spare], axis=1)


def weights_kernel(n_cols, relocate_ref, wgu_hbm, wdn_hbm, case_ref, weights_ref, sems):
    split = wgu_hbm.shape[0]
    copies = [
        pltpu.make_async_copy(wgu_hbm, weights_ref.at[pl.ds(0, split)], sems.at[0]),
        pltpu.make_async_copy(wdn_hbm, weights_ref.at[pl.ds(split, wdn_hbm.shape[0])], sems.at[1]),
    ]
    for copy in copies:
        copy.start()
    pairs = n_cols // 4
    case_ref[0] = sum(relocate_ref[col] * 3 ** (pairs - 1 - col // 2) for col in range(n_cols // 2)) - 1
    for copy in copies:
        copy.wait()


def forward_kernel(n_cols, n_rows, n_z, relocate_ref, *refs):
    columns = refs[: n_rows - 1]
    diagonal = refs[n_rows - 1 : n_rows - 1 + n_z]
    weights_own, wgu_sib, wdn_sib, plane_ref, acts_ref, one_ref, kept_ref, *sent_refs = refs[n_rows - 1 + n_z :]
    tok_dev = diagonal[0].shape[0]
    for z in range(n_z):
        for d in range(n_rows):
            start = (z * n_rows + d) * tok_dev
            if d < n_rows - 1:
                block = columns[d][z * tok_dev : (z + 1) * tok_dev]
            else:
                block = diagonal[z][...]
            plane_ref[start : start + tok_dev] = block
    units, width = wdn_sib.shape
    split = wgu_sib.shape[0]
    col_here = lax.axis_index("expert")
    lane = lax.broadcasted_iota(jnp.int32, (8, 128), 1)
    row = lax.broadcasted_iota(jnp.int32, (8, 128), 0)
    wanted = jnp.where(row == 0, col_here, col_here ^ 1)
    chosen = (row < 2) & (lane % n_cols == wanted) & (lane < 3 * n_cols)
    gate_rows = lax.dot_general(
        jnp.where(chosen, 1.0, 0.0).astype(jnp.bfloat16),
        plane_ref[:, 2 * width :],
        contract_last,
        preferred_element_type=jnp.float32,
    )
    rows_x = plane_ref[:, :width]
    rows_u = plane_ref[:, width : 2 * width]
    total = None
    for index, (wgu, wdn) in enumerate(((weights_own[:split], weights_own[split:]), (wgu_sib[...], wdn_sib[...]))):
        gate = gate_rows[index : index + 1, :]
        pre = lax.dot_general(wgu, rows_x, contract_last, preferred_element_type=jnp.float32)
        hidden_grad = gate * lax.dot_general(wdn, rows_u, contract_last, preferred_element_type=jnp.float32)
        activated, slope_of = silu_parts(pre[:units])
        up_pre = pre[units:]
        base = index * 3 * units
        acts_ref[base : base + units] = (hidden_grad * up_pre * slope_of).astype(jnp.bfloat16)
        acts_ref[base + units : base + 2 * units] = (hidden_grad * activated).astype(jnp.bfloat16)
        acts_ref[base + 2 * units : base + 3 * units] = (activated * up_pre * gate).astype(jnp.bfloat16)
        part = lax.dot_general(acts_ref[base : base + 2 * units], wgu, contract_first, preferred_element_type=jnp.float32)
        total = part if total is None else total + part
    for z in range(n_z):
        for d in range(n_rows):
            start = (z * n_rows + d) * tok_dev
            block = total[start : start + tok_dev]
            if d == 0:
                kept_ref[z] = block
            else:
                sent_refs[d - 1][z] = block.astype(jnp.bfloat16)
    one_ref[...] = jnp.where(relocate_ref[col_here] == 1, acts_ref[: 3 * units], acts_ref[3 * units :])


def weight_grad_kernel(same_ref, cross_ref, plane_ref, other_ref, gu_ref, dn_ref):
    units, width = dn_ref.shape
    for out, low, start in ((gu_ref, 0, 0), (dn_ref, 2 * units, width)):
        high = low + out.shape[0]
        out[...] = (
            jnp.dot(same_ref[low:high], plane_ref[:, start : start + width], preferred_element_type=jnp.float32)
            + jnp.dot(cross_ref[low:high], other_ref[:, start : start + width], preferred_element_type=jnp.float32)
        ).astype(jnp.bfloat16)


def join_kernel(*refs):
    joined_ref = refs[-1]
    start = 0
    for block in refs[:-1]:
        joined_ref[start : start + block.shape[0]] = block[...]
        start += block.shape[0]


def sum_kernel(kept_ref, *refs):
    n_z = kept_ref.shape[0]
    got, outs = refs[:-n_z], refs[-n_z:]
    for z, out in enumerate(outs):
        total = kept_ref[z]
        for block in got:
            total += block[z].astype(jnp.float32)
        out[...] = total.astype(out.dtype)


def final_kernel(kept_ref, *refs):
    total = kept_ref[...]
    for block in refs[:-1]:
        total += block[...].astype(jnp.float32)
    refs[-1][...] = total.astype(jnp.bfloat16)


def place_kernel(moving, relocate_ref, acts_ref, *refs):
    *arrived, same_ref, other_ref = refs
    rows, lanes = same_ref.shape
    half = lanes // 2
    col_here = lax.axis_index("expert")
    both = None if 2 not in moving else arrived[-1]
    one = None if 1 not in moving else arrived[0]
    for out, low, col in ((same_ref, 0, col_here), (other_ref, rows, col_here ^ 1)):
        if both is None:
            come = one[...]
        elif one is None:
            come = both[low : low + rows]
        else:
            chip = col_here // 2 % len(moving)
            come = jnp.where(chip == moving.index(1), one[...], both[low : low + rows])
        moved = relocate_ref[col] == 1
        out[:, :half] = jnp.where(moved, come[:, half:], acts_ref[low : low + rows, :half])
        out[:, half:] = jnp.where(moved, come[:, :half], acts_ref[low : low + rows, half:])


def small(megabytes, flops=0, moved=0):
    return dict(
        compiler_params=pltpu.CompilerParams(vmem_limit_bytes=megabytes * 2**20),
        cost_estimate=pl.CostEstimate(flops=flops, bytes_accessed=moved, transcendentals=0),
    )


def exchanges(moving, relocate, acts, one, kept, sent_rows):
    n_cols = lax.axis_size("expert")
    half = n_cols // 2
    placed = jax.ShapeDtypeStruct(one.shape, one.dtype)
    block = kept.shape[1:]

    def route(count):
        return [(col, col ^ half) for col in range(n_cols) if moving[col % half // 2] == count]

    arrived = []
    if 1 in moving:
        arrived.append(lax.ppermute(one, "expert", route(1)))
    if 2 in moving:
        arrived.append(lax.ppermute(acts, "expert", route(2)))
    got = [crossed(rows, "dp", d + 1) for d, rows in enumerate(sent_rows)]
    parts = pl.pallas_call(
        sum_kernel,
        out_shape=[jax.ShapeDtypeStruct(block, jnp.float32)] + [jax.ShapeDtypeStruct(block, jnp.bfloat16)] * (half - 1),
        in_specs=whole(1 + len(got)),
        out_specs=whole(half),
        name="sums",
        **small(4),
    )(kept, *got)
    same, others = pl.pallas_call(
        functools.partial(place_kernel, moving),
        out_shape=[placed, placed],
        in_specs=[pl.BlockSpec(memory_space=pltpu.SMEM)] + whole(1 + len(arrived)),
        out_specs=whole(2),
        name="place",
        **small(4),
    )(relocate, acts, *arrived)
    return same, others, parts


def dense_device(tokens, upstream, expert_ids, gates, relocate, w_gate_up, w_down):
    n_rows = lax.axis_size("dp")
    n_cols = lax.axis_size("expert")
    n_z = n_cols // 2
    tok_dev = tokens.shape[0]
    half = n_cols // 2
    units, width = w_down.shape[2:]
    plane_rows = n_rows * n_z * tok_dev
    bf16 = jnp.bfloat16

    wgu_sib = crossed(w_gate_up[0, 0], "expert", 1)
    wdn_sib = crossed(w_down[0, 0], "expert", 1)
    own = packed(tokens, upstream, expert_ids, gates, n_cols)

    along_z = [crossed(own, "expert", 2 * dz) for dz in range(1, n_z)]
    diagonal = crossed(own, "dp", n_rows - 1)
    pairs = half // 2
    order = lax.optimization_barrier(along_z[:1] + [diagonal] + along_z[1:] + [wgu_sib, wdn_sib])
    wdn_sib, wgu_sib = order.pop(), order.pop()
    along_z, diagonal = order[:1] + order[2:], order[1]
    column = pl.pallas_call(
        join_kernel,
        out_shape=jax.ShapeDtypeStruct((tok_dev * n_z, own.shape[1]), bf16),
        in_specs=whole(n_z),
        out_specs=whole(1)[0],
        name="join",
        **small(4),
    )(own, *along_z)
    columns = [crossed(column, "dp", d) for d in range(1, n_rows - 1)]
    diagonals = [crossed(diagonal, "expert", 2 * dz) for dz in range(1, n_z)]
    columns[0], wgu_own, wdn_own = lax.optimization_barrier((columns[0], w_gate_up[0, 0], w_down[0, 0]))
    case, weights_own = pl.pallas_call(
        functools.partial(weights_kernel, n_cols),
        out_shape=[jax.ShapeDtypeStruct((1,), jnp.int32), jax.ShapeDtypeStruct((3 * units, width), bf16)],
        in_specs=[pl.BlockSpec(memory_space=pltpu.SMEM)] + [pl.BlockSpec(memory_space=pl.ANY)] * 2,
        out_specs=[pl.BlockSpec(memory_space=pltpu.SMEM)] + whole(1),
        scratch_shapes=[pltpu.SemaphoreType.DMA((2,))],
        name="weights",
        **small(4),
    )(relocate[:, 0], wgu_own, wdn_own)

    plane, acts, one, kept, *sent = pl.pallas_call(
        functools.partial(forward_kernel, n_cols, n_rows, n_z),
        out_shape=[
            jax.ShapeDtypeStruct((plane_rows, own.shape[1]), bf16),
            jax.ShapeDtypeStruct((6 * units, plane_rows), bf16),
            jax.ShapeDtypeStruct((3 * units, plane_rows), bf16),
            jax.ShapeDtypeStruct((n_z, tok_dev, width), jnp.float32),
        ]
        + [jax.ShapeDtypeStruct((n_z, tok_dev, width), bf16)] * (n_rows - 1),
        in_specs=[pl.BlockSpec(memory_space=pltpu.SMEM)] + whole(n_rows - 1 + n_z + 3),
        out_specs=whole(3 + n_rows),
        name="forward",
        **small(16, flops=2 * 6 * units * 2 * width * plane_rows, moved=8 * 2**20),
    )(relocate[:, 0], column, *columns, diagonal, *diagonals, weights_own, wgu_sib, wdn_sib)

    plane_sib = crossed(plane, "expert", 1)
    cases = [tuple(number // 3 ** (pairs - 1 - p) % 3 for p in range(pairs)) for number in range(1, 3**pairs - 1)]
    same, others, parts = lax.switch(
        case[0], [functools.partial(exchanges, moving) for moving in cases], relocate[:, 0], acts, one, kept, sent
    )
    cross = crossed(others, "expert", 1)
    got_z = [crossed(parts[dz], "expert", 2 * dz) for dz in range(1, n_z)]
    grad_gu, grad_dn = pl.pallas_call(
        weight_grad_kernel,
        out_shape=[jax.ShapeDtypeStruct((2 * units, width), bf16), jax.ShapeDtypeStruct((units, width), bf16)],
        in_specs=whole(4),
        out_specs=whole(2),
        name="weight_grads",
        **small(16, flops=2 * 3 * units * width * 2 * plane_rows * 8, moved=32 * 2**20),
    )(same, cross, plane, plane_sib)
    kept, grad_dn = lax.optimization_barrier((parts[0], grad_dn))
    grad_tokens = pl.pallas_call(
        final_kernel,
        out_shape=jax.ShapeDtypeStruct((tok_dev, width), bf16),
        in_specs=whole(n_z),
        out_specs=whole(1)[0],
        name="grad_tokens",
        **small(4),
    )(kept, *got_z[::-1])
    return grad_tokens, grad_gu.reshape(w_gate_up.shape), grad_dn.reshape(w_down.shape)


def solution(mesh):
    def per_device(*arrays):
        n_rows, n_cols = mesh.shape["dp"], mesh.shape["expert"]
        dense = n_rows == SLICES and arrays[2].shape[1] == n_cols and 4 <= n_cols <= 8
        return (dense_device if dense else routed_device)(*arrays)

    return jax.shard_map(
        per_device,
        mesh=mesh,
        in_specs=(
            P(("dp", "expert"), None),
            P(("dp", "expert"), None),
            P(("dp", "expert"), None),
            P(("dp", "expert"), None),
            P(),
            P("expert", "dp", None, None),
            P("expert", "dp", None, None),
        ),
        out_specs=(
            P(("dp", "expert"), None),
            P("expert", "dp", None, None),
            P("expert", "dp", None, None),
        ),
        check_vma=False,
    )
```

```python
import functools

import jax
import jax.numpy as jnp
from jax import lax
from jax.experimental import pallas as pl
from jax.experimental.pallas import tpu as pltpu
from jax.sharding import PartitionSpec as P

SLICES = 4


contract_last = (((1,), (1,)), ((), ()))
contract_first = (((0,), (0,)), ((), ()))


def swapped(block, axis, apart):
    count = lax.axis_size(axis)
    route = []
    for low in range(count):
        high = low | 1 << apart
        if high != low and high < count:
            route += [(low, high), (high, low)]
    return lax.ppermute(block, axis, route)


def silu_parts(values_in):
    sigmoid_of = jax.nn.sigmoid(values_in)
    return (values_in * sigmoid_of, sigmoid_of * (1.0 + values_in * (1.0 - sigmoid_of)))


def pick_entry(lookup_table, row_index, col_index):
    rows_hit = jnp.arange(lookup_table.shape[0], dtype=jnp.int32)[:, None] == row_index
    cols_hit = jnp.arange(lookup_table.shape[1], dtype=jnp.int32)[None, :] == col_index
    return jnp.sum(jnp.where(rows_hit & cols_hit, lookup_table, 0))


def routed_device(tokens, upstream, expert_ids, gates, relocate, w_gate_up, w_down):
    n_rows = lax.axis_size("dp")
    n_cols = lax.axis_size("expert")
    slot_count = n_rows // SLICES
    experts = slot_count * n_cols
    tok_dev, feature_width = tokens.shape
    top_count = expert_ids.shape[1]
    capacity = min(tok_dev, max(2, (3 * tok_dev * top_count + 2 * experts - 1) // (2 * experts)))
    pair_count = tok_dev * top_count
    buffer_rows = experts * capacity
    slice_width = w_down.shape[2]
    col_block = n_cols // SLICES
    col_here = lax.axis_index("expert")
    row_here = lax.axis_index("dp")
    slot_here = row_here // SLICES
    slice_here = row_here % SLICES
    far_bit = n_cols.bit_length() - 2
    half_cols = n_cols // 2
    flat_ids = expert_ids.reshape(pair_count)
    home_column = flat_ids // slot_count
    slot_of = flat_ids % slot_count
    expert_iota = jnp.arange(experts, dtype=jnp.int32)
    relocated = jnp.sum(
        jnp.where(flat_ids[:, None] == expert_iota[None, :], relocate.reshape(experts)[None, :], 0),
        axis=1,
    )
    column = (home_column + half_cols * relocated) % n_cols
    pair_iota = jnp.arange(pair_count, dtype=jnp.int32)
    earlier = (flat_ids[:, None] == flat_ids[None, :]) & (pair_iota[None, :] < pair_iota[:, None])
    slot_rank = jnp.sum(earlier.astype(jnp.int32), axis=1)
    target = (slot_of * n_cols + column) * capacity + slot_rank
    placing = (target[None, :] == jnp.arange(buffer_rows, dtype=jnp.int32)[:, None]).astype(
        jnp.bfloat16
    )
    x_pairs = jnp.repeat(tokens, top_count, axis=0)
    d_pairs = (
        gates.reshape(pair_count, 1) * jnp.repeat(upstream, top_count, axis=0).astype(jnp.float32)
    ).astype(jnp.bfloat16)
    pair_data = jnp.stack([x_pairs, d_pairs])
    sent = jnp.einsum("bp,kpw->kbw", placing, pair_data, preferred_element_type=jnp.float32).astype(
        jnp.bfloat16
    )
    sent = sent.reshape(2, slot_count, n_cols, capacity, feature_width)
    at_column = lax.all_to_all(sent, "expert", split_axis=2, concat_axis=2, tiled=True)
    swapped_here = pick_entry(relocate, col_here, slot_here)
    own_pack = jnp.concatenate([w_gate_up, w_down], axis=2)
    far_pack = swapped(own_pack, "expert", far_bit)
    own_pack = jnp.where(swapped_here == 1, far_pack, own_pack)
    gate_up = own_pack[0, 0, : 2 * slice_width]
    down_rows = own_pack[0, 0, 2 * slice_width :]
    grouped = at_column.reshape(2, n_rows, col_block, capacity, feature_width)
    at_row = lax.all_to_all(grouped, "dp", split_axis=1, concat_axis=1, tiled=True)
    gathered = at_row[:, None]
    for bit_index in range(SLICES.bit_length() - 1):
        far_rows = swapped(gathered, "dp", bit_index)
        lower_half = slice_here // (1 << bit_index) % 2 == 0
        first_part = jnp.where(lower_half, gathered, far_rows)
        second_part = jnp.where(lower_half, far_rows, gathered)
        gathered = jnp.concatenate([first_part, second_part], axis=1)
    all_rows = gathered.reshape(2, -1, feature_width)
    rows_x = all_rows[0]
    rows_d = all_rows[1]
    gate_and_up = lax.dot_general(
        rows_x, gate_up, contract_last, preferred_element_type=jnp.float32
    )
    gate_pre = gate_and_up[:, :slice_width]
    up_pre = gate_and_up[:, slice_width:]
    activated, slope_of = silu_parts(gate_pre)
    hidden = (activated * up_pre).astype(jnp.bfloat16)
    hidden_grad = lax.dot_general(
        rows_d, down_rows, contract_last, preferred_element_type=jnp.float32
    )
    pre_grads = jnp.concatenate(
        [
            (hidden_grad * up_pre * slope_of).astype(jnp.bfloat16),
            (hidden_grad * activated).astype(jnp.bfloat16),
        ],
        axis=1,
    )
    grad_gu = lax.dot_general(
        pre_grads, rows_x, contract_first, preferred_element_type=jnp.float32
    ).astype(jnp.bfloat16)
    grad_dn = lax.dot_general(
        hidden, rows_d, contract_first, preferred_element_type=jnp.float32
    ).astype(jnp.bfloat16)
    slice_part = jnp.dot(pre_grads, gate_up, preferred_element_type=jnp.float32).astype(
        jnp.bfloat16
    )
    grad_pack = jnp.concatenate([grad_gu, grad_dn], axis=0)
    blocks = slice_part.reshape(2, 2, n_rows, col_block, capacity, feature_width)
    upper_half = slice_here // 2 % 2 == 1
    keep_half = jnp.where(upper_half, blocks[1], blocks[0])
    send_half = jnp.where(upper_half, blocks[0], blocks[1])
    got_half = swapped(send_half, "dp", 1)
    pairsum = keep_half.astype(jnp.float32) + got_half.astype(jnp.float32)
    odd_slice = slice_here % 2 == 1
    keep_last = jnp.where(odd_slice, pairsum[1], pairsum[0])
    send_last = jnp.where(odd_slice, pairsum[0], pairsum[1])
    got_last = swapped(send_last, "dp", 0)
    summed = keep_last + got_last
    back_rows = lax.all_to_all(summed, "dp", split_axis=0, concat_axis=0, tiled=True).reshape(
        slot_count, n_cols, capacity, feature_width
    )
    home_rows = lax.all_to_all(
        back_rows, "expert", split_axis=1, concat_axis=1, tiled=True
    ).reshape(buffer_rows, feature_width)
    hits = (
        target.reshape(tok_dev, top_count)[:, :, None]
        == jnp.arange(buffer_rows, dtype=jnp.int32)[None, None, :]
    )
    gather_mat = jnp.sum(hits.astype(jnp.float32), axis=1)
    grad_tokens = jnp.dot(
        gather_mat, home_rows, precision=lax.Precision.HIGHEST, preferred_element_type=jnp.float32
    ).astype(jnp.bfloat16)
    grad_gate_up = grad_pack[: 2 * slice_width].reshape(w_gate_up.shape)
    grad_down = grad_pack[2 * slice_width :].reshape(w_down.shape)
    return (grad_tokens, grad_gate_up, grad_down)


def crossed(block, axis, apart):
    return lax.ppermute(block, axis, [(i, i ^ apart) for i in range(lax.axis_size(axis))])


def whole(count):
    return [pl.BlockSpec(memory_space=pltpu.VMEM)] * count


def packed(tokens, upstream, expert_ids, gates, n_cols):
    experts = jnp.arange(n_cols, dtype=jnp.int32)[None, None, :]
    by_expert = jnp.sum(jnp.where(expert_ids[:, :, None] == experts, gates[:, :, None], 0.0), axis=1)
    high = lax.reduce_precision(by_expert, 8, 7)
    middle = lax.reduce_precision(by_expert - high, 8, 7)
    low = by_expert - high - middle
    spare = jnp.zeros((tokens.shape[0], 128 - 3 * n_cols), jnp.bfloat16)
    summands = [part.astype(jnp.bfloat16) for part in (high, middle, low)]
    return jnp.concatenate([tokens, upstream] + summands + [spare], axis=1)


def weights_kernel(n_cols, relocate_ref, wgu_hbm, wdn_hbm, case_ref, weights_ref, sems):
    split = wgu_hbm.shape[0]
    copies = [
        pltpu.make_async_copy(wgu_hbm, weights_ref.at[pl.ds(0, split)], sems.at[0]),
        pltpu.make_async_copy(wdn_hbm, weights_ref.at[pl.ds(split, wdn_hbm.shape[0])], sems.at[1]),
    ]
    for copy in copies:
        copy.start()
    pairs = n_cols // 4
    case_ref[0] = sum(relocate_ref[col] * 3 ** (pairs - 1 - col // 2) for col in range(n_cols // 2)) - 1
    for copy in copies:
        copy.wait()


def forward_kernel(n_cols, n_rows, n_z, relocate_ref, *refs):
    columns = refs[: n_rows - 1]
    diagonal = refs[n_rows - 1 : n_rows - 1 + n_z]
    weights_own, wgu_sib, wdn_sib, plane_ref, acts_ref, one_ref, kept_ref, *sent_refs = refs[n_rows - 1 + n_z :]
    tok_dev = diagonal[0].shape[0]
    for z in range(n_z):
        for d in range(n_rows):
            start = (z * n_rows + d) * tok_dev
            if d < n_rows - 1:
                block = columns[d][z * tok_dev : (z + 1) * tok_dev]
            else:
                block = diagonal[z][...]
            plane_ref[start : start + tok_dev] = block
    units, width = wdn_sib.shape
    split = wgu_sib.shape[0]
    col_here = lax.axis_index("expert")
    lane = lax.broadcasted_iota(jnp.int32, (8, 128), 1)
    row = lax.broadcasted_iota(jnp.int32, (8, 128), 0)
    wanted = jnp.where(row == 0, col_here, col_here ^ 1)
    chosen = (row < 2) & (lane % n_cols == wanted) & (lane < 3 * n_cols)
    gate_rows = lax.dot_general(
        jnp.where(chosen, 1.0, 0.0).astype(jnp.bfloat16),
        plane_ref[:, 2 * width :],
        contract_last,
        preferred_element_type=jnp.float32,
    )
    rows_x = plane_ref[:, :width]
    rows_u = plane_ref[:, width : 2 * width]
    total = None
    for index, (wgu, wdn) in enumerate(((weights_own[:split], weights_own[split:]), (wgu_sib[...], wdn_sib[...]))):
        gate = gate_rows[index : index + 1, :]
        pre = lax.dot_general(wgu, rows_x, contract_last, preferred_element_type=jnp.float32)
        hidden_grad = gate * lax.dot_general(wdn, rows_u, contract_last, preferred_element_type=jnp.float32)
        activated, slope_of = silu_parts(pre[:units])
        up_pre = pre[units:]
        base = index * 3 * units
        acts_ref[base : base + units] = (hidden_grad * up_pre * slope_of).astype(jnp.bfloat16)
        acts_ref[base + units : base + 2 * units] = (hidden_grad * activated).astype(jnp.bfloat16)
        acts_ref[base + 2 * units : base + 3 * units] = (activated * up_pre * gate).astype(jnp.bfloat16)
        part = lax.dot_general(acts_ref[base : base + 2 * units], wgu, contract_first, preferred_element_type=jnp.float32)
        total = part if total is None else total + part
    for z in range(n_z):
        for d in range(n_rows):
            start = (z * n_rows + d) * tok_dev
            block = total[start : start + tok_dev]
            if d == 0:
                kept_ref[z] = block
            else:
                sent_refs[d - 1][z] = block.astype(jnp.bfloat16)
    one_ref[...] = jnp.where(relocate_ref[col_here] == 1, acts_ref[: 3 * units], acts_ref[3 * units :])


def weight_grad_kernel(same_ref, cross_ref, plane_ref, other_ref, gu_ref, dn_ref):
    units, width = dn_ref.shape
    for out, low, start in ((gu_ref, 0, 0), (dn_ref, 2 * units, width)):
        high = low + out.shape[0]
        out[...] = (
            jnp.dot(same_ref[low:high], plane_ref[:, start : start + width], preferred_element_type=jnp.float32)
            + jnp.dot(cross_ref[low:high], other_ref[:, start : start + width], preferred_element_type=jnp.float32)
        ).astype(jnp.bfloat16)


def join_kernel(*refs):
    joined_ref = refs[-1]
    start = 0
    for block in refs[:-1]:
        joined_ref[start : start + block.shape[0]] = block[...]
        start += block.shape[0]


def sum_kernel(kept_ref, *refs):
    n_z = kept_ref.shape[0]
    got, outs = refs[:-n_z], refs[-n_z:]
    for z, out in enumerate(outs):
        total = kept_ref[z]
        for block in got:
            total += block[z].astype(jnp.float32)
        out[...] = total.astype(out.dtype)


def final_kernel(kept_ref, *refs):
    total = kept_ref[...]
    for block in refs[:-1]:
        total += block[...].astype(jnp.float32)
    refs[-1][...] = total.astype(jnp.bfloat16)


def place_kernel(moving, relocate_ref, acts_ref, *refs):
    *arrived, same_ref, other_ref = refs
    rows, lanes = same_ref.shape
    half = lanes // 2
    col_here = lax.axis_index("expert")
    both = None if 2 not in moving else arrived[-1]
    one = None if 1 not in moving else arrived[0]
    for out, low, col in ((same_ref, 0, col_here), (other_ref, rows, col_here ^ 1)):
        if both is None:
            come = one[...]
        elif one is None:
            come = both[low : low + rows]
        else:
            chip = col_here // 2 % len(moving)
            come = jnp.where(chip == moving.index(1), one[...], both[low : low + rows])
        moved = relocate_ref[col] == 1
        out[:, :half] = jnp.where(moved, come[:, half:], acts_ref[low : low + rows, :half])
        out[:, half:] = jnp.where(moved, come[:, :half], acts_ref[low : low + rows, half:])


def small(megabytes, flops=0, moved=0):
    return dict(
        compiler_params=pltpu.CompilerParams(vmem_limit_bytes=megabytes * 2**20),
        cost_estimate=pl.CostEstimate(flops=flops, bytes_accessed=moved, transcendentals=0),
    )


def exchanges(moving, relocate, acts, one, kept, sent_rows):
    n_cols = lax.axis_size("expert")
    half = n_cols // 2
    placed = jax.ShapeDtypeStruct(one.shape, one.dtype)
    block = kept.shape[1:]

    def route(count):
        return [(col, col ^ half) for col in range(n_cols) if moving[col % half // 2] == count]

    arrived = []
    if 1 in moving:
        arrived.append(lax.ppermute(one, "expert", route(1)))
    if 2 in moving:
        arrived.append(lax.ppermute(acts, "expert", route(2)))
    got = [crossed(rows, "dp", d + 1) for d, rows in enumerate(sent_rows)]
    parts = pl.pallas_call(
        sum_kernel,
        out_shape=[jax.ShapeDtypeStruct(block, jnp.float32)] + [jax.ShapeDtypeStruct(block, jnp.bfloat16)] * (half - 1),
        in_specs=whole(1 + len(got)),
        out_specs=whole(half),
        name="sums",
        **small(4),
    )(kept, *got)
    same, others = pl.pallas_call(
        functools.partial(place_kernel, moving),
        out_shape=[placed, placed],
        in_specs=[pl.BlockSpec(memory_space=pltpu.SMEM)] + whole(1 + len(arrived)),
        out_specs=whole(2),
        name="place",
        **small(4),
    )(relocate, acts, *arrived)
    return same, others, parts


def dense_device(tokens, upstream, expert_ids, gates, relocate, w_gate_up, w_down):
    n_rows = lax.axis_size("dp")
    n_cols = lax.axis_size("expert")
    n_z = n_cols // 2
    tok_dev = tokens.shape[0]
    half = n_cols // 2
    units, width = w_down.shape[2:]
    plane_rows = n_rows * n_z * tok_dev
    bf16 = jnp.bfloat16

    wgu_sib = crossed(w_gate_up[0, 0], "expert", 1)
    wdn_sib = crossed(w_down[0, 0], "expert", 1)
    own = packed(tokens, upstream, expert_ids, gates, n_cols)

    pairs = half // 2
    near_z = crossed(own, "expert", 2)
    across = crossed(own, "expert", half)
    diagonal = crossed(own, "dp", n_rows - 1)
    across, near_z = lax.optimization_barrier((across, near_z))
    beyond = crossed(across, "expert", 2)
    along_z = [near_z, across, beyond]
    along_z, diagonal, wgu_sib, wdn_sib = lax.optimization_barrier((along_z, diagonal, wgu_sib, wdn_sib))
    column = pl.pallas_call(
        join_kernel,
        out_shape=jax.ShapeDtypeStruct((tok_dev * n_z, own.shape[1]), bf16),
        in_specs=whole(n_z),
        out_specs=whole(1)[0],
        name="join",
        **small(4),
    )(own, *along_z)
    columns = [crossed(column, "dp", d) for d in range(1, n_rows - 1)]
    diagonals = [crossed(diagonal, "expert", 2 * dz) for dz in range(1, n_z)]
    columns[0], wgu_own, wdn_own = lax.optimization_barrier((columns[0], w_gate_up[0, 0], w_down[0, 0]))
    case, weights_own = pl.pallas_call(
        functools.partial(weights_kernel, n_cols),
        out_shape=[jax.ShapeDtypeStruct((1,), jnp.int32), jax.ShapeDtypeStruct((3 * units, width), bf16)],
        in_specs=[pl.BlockSpec(memory_space=pltpu.SMEM)] + [pl.BlockSpec(memory_space=pl.ANY)] * 2,
        out_specs=[pl.BlockSpec(memory_space=pltpu.SMEM)] + whole(1),
        scratch_shapes=[pltpu.SemaphoreType.DMA((2,))],
        name="weights",
        **small(4),
    )(relocate[:, 0], wgu_own, wdn_own)

    plane, acts, one, kept, *sent = pl.pallas_call(
        functools.partial(forward_kernel, n_cols, n_rows, n_z),
        out_shape=[
            jax.ShapeDtypeStruct((plane_rows, own.shape[1]), bf16),
            jax.ShapeDtypeStruct((6 * units, plane_rows), bf16),
            jax.ShapeDtypeStruct((3 * units, plane_rows), bf16),
            jax.ShapeDtypeStruct((n_z, tok_dev, width), jnp.float32),
        ]
        + [jax.ShapeDtypeStruct((n_z, tok_dev, width), bf16)] * (n_rows - 1),
        in_specs=[pl.BlockSpec(memory_space=pltpu.SMEM)] + whole(n_rows - 1 + n_z + 3),
        out_specs=whole(3 + n_rows),
        name="forward",
        **small(16, flops=2 * 6 * units * 2 * width * plane_rows, moved=8 * 2**20),
    )(relocate[:, 0], column, *columns, diagonal, *diagonals, weights_own, wgu_sib, wdn_sib)

    plane_sib = crossed(plane, "expert", 1)
    cases = [tuple(number // 3 ** (pairs - 1 - p) % 3 for p in range(pairs)) for number in range(1, 3**pairs - 1)]
    same, others, parts = lax.switch(
        case[0], [functools.partial(exchanges, moving) for moving in cases], relocate[:, 0], acts, one, kept, sent
    )
    cross = crossed(others, "expert", 1)
    got_z = [crossed(parts[dz], "expert", 2 * dz) for dz in range(1, n_z)]
    grad_gu, grad_dn = pl.pallas_call(
        weight_grad_kernel,
        out_shape=[jax.ShapeDtypeStruct((2 * units, width), bf16), jax.ShapeDtypeStruct((units, width), bf16)],
        in_specs=whole(4),
        out_specs=whole(2),
        name="weight_grads",
        **small(16, flops=2 * 3 * units * width * 2 * plane_rows * 8, moved=32 * 2**20),
    )(same, cross, plane, plane_sib)
    kept, grad_dn = lax.optimization_barrier((parts[0], grad_dn))
    grad_tokens = pl.pallas_call(
        final_kernel,
        out_shape=jax.ShapeDtypeStruct((tok_dev, width), bf16),
        in_specs=whole(n_z),
        out_specs=whole(1)[0],
        name="grad_tokens",
        **small(4),
    )(kept, *got_z[::-1])
    return grad_tokens, grad_gu.reshape(w_gate_up.shape), grad_dn.reshape(w_down.shape)


def solution(mesh):
    def per_device(*arrays):
        n_rows, n_cols = mesh.shape["dp"], mesh.shape["expert"]
        dense = n_rows == SLICES and arrays[2].shape[1] == n_cols and 4 <= n_cols <= 8
        return (dense_device if dense else routed_device)(*arrays)

    return jax.shard_map(
        per_device,
        mesh=mesh,
        in_specs=(
            P(("dp", "expert"), None),
            P(("dp", "expert"), None),
            P(("dp", "expert"), None),
            P(("dp", "expert"), None),
            P(),
            P("expert", "dp", None, None),
            P("expert", "dp", None, None),
        ),
        out_specs=(
            P(("dp", "expert"), None),
            P("expert", "dp", None, None),
            P("expert", "dp", None, None),
        ),
        check_vma=False,
    )
```

```python
import functools

import jax
import jax.numpy as jnp
from jax import lax
from jax.experimental import pallas as pl
from jax.experimental.pallas import tpu as pltpu
from jax.sharding import PartitionSpec as P

SLICES = 4


contract_last = (((1,), (1,)), ((), ()))
contract_first = (((0,), (0,)), ((), ()))


def swapped(block, axis, apart):
    count = lax.axis_size(axis)
    route = []
    for low in range(count):
        high = low | 1 << apart
        if high != low and high < count:
            route += [(low, high), (high, low)]
    return lax.ppermute(block, axis, route)


def silu_parts(values_in):
    sigmoid_of = jax.nn.sigmoid(values_in)
    return (values_in * sigmoid_of, sigmoid_of * (1.0 + values_in * (1.0 - sigmoid_of)))


def pick_entry(lookup_table, row_index, col_index):
    rows_hit = jnp.arange(lookup_table.shape[0], dtype=jnp.int32)[:, None] == row_index
    cols_hit = jnp.arange(lookup_table.shape[1], dtype=jnp.int32)[None, :] == col_index
    return jnp.sum(jnp.where(rows_hit & cols_hit, lookup_table, 0))


def routed_device(tokens, upstream, expert_ids, gates, relocate, w_gate_up, w_down):
    n_rows = lax.axis_size("dp")
    n_cols = lax.axis_size("expert")
    slot_count = n_rows // SLICES
    experts = slot_count * n_cols
    tok_dev, feature_width = tokens.shape
    top_count = expert_ids.shape[1]
    capacity = min(tok_dev, max(2, (3 * tok_dev * top_count + 2 * experts - 1) // (2 * experts)))
    pair_count = tok_dev * top_count
    buffer_rows = experts * capacity
    slice_width = w_down.shape[2]
    col_block = n_cols // SLICES
    col_here = lax.axis_index("expert")
    row_here = lax.axis_index("dp")
    slot_here = row_here // SLICES
    slice_here = row_here % SLICES
    far_bit = n_cols.bit_length() - 2
    half_cols = n_cols // 2
    flat_ids = expert_ids.reshape(pair_count)
    home_column = flat_ids // slot_count
    slot_of = flat_ids % slot_count
    expert_iota = jnp.arange(experts, dtype=jnp.int32)
    relocated = jnp.sum(
        jnp.where(flat_ids[:, None] == expert_iota[None, :], relocate.reshape(experts)[None, :], 0),
        axis=1,
    )
    column = (home_column + half_cols * relocated) % n_cols
    pair_iota = jnp.arange(pair_count, dtype=jnp.int32)
    earlier = (flat_ids[:, None] == flat_ids[None, :]) & (pair_iota[None, :] < pair_iota[:, None])
    slot_rank = jnp.sum(earlier.astype(jnp.int32), axis=1)
    target = (slot_of * n_cols + column) * capacity + slot_rank
    placing = (target[None, :] == jnp.arange(buffer_rows, dtype=jnp.int32)[:, None]).astype(
        jnp.bfloat16
    )
    x_pairs = jnp.repeat(tokens, top_count, axis=0)
    d_pairs = (
        gates.reshape(pair_count, 1) * jnp.repeat(upstream, top_count, axis=0).astype(jnp.float32)
    ).astype(jnp.bfloat16)
    pair_data = jnp.stack([x_pairs, d_pairs])
    sent = jnp.einsum("bp,kpw->kbw", placing, pair_data, preferred_element_type=jnp.float32).astype(
        jnp.bfloat16
    )
    sent = sent.reshape(2, slot_count, n_cols, capacity, feature_width)
    at_column = lax.all_to_all(sent, "expert", split_axis=2, concat_axis=2, tiled=True)
    swapped_here = pick_entry(relocate, col_here, slot_here)
    own_pack = jnp.concatenate([w_gate_up, w_down], axis=2)
    far_pack = swapped(own_pack, "expert", far_bit)
    own_pack = jnp.where(swapped_here == 1, far_pack, own_pack)
    gate_up = own_pack[0, 0, : 2 * slice_width]
    down_rows = own_pack[0, 0, 2 * slice_width :]
    grouped = at_column.reshape(2, n_rows, col_block, capacity, feature_width)
    at_row = lax.all_to_all(grouped, "dp", split_axis=1, concat_axis=1, tiled=True)
    gathered = at_row[:, None]
    for bit_index in range(SLICES.bit_length() - 1):
        far_rows = swapped(gathered, "dp", bit_index)
        lower_half = slice_here // (1 << bit_index) % 2 == 0
        first_part = jnp.where(lower_half, gathered, far_rows)
        second_part = jnp.where(lower_half, far_rows, gathered)
        gathered = jnp.concatenate([first_part, second_part], axis=1)
    all_rows = gathered.reshape(2, -1, feature_width)
    rows_x = all_rows[0]
    rows_d = all_rows[1]
    gate_and_up = lax.dot_general(
        rows_x, gate_up, contract_last, preferred_element_type=jnp.float32
    )
    gate_pre = gate_and_up[:, :slice_width]
    up_pre = gate_and_up[:, slice_width:]
    activated, slope_of = silu_parts(gate_pre)
    hidden = (activated * up_pre).astype(jnp.bfloat16)
    hidden_grad = lax.dot_general(
        rows_d, down_rows, contract_last, preferred_element_type=jnp.float32
    )
    pre_grads = jnp.concatenate(
        [
            (hidden_grad * up_pre * slope_of).astype(jnp.bfloat16),
            (hidden_grad * activated).astype(jnp.bfloat16),
        ],
        axis=1,
    )
    grad_gu = lax.dot_general(
        pre_grads, rows_x, contract_first, preferred_element_type=jnp.float32
    ).astype(jnp.bfloat16)
    grad_dn = lax.dot_general(
        hidden, rows_d, contract_first, preferred_element_type=jnp.float32
    ).astype(jnp.bfloat16)
    slice_part = jnp.dot(pre_grads, gate_up, preferred_element_type=jnp.float32).astype(
        jnp.bfloat16
    )
    grad_pack = jnp.concatenate([grad_gu, grad_dn], axis=0)
    blocks = slice_part.reshape(2, 2, n_rows, col_block, capacity, feature_width)
    upper_half = slice_here // 2 % 2 == 1
    keep_half = jnp.where(upper_half, blocks[1], blocks[0])
    send_half = jnp.where(upper_half, blocks[0], blocks[1])
    got_half = swapped(send_half, "dp", 1)
    pairsum = keep_half.astype(jnp.float32) + got_half.astype(jnp.float32)
    odd_slice = slice_here % 2 == 1
    keep_last = jnp.where(odd_slice, pairsum[1], pairsum[0])
    send_last = jnp.where(odd_slice, pairsum[0], pairsum[1])
    got_last = swapped(send_last, "dp", 0)
    summed = keep_last + got_last
    back_rows = lax.all_to_all(summed, "dp", split_axis=0, concat_axis=0, tiled=True).reshape(
        slot_count, n_cols, capacity, feature_width
    )
    home_rows = lax.all_to_all(
        back_rows, "expert", split_axis=1, concat_axis=1, tiled=True
    ).reshape(buffer_rows, feature_width)
    hits = (
        target.reshape(tok_dev, top_count)[:, :, None]
        == jnp.arange(buffer_rows, dtype=jnp.int32)[None, None, :]
    )
    gather_mat = jnp.sum(hits.astype(jnp.float32), axis=1)
    grad_tokens = jnp.dot(
        gather_mat, home_rows, precision=lax.Precision.HIGHEST, preferred_element_type=jnp.float32
    ).astype(jnp.bfloat16)
    grad_gate_up = grad_pack[: 2 * slice_width].reshape(w_gate_up.shape)
    grad_down = grad_pack[2 * slice_width :].reshape(w_down.shape)
    return (grad_tokens, grad_gate_up, grad_down)


def crossed(block, axis, apart):
    return lax.ppermute(block, axis, [(i, i ^ apart) for i in range(lax.axis_size(axis))])


def whole(count):
    return [pl.BlockSpec(memory_space=pltpu.VMEM)] * count


def packed(tokens, upstream, expert_ids, gates, n_cols):
    experts = jnp.arange(n_cols, dtype=jnp.int32)[None, None, :]
    by_expert = jnp.sum(jnp.where(expert_ids[:, :, None] == experts, gates[:, :, None], 0.0), axis=1)
    high = lax.reduce_precision(by_expert, 8, 7)
    middle = lax.reduce_precision(by_expert - high, 8, 7)
    low = by_expert - high - middle
    spare = jnp.zeros((tokens.shape[0], 128 - 3 * n_cols), jnp.bfloat16)
    summands = [part.astype(jnp.bfloat16) for part in (high, middle, low)]
    return jnp.concatenate([tokens, upstream] + summands + [spare], axis=1)


def case_kernel(n_cols, relocate_ref, case_ref):
    pairs = n_cols // 4
    case_ref[0] = sum(relocate_ref[col] * 3 ** (pairs - 1 - col // 2) for col in range(n_cols // 2)) - 1


def weights_kernel(wgu_hbm, wdn_hbm, weights_ref, sems):
    split = wgu_hbm.shape[0]
    copies = [
        pltpu.make_async_copy(wgu_hbm, weights_ref.at[pl.ds(0, split)], sems.at[0]),
        pltpu.make_async_copy(wdn_hbm, weights_ref.at[pl.ds(split, wdn_hbm.shape[0])], sems.at[1]),
    ]
    for copy in copies:
        copy.start()
    for copy in copies:
        copy.wait()


def forward_kernel(n_cols, n_rows, n_z, relocate_ref, *refs):
    columns = refs[: n_rows - 1]
    diagonal = refs[n_rows - 1 : n_rows - 1 + n_z]
    weights_own, wgu_sib, wdn_sib, plane_ref, acts_ref, one_ref, kept_ref, *sent_refs = refs[n_rows - 1 + n_z :]
    tok_dev = diagonal[0].shape[0]
    for z in range(n_z):
        for d in range(n_rows):
            start = (z * n_rows + d) * tok_dev
            if d < n_rows - 1:
                block = columns[d][z * tok_dev : (z + 1) * tok_dev]
            else:
                block = diagonal[z][...]
            plane_ref[start : start + tok_dev] = block
    units, width = wdn_sib.shape
    split = wgu_sib.shape[0]
    col_here = lax.axis_index("expert")
    lane = lax.broadcasted_iota(jnp.int32, (8, 128), 1)
    row = lax.broadcasted_iota(jnp.int32, (8, 128), 0)
    wanted = jnp.where(row == 0, col_here, col_here ^ 1)
    chosen = (row < 2) & (lane % n_cols == wanted) & (lane < 3 * n_cols)
    gate_rows = lax.dot_general(
        jnp.where(chosen, 1.0, 0.0).astype(jnp.bfloat16),
        plane_ref[:, 2 * width :],
        contract_last,
        preferred_element_type=jnp.float32,
    )
    rows_x = plane_ref[:, :width]
    rows_u = plane_ref[:, width : 2 * width]
    total = None
    for index, (wgu, wdn) in enumerate(((weights_own[:split], weights_own[split:]), (wgu_sib[...], wdn_sib[...]))):
        gate = gate_rows[index : index + 1, :]
        pre = lax.dot_general(wgu, rows_x, contract_last, preferred_element_type=jnp.float32)
        hidden_grad = gate * lax.dot_general(wdn, rows_u, contract_last, preferred_element_type=jnp.float32)
        activated, slope_of = silu_parts(pre[:units])
        up_pre = pre[units:]
        base = index * 3 * units
        acts_ref[base : base + units] = (hidden_grad * up_pre * slope_of).astype(jnp.bfloat16)
        acts_ref[base + units : base + 2 * units] = (hidden_grad * activated).astype(jnp.bfloat16)
        acts_ref[base + 2 * units : base + 3 * units] = (activated * up_pre * gate).astype(jnp.bfloat16)
        part = lax.dot_general(acts_ref[base : base + 2 * units], wgu, contract_first, preferred_element_type=jnp.float32)
        total = part if total is None else total + part
    for z in range(n_z):
        for d in range(n_rows):
            start = (z * n_rows + d) * tok_dev
            block = total[start : start + tok_dev]
            if d == 0:
                kept_ref[z] = block
            else:
                sent_refs[d - 1][z] = block.astype(jnp.bfloat16)
    one_ref[...] = jnp.where(relocate_ref[col_here] == 1, acts_ref[: 3 * units], acts_ref[3 * units :])


def weight_grad_kernel(same_ref, cross_ref, plane_ref, other_ref, gu_ref, dn_ref):
    units, width = dn_ref.shape
    for out, low, start in ((gu_ref, 0, 0), (dn_ref, 2 * units, width)):
        high = low + out.shape[0]
        out[...] = (
            jnp.dot(same_ref[low:high], plane_ref[:, start : start + width], preferred_element_type=jnp.float32)
            + jnp.dot(cross_ref[low:high], other_ref[:, start : start + width], preferred_element_type=jnp.float32)
        ).astype(jnp.bfloat16)


def join_kernel(*refs):
    joined_ref = refs[-1]
    start = 0
    for block in refs[:-1]:
        joined_ref[start : start + block.shape[0]] = block[...]
        start += block.shape[0]


def sum_kernel(kept_ref, *refs):
    n_z = kept_ref.shape[0]
    got, outs = refs[:-n_z], refs[-n_z:]
    for z, out in enumerate(outs):
        total = kept_ref[z]
        for block in got:
            total += block[z].astype(jnp.float32)
        out[...] = total.astype(out.dtype)


def final_kernel(kept_ref, *refs):
    total = kept_ref[...]
    for block in refs[:-1]:
        total += block[...].astype(jnp.float32)
    refs[-1][...] = total.astype(jnp.bfloat16)


def place_kernel(moving, relocate_ref, acts_ref, *refs):
    *arrived, same_ref, other_ref = refs
    rows, lanes = same_ref.shape
    half = lanes // 2
    col_here = lax.axis_index("expert")
    both = None if 2 not in moving else arrived[-1]
    one = None if 1 not in moving else arrived[0]
    for out, low, col in ((same_ref, 0, col_here), (other_ref, rows, col_here ^ 1)):
        if both is None:
            come = one[...]
        elif one is None:
            come = both[low : low + rows]
        else:
            chip = col_here // 2 % len(moving)
            come = jnp.where(chip == moving.index(1), one[...], both[low : low + rows])
        moved = relocate_ref[col] == 1
        out[:, :half] = jnp.where(moved, come[:, half:], acts_ref[low : low + rows, :half])
        out[:, half:] = jnp.where(moved, come[:, :half], acts_ref[low : low + rows, half:])


def small(megabytes, flops=0, moved=0):
    return dict(
        compiler_params=pltpu.CompilerParams(vmem_limit_bytes=megabytes * 2**20),
        cost_estimate=pl.CostEstimate(flops=flops, bytes_accessed=moved, transcendentals=0),
    )


def exchanges(moving, relocate, acts, one, kept, sent_rows):
    n_cols = lax.axis_size("expert")
    half = n_cols // 2
    placed = jax.ShapeDtypeStruct(one.shape, one.dtype)
    block = kept.shape[1:]

    def route(count):
        return [(col, col ^ half) for col in range(n_cols) if moving[col % half // 2] == count]

    arrived = []
    if 1 in moving:
        arrived.append(lax.ppermute(one, "expert", route(1)))
    if 2 in moving:
        arrived.append(lax.ppermute(acts, "expert", route(2)))
    got = [crossed(rows, "dp", d + 1) for d, rows in enumerate(sent_rows)]
    parts = pl.pallas_call(
        sum_kernel,
        out_shape=[jax.ShapeDtypeStruct(block, jnp.float32)] + [jax.ShapeDtypeStruct(block, jnp.bfloat16)] * (half - 1),
        in_specs=whole(1 + len(got)),
        out_specs=whole(half),
        name="sums",
        **small(4),
    )(kept, *got)
    same, others = pl.pallas_call(
        functools.partial(place_kernel, moving),
        out_shape=[placed, placed],
        in_specs=[pl.BlockSpec(memory_space=pltpu.SMEM)] + whole(1 + len(arrived)),
        out_specs=whole(2),
        name="place",
        **small(4),
    )(relocate, acts, *arrived)
    return same, others, parts


def dense_device(tokens, upstream, expert_ids, gates, relocate, w_gate_up, w_down):
    n_rows = lax.axis_size("dp")
    n_cols = lax.axis_size("expert")
    n_z = n_cols // 2
    tok_dev = tokens.shape[0]
    half = n_cols // 2
    units, width = w_down.shape[2:]
    plane_rows = n_rows * n_z * tok_dev
    bf16 = jnp.bfloat16

    wgu_sib = crossed(w_gate_up[0, 0], "expert", 1)
    wdn_sib = crossed(w_down[0, 0], "expert", 1)
    own = packed(tokens, upstream, expert_ids, gates, n_cols)

    pairs = half // 2
    near_z = crossed(own, "expert", 2)
    across = crossed(own, "expert", half)
    diagonal = crossed(own, "dp", n_rows - 1)
    across, near_z, flags = lax.optimization_barrier((across, near_z, relocate[:, 0]))
    beyond = crossed(across, "expert", 2)
    along_z = [near_z, across, beyond]
    case = pl.pallas_call(
        functools.partial(case_kernel, n_cols),
        out_shape=jax.ShapeDtypeStruct((1,), jnp.int32),
        in_specs=[pl.BlockSpec(memory_space=pltpu.SMEM)],
        out_specs=pl.BlockSpec(memory_space=pltpu.SMEM),
        name="case",
        **small(4),
    )(flags)
    along_z, diagonal, wgu_sib, wdn_sib, case = lax.optimization_barrier((along_z, diagonal, wgu_sib, wdn_sib, case))
    column = pl.pallas_call(
        join_kernel,
        out_shape=jax.ShapeDtypeStruct((tok_dev * n_z, own.shape[1]), bf16),
        in_specs=whole(n_z),
        out_specs=whole(1)[0],
        name="join",
        **small(4),
    )(own, *along_z)
    columns = [crossed(column, "dp", d) for d in range(1, n_rows - 1)]
    diagonals = [crossed(diagonal, "expert", 2 * dz) for dz in range(1, n_z)]
    columns[0], wgu_own, wdn_own = lax.optimization_barrier((columns[0], w_gate_up[0, 0], w_down[0, 0]))
    weights_own = pl.pallas_call(
        weights_kernel,
        out_shape=jax.ShapeDtypeStruct((3 * units, width), bf16),
        in_specs=[pl.BlockSpec(memory_space=pl.ANY)] * 2,
        out_specs=whole(1)[0],
        scratch_shapes=[pltpu.SemaphoreType.DMA((2,))],
        name="weights",
        **small(4),
    )(wgu_own, wdn_own)

    plane, acts, one, kept, *sent = pl.pallas_call(
        functools.partial(forward_kernel, n_cols, n_rows, n_z),
        out_shape=[
            jax.ShapeDtypeStruct((plane_rows, own.shape[1]), bf16),
            jax.ShapeDtypeStruct((6 * units, plane_rows), bf16),
            jax.ShapeDtypeStruct((3 * units, plane_rows), bf16),
            jax.ShapeDtypeStruct((n_z, tok_dev, width), jnp.float32),
        ]
        + [jax.ShapeDtypeStruct((n_z, tok_dev, width), bf16)] * (n_rows - 1),
        in_specs=[pl.BlockSpec(memory_space=pltpu.SMEM)] + whole(n_rows - 1 + n_z + 3),
        out_specs=whole(3 + n_rows),
        name="forward",
        **small(16, flops=2 * 6 * units * 2 * width * plane_rows, moved=8 * 2**20),
    )(relocate[:, 0], column, *columns, diagonal, *diagonals, weights_own, wgu_sib, wdn_sib)

    plane_sib = crossed(plane, "expert", 1)
    cases = [tuple(number // 3 ** (pairs - 1 - p) % 3 for p in range(pairs)) for number in range(1, 3**pairs - 1)]
    same, others, parts = lax.switch(
        case[0], [functools.partial(exchanges, moving) for moving in cases], relocate[:, 0], acts, one, kept, sent
    )
    cross = crossed(others, "expert", 1)
    got_z = [crossed(parts[dz], "expert", 2 * dz) for dz in range(1, n_z)]
    grad_gu, grad_dn = pl.pallas_call(
        weight_grad_kernel,
        out_shape=[jax.ShapeDtypeStruct((2 * units, width), bf16), jax.ShapeDtypeStruct((units, width), bf16)],
        in_specs=whole(4),
        out_specs=whole(2),
        name="weight_grads",
        **small(16, flops=2 * 3 * units * width * 2 * plane_rows * 8, moved=32 * 2**20),
    )(same, cross, plane, plane_sib)
    kept, grad_dn = lax.optimization_barrier((parts[0], grad_dn))
    grad_tokens = pl.pallas_call(
        final_kernel,
        out_shape=jax.ShapeDtypeStruct((tok_dev, width), bf16),
        in_specs=whole(n_z),
        out_specs=whole(1)[0],
        name="grad_tokens",
        **small(4),
    )(kept, *got_z[::-1])
    return grad_tokens, grad_gu.reshape(w_gate_up.shape), grad_dn.reshape(w_down.shape)


def solution(mesh):
    def per_device(*arrays):
        n_rows, n_cols = mesh.shape["dp"], mesh.shape["expert"]
        dense = n_rows == SLICES and arrays[2].shape[1] == n_cols and 4 <= n_cols <= 8
        return (dense_device if dense else routed_device)(*arrays)

    return jax.shard_map(
        per_device,
        mesh=mesh,
        in_specs=(
            P(("dp", "expert"), None),
            P(("dp", "expert"), None),
            P(("dp", "expert"), None),
            P(("dp", "expert"), None),
            P(),
            P("expert", "dp", None, None),
            P("expert", "dp", None, None),
        ),
        out_specs=(
            P(("dp", "expert"), None),
            P("expert", "dp", None, None),
            P("expert", "dp", None, None),
        ),
        check_vma=False,
    )
```

```python
import functools

import jax
import jax.numpy as jnp
from jax import lax
from jax.experimental import pallas as pl
from jax.experimental.pallas import tpu as pltpu
from jax.sharding import PartitionSpec as P

SLICES = 4


contract_last = (((1,), (1,)), ((), ()))
contract_first = (((0,), (0,)), ((), ()))


def swapped(block, axis, apart):
    count = lax.axis_size(axis)
    route = []
    for low in range(count):
        high = low | 1 << apart
        if high != low and high < count:
            route += [(low, high), (high, low)]
    return lax.ppermute(block, axis, route)


def silu_parts(values_in):
    sigmoid_of = jax.nn.sigmoid(values_in)
    return (values_in * sigmoid_of, sigmoid_of * (1.0 + values_in * (1.0 - sigmoid_of)))


def pick_entry(lookup_table, row_index, col_index):
    rows_hit = jnp.arange(lookup_table.shape[0], dtype=jnp.int32)[:, None] == row_index
    cols_hit = jnp.arange(lookup_table.shape[1], dtype=jnp.int32)[None, :] == col_index
    return jnp.sum(jnp.where(rows_hit & cols_hit, lookup_table, 0))


def routed_device(tokens, upstream, expert_ids, gates, relocate, w_gate_up, w_down):
    n_rows = lax.axis_size("dp")
    n_cols = lax.axis_size("expert")
    slot_count = n_rows // SLICES
    experts = slot_count * n_cols
    tok_dev, feature_width = tokens.shape
    top_count = expert_ids.shape[1]
    capacity = min(tok_dev, max(2, (3 * tok_dev * top_count + 2 * experts - 1) // (2 * experts)))
    pair_count = tok_dev * top_count
    buffer_rows = experts * capacity
    slice_width = w_down.shape[2]
    col_block = n_cols // SLICES
    col_here = lax.axis_index("expert")
    row_here = lax.axis_index("dp")
    slot_here = row_here // SLICES
    slice_here = row_here % SLICES
    far_bit = n_cols.bit_length() - 2
    half_cols = n_cols // 2
    flat_ids = expert_ids.reshape(pair_count)
    home_column = flat_ids // slot_count
    slot_of = flat_ids % slot_count
    expert_iota = jnp.arange(experts, dtype=jnp.int32)
    relocated = jnp.sum(
        jnp.where(flat_ids[:, None] == expert_iota[None, :], relocate.reshape(experts)[None, :], 0),
        axis=1,
    )
    column = (home_column + half_cols * relocated) % n_cols
    pair_iota = jnp.arange(pair_count, dtype=jnp.int32)
    earlier = (flat_ids[:, None] == flat_ids[None, :]) & (pair_iota[None, :] < pair_iota[:, None])
    slot_rank = jnp.sum(earlier.astype(jnp.int32), axis=1)
    target = (slot_of * n_cols + column) * capacity + slot_rank
    placing = (target[None, :] == jnp.arange(buffer_rows, dtype=jnp.int32)[:, None]).astype(
        jnp.bfloat16
    )
    x_pairs = jnp.repeat(tokens, top_count, axis=0)
    d_pairs = (
        gates.reshape(pair_count, 1) * jnp.repeat(upstream, top_count, axis=0).astype(jnp.float32)
    ).astype(jnp.bfloat16)
    pair_data = jnp.stack([x_pairs, d_pairs])
    sent = jnp.einsum("bp,kpw->kbw", placing, pair_data, preferred_element_type=jnp.float32).astype(
        jnp.bfloat16
    )
    sent = sent.reshape(2, slot_count, n_cols, capacity, feature_width)
    at_column = lax.all_to_all(sent, "expert", split_axis=2, concat_axis=2, tiled=True)
    swapped_here = pick_entry(relocate, col_here, slot_here)
    own_pack = jnp.concatenate([w_gate_up, w_down], axis=2)
    far_pack = swapped(own_pack, "expert", far_bit)
    own_pack = jnp.where(swapped_here == 1, far_pack, own_pack)
    gate_up = own_pack[0, 0, : 2 * slice_width]
    down_rows = own_pack[0, 0, 2 * slice_width :]
    grouped = at_column.reshape(2, n_rows, col_block, capacity, feature_width)
    at_row = lax.all_to_all(grouped, "dp", split_axis=1, concat_axis=1, tiled=True)
    gathered = at_row[:, None]
    for bit_index in range(SLICES.bit_length() - 1):
        far_rows = swapped(gathered, "dp", bit_index)
        lower_half = slice_here // (1 << bit_index) % 2 == 0
        first_part = jnp.where(lower_half, gathered, far_rows)
        second_part = jnp.where(lower_half, far_rows, gathered)
        gathered = jnp.concatenate([first_part, second_part], axis=1)
    all_rows = gathered.reshape(2, -1, feature_width)
    rows_x = all_rows[0]
    rows_d = all_rows[1]
    gate_and_up = lax.dot_general(
        rows_x, gate_up, contract_last, preferred_element_type=jnp.float32
    )
    gate_pre = gate_and_up[:, :slice_width]
    up_pre = gate_and_up[:, slice_width:]
    activated, slope_of = silu_parts(gate_pre)
    hidden = (activated * up_pre).astype(jnp.bfloat16)
    hidden_grad = lax.dot_general(
        rows_d, down_rows, contract_last, preferred_element_type=jnp.float32
    )
    pre_grads = jnp.concatenate(
        [
            (hidden_grad * up_pre * slope_of).astype(jnp.bfloat16),
            (hidden_grad * activated).astype(jnp.bfloat16),
        ],
        axis=1,
    )
    grad_gu = lax.dot_general(
        pre_grads, rows_x, contract_first, preferred_element_type=jnp.float32
    ).astype(jnp.bfloat16)
    grad_dn = lax.dot_general(
        hidden, rows_d, contract_first, preferred_element_type=jnp.float32
    ).astype(jnp.bfloat16)
    slice_part = jnp.dot(pre_grads, gate_up, preferred_element_type=jnp.float32).astype(
        jnp.bfloat16
    )
    grad_pack = jnp.concatenate([grad_gu, grad_dn], axis=0)
    blocks = slice_part.reshape(2, 2, n_rows, col_block, capacity, feature_width)
    upper_half = slice_here // 2 % 2 == 1
    keep_half = jnp.where(upper_half, blocks[1], blocks[0])
    send_half = jnp.where(upper_half, blocks[0], blocks[1])
    got_half = swapped(send_half, "dp", 1)
    pairsum = keep_half.astype(jnp.float32) + got_half.astype(jnp.float32)
    odd_slice = slice_here % 2 == 1
    keep_last = jnp.where(odd_slice, pairsum[1], pairsum[0])
    send_last = jnp.where(odd_slice, pairsum[0], pairsum[1])
    got_last = swapped(send_last, "dp", 0)
    summed = keep_last + got_last
    back_rows = lax.all_to_all(summed, "dp", split_axis=0, concat_axis=0, tiled=True).reshape(
        slot_count, n_cols, capacity, feature_width
    )
    home_rows = lax.all_to_all(
        back_rows, "expert", split_axis=1, concat_axis=1, tiled=True
    ).reshape(buffer_rows, feature_width)
    hits = (
        target.reshape(tok_dev, top_count)[:, :, None]
        == jnp.arange(buffer_rows, dtype=jnp.int32)[None, None, :]
    )
    gather_mat = jnp.sum(hits.astype(jnp.float32), axis=1)
    grad_tokens = jnp.dot(
        gather_mat, home_rows, precision=lax.Precision.HIGHEST, preferred_element_type=jnp.float32
    ).astype(jnp.bfloat16)
    grad_gate_up = grad_pack[: 2 * slice_width].reshape(w_gate_up.shape)
    grad_down = grad_pack[2 * slice_width :].reshape(w_down.shape)
    return (grad_tokens, grad_gate_up, grad_down)


def crossed(block, axis, apart):
    return lax.ppermute(block, axis, [(i, i ^ apart) for i in range(lax.axis_size(axis))])


def whole(count):
    return [pl.BlockSpec(memory_space=pltpu.VMEM)] * count


def packed(tokens, upstream, expert_ids, gates, n_cols):
    experts = jnp.arange(n_cols, dtype=jnp.int32)[None, None, :]
    by_expert = jnp.sum(jnp.where(expert_ids[:, :, None] == experts, gates[:, :, None], 0.0), axis=1)
    high = lax.reduce_precision(by_expert, 8, 7)
    middle = lax.reduce_precision(by_expert - high, 8, 7)
    low = by_expert - high - middle
    spare = jnp.zeros((tokens.shape[0], 128 - 3 * n_cols), jnp.bfloat16)
    summands = [part.astype(jnp.bfloat16) for part in (high, middle, low)]
    return jnp.concatenate([tokens, upstream] + summands + [spare], axis=1)


def case_kernel(n_cols, relocate_ref, case_ref):
    pairs = n_cols // 4
    case_ref[0] = sum(relocate_ref[col] * 3 ** (pairs - 1 - col // 2) for col in range(n_cols // 2)) - 1


def weights_kernel(wgu_hbm, wdn_hbm, weights_ref, sems):
    split = wgu_hbm.shape[0]
    copies = [
        pltpu.make_async_copy(wgu_hbm, weights_ref.at[pl.ds(0, split)], sems.at[0]),
        pltpu.make_async_copy(wdn_hbm, weights_ref.at[pl.ds(split, wdn_hbm.shape[0])], sems.at[1]),
    ]
    for copy in copies:
        copy.start()
    for copy in copies:
        copy.wait()


def forward_kernel(n_cols, n_rows, n_z, relocate_ref, *refs):
    columns = refs[: n_rows - 1]
    diagonal = refs[n_rows - 1 : n_rows - 1 + n_z]
    weights_own, wgu_sib, wdn_sib, plane_ref, acts_ref, one_ref, kept_ref, *sent_refs = refs[n_rows - 1 + n_z :]
    tok_dev = diagonal[0].shape[0]
    for z in range(n_z):
        for d in range(n_rows):
            start = (z * n_rows + d) * tok_dev
            if d < n_rows - 1:
                block = columns[d][z * tok_dev : (z + 1) * tok_dev]
            else:
                block = diagonal[z][...]
            plane_ref[start : start + tok_dev] = block
    units, width = wdn_sib.shape
    split = wgu_sib.shape[0]
    col_here = lax.axis_index("expert")
    lane = lax.broadcasted_iota(jnp.int32, (8, 128), 1)
    row = lax.broadcasted_iota(jnp.int32, (8, 128), 0)
    wanted = jnp.where(row == 0, col_here, col_here ^ 1)
    chosen = (row < 2) & (lane % n_cols == wanted) & (lane < 3 * n_cols)
    gate_rows = lax.dot_general(
        jnp.where(chosen, 1.0, 0.0).astype(jnp.bfloat16),
        plane_ref[:, 2 * width :],
        contract_last,
        preferred_element_type=jnp.float32,
    )
    rows_x = plane_ref[:, :width]
    rows_u = plane_ref[:, width : 2 * width]
    total = None
    for index, (wgu, wdn) in enumerate(((weights_own[:split], weights_own[split:]), (wgu_sib[...], wdn_sib[...]))):
        gate = gate_rows[index : index + 1, :]
        pre = lax.dot_general(wgu, rows_x, contract_last, preferred_element_type=jnp.float32)
        hidden_grad = gate * lax.dot_general(wdn, rows_u, contract_last, preferred_element_type=jnp.float32)
        activated, slope_of = silu_parts(pre[:units])
        up_pre = pre[units:]
        base = index * 3 * units
        acts_ref[base : base + units] = (hidden_grad * up_pre * slope_of).astype(jnp.bfloat16)
        acts_ref[base + units : base + 2 * units] = (hidden_grad * activated).astype(jnp.bfloat16)
        acts_ref[base + 2 * units : base + 3 * units] = (activated * up_pre * gate).astype(jnp.bfloat16)
        part = lax.dot_general(acts_ref[base : base + 2 * units], wgu, contract_first, preferred_element_type=jnp.float32)
        total = part if total is None else total + part
    for z in range(n_z):
        for d in range(n_rows):
            start = (z * n_rows + d) * tok_dev
            block = total[start : start + tok_dev]
            if d == 0:
                kept_ref[z] = block
            else:
                sent_refs[d - 1][z] = block.astype(jnp.bfloat16)
    one_ref[...] = jnp.where(relocate_ref[col_here] == 1, acts_ref[: 3 * units], acts_ref[3 * units :])


def weight_grad_kernel(same_ref, cross_ref, plane_ref, other_ref, gu_ref, dn_ref):
    units, width = dn_ref.shape
    for out, low, start in ((gu_ref, 0, 0), (dn_ref, 2 * units, width)):
        high = low + out.shape[0]
        out[...] = (
            jnp.dot(same_ref[low:high], plane_ref[:, start : start + width], preferred_element_type=jnp.float32)
            + jnp.dot(cross_ref[low:high], other_ref[:, start : start + width], preferred_element_type=jnp.float32)
        ).astype(jnp.bfloat16)


def join_kernel(*refs):
    joined_ref = refs[-1]
    start = 0
    for block in refs[:-1]:
        joined_ref[start : start + block.shape[0]] = block[...]
        start += block.shape[0]


def sum_kernel(kept_ref, *refs):
    n_z = kept_ref.shape[0]
    got, outs = refs[:-n_z], refs[-n_z:]
    for z, out in enumerate(outs):
        total = kept_ref[z]
        for block in got:
            total += block[z].astype(jnp.float32)
        out[...] = total.astype(out.dtype)


def final_kernel(kept_ref, *refs):
    total = kept_ref[...]
    for block in refs[:-1]:
        total += block[...].astype(jnp.float32)
    refs[-1][...] = total.astype(jnp.bfloat16)


def place_kernel(moving, relocate_ref, acts_ref, *refs):
    *arrived, same_ref, other_ref = refs
    rows, lanes = same_ref.shape
    half = lanes // 2
    col_here = lax.axis_index("expert")
    both = None if 2 not in moving else arrived[-1]
    one = None if 1 not in moving else arrived[0]
    for out, low, col in ((same_ref, 0, col_here), (other_ref, rows, col_here ^ 1)):
        if both is None:
            come = one[...]
        elif one is None:
            come = both[low : low + rows]
        else:
            chip = col_here // 2 % len(moving)
            come = jnp.where(chip == moving.index(1), one[...], both[low : low + rows])
        moved = relocate_ref[col] == 1
        out[:, :half] = jnp.where(moved, come[:, half:], acts_ref[low : low + rows, :half])
        out[:, half:] = jnp.where(moved, come[:, :half], acts_ref[low : low + rows, half:])


def small(megabytes, flops=0, moved=0):
    return dict(
        compiler_params=pltpu.CompilerParams(vmem_limit_bytes=megabytes * 2**20),
        cost_estimate=pl.CostEstimate(flops=flops, bytes_accessed=moved, transcendentals=0),
    )


def exchanges(moving, relocate, acts, one, kept, sent_rows):
    n_cols = lax.axis_size("expert")
    half = n_cols // 2
    placed = jax.ShapeDtypeStruct(one.shape, one.dtype)
    block = kept.shape[1:]

    def route(count):
        return [(col, col ^ half) for col in range(n_cols) if moving[col % half // 2] == count]

    arrived = []
    if 1 in moving:
        arrived.append(lax.ppermute(one, "expert", route(1)))
    if 2 in moving:
        arrived.append(lax.ppermute(acts, "expert", route(2)))
    got = [crossed(rows, "dp", d + 1) for d, rows in enumerate(sent_rows)]
    parts = pl.pallas_call(
        sum_kernel,
        out_shape=[jax.ShapeDtypeStruct(block, jnp.float32)] + [jax.ShapeDtypeStruct(block, jnp.bfloat16)] * (half - 1),
        in_specs=whole(1 + len(got)),
        out_specs=whole(half),
        name="sums",
        **small(4),
    )(kept, *got)
    same, others = pl.pallas_call(
        functools.partial(place_kernel, moving),
        out_shape=[placed, placed],
        in_specs=[pl.BlockSpec(memory_space=pltpu.SMEM)] + whole(1 + len(arrived)),
        out_specs=whole(2),
        name="place",
        **small(4),
    )(relocate, acts, *arrived)
    return same, others, parts


def dense_device(tokens, upstream, expert_ids, gates, relocate, w_gate_up, w_down):
    n_rows = lax.axis_size("dp")
    n_cols = lax.axis_size("expert")
    n_z = n_cols // 2
    tok_dev = tokens.shape[0]
    half = n_cols // 2
    units, width = w_down.shape[2:]
    plane_rows = n_rows * n_z * tok_dev
    bf16 = jnp.bfloat16

    wgu_sib = crossed(w_gate_up[0, 0], "expert", 1)
    wdn_sib = crossed(w_down[0, 0], "expert", 1)
    own = packed(tokens, upstream, expert_ids, gates, n_cols)

    pairs = half // 2
    near_z = crossed(own, "expert", 2)
    across = crossed(own, "expert", half)
    diagonal = crossed(own, "dp", n_rows - 1)
    across, near_z, flags = lax.optimization_barrier((across, near_z, relocate[:, 0]))
    beyond = crossed(across, "expert", 2)
    along_z = [near_z, across, beyond]
    case = pl.pallas_call(
        functools.partial(case_kernel, n_cols),
        out_shape=jax.ShapeDtypeStruct((1,), jnp.int32),
        in_specs=[pl.BlockSpec(memory_space=pltpu.SMEM)],
        out_specs=pl.BlockSpec(memory_space=pltpu.SMEM),
        name="case",
        **small(4),
    )(flags)
    along_z, diagonal, wgu_sib, wdn_sib, case = lax.optimization_barrier((along_z, diagonal, wgu_sib, wdn_sib, case))
    column = pl.pallas_call(
        join_kernel,
        out_shape=jax.ShapeDtypeStruct((tok_dev * n_z, own.shape[1]), bf16),
        in_specs=whole(n_z),
        out_specs=whole(1)[0],
        name="join",
        **small(4),
    )(own, *along_z)
    columns = [crossed(column, "dp", d) for d in range(1, n_rows - 1)]
    diagonals = [crossed(diagonal, "expert", 2 * dz) for dz in range(1, n_z)]
    columns[1], wgu_own, wdn_own = lax.optimization_barrier((columns[1], w_gate_up[0, 0], w_down[0, 0]))
    weights_own = pl.pallas_call(
        weights_kernel,
        out_shape=jax.ShapeDtypeStruct((3 * units, width), bf16),
        in_specs=[pl.BlockSpec(memory_space=pl.ANY)] * 2,
        out_specs=whole(1)[0],
        scratch_shapes=[pltpu.SemaphoreType.DMA((2,))],
        name="weights",
        **small(4),
    )(wgu_own, wdn_own)

    plane, acts, one, kept, *sent = pl.pallas_call(
        functools.partial(forward_kernel, n_cols, n_rows, n_z),
        out_shape=[
            jax.ShapeDtypeStruct((plane_rows, own.shape[1]), bf16),
            jax.ShapeDtypeStruct((6 * units, plane_rows), bf16),
            jax.ShapeDtypeStruct((3 * units, plane_rows), bf16),
            jax.ShapeDtypeStruct((n_z, tok_dev, width), jnp.float32),
        ]
        + [jax.ShapeDtypeStruct((n_z, tok_dev, width), bf16)] * (n_rows - 1),
        in_specs=[pl.BlockSpec(memory_space=pltpu.SMEM)] + whole(n_rows - 1 + n_z + 3),
        out_specs=whole(3 + n_rows),
        name="forward",
        **small(16, flops=2 * 6 * units * 2 * width * plane_rows, moved=8 * 2**20),
    )(relocate[:, 0], column, *columns, diagonal, *diagonals, weights_own, wgu_sib, wdn_sib)

    plane_sib = crossed(plane, "expert", 1)
    cases = [tuple(number // 3 ** (pairs - 1 - p) % 3 for p in range(pairs)) for number in range(1, 3**pairs - 1)]
    same, others, parts = lax.switch(
        case[0], [functools.partial(exchanges, moving) for moving in cases], relocate[:, 0], acts, one, kept, sent
    )
    cross = crossed(others, "expert", 1)
    got_z = [crossed(parts[dz], "expert", 2 * dz) for dz in range(1, n_z)]
    grad_gu, grad_dn = pl.pallas_call(
        weight_grad_kernel,
        out_shape=[jax.ShapeDtypeStruct((2 * units, width), bf16), jax.ShapeDtypeStruct((units, width), bf16)],
        in_specs=whole(4),
        out_specs=whole(2),
        name="weight_grads",
        **small(16, flops=2 * 3 * units * width * 2 * plane_rows * 8, moved=32 * 2**20),
    )(same, cross, plane, plane_sib)
    kept, grad_dn = lax.optimization_barrier((parts[0], grad_dn))
    grad_tokens = pl.pallas_call(
        final_kernel,
        out_shape=jax.ShapeDtypeStruct((tok_dev, width), bf16),
        in_specs=whole(n_z),
        out_specs=whole(1)[0],
        name="grad_tokens",
        **small(4),
    )(kept, got_z[1], got_z[2], got_z[0])
    return grad_tokens, grad_gu.reshape(w_gate_up.shape), grad_dn.reshape(w_down.shape)


def solution(mesh):
    def per_device(*arrays):
        n_rows, n_cols = mesh.shape["dp"], mesh.shape["expert"]
        dense = n_rows == SLICES and arrays[2].shape[1] == n_cols == 2 * SLICES
        return (dense_device if dense else routed_device)(*arrays)

    return jax.shard_map(
        per_device,
        mesh=mesh,
        in_specs=(
            P(("dp", "expert"), None),
            P(("dp", "expert"), None),
            P(("dp", "expert"), None),
            P(("dp", "expert"), None),
            P(),
            P("expert", "dp", None, None),
            P("expert", "dp", None, None),
        ),
        out_specs=(
            P(("dp", "expert"), None),
            P("expert", "dp", None, None),
            P("expert", "dp", None, None),
        ),
        check_vma=False,
    )
```

```python
import functools

import jax
import jax.numpy as jnp
from jax import lax
from jax.experimental import pallas as pl
from jax.experimental.pallas import tpu as pltpu
from jax.sharding import PartitionSpec as P

SLICES = 4


contract_last = (((1,), (1,)), ((), ()))
contract_first = (((0,), (0,)), ((), ()))


def swapped(block, axis, apart):
    count = lax.axis_size(axis)
    route = []
    for low in range(count):
        high = low | 1 << apart
        if high != low and high < count:
            route += [(low, high), (high, low)]
    return lax.ppermute(block, axis, route)


def silu_parts(values_in):
    sigmoid_of = jax.nn.sigmoid(values_in)
    return (values_in * sigmoid_of, sigmoid_of * (1.0 + values_in * (1.0 - sigmoid_of)))


def pick_entry(lookup_table, row_index, col_index):
    rows_hit = jnp.arange(lookup_table.shape[0], dtype=jnp.int32)[:, None] == row_index
    cols_hit = jnp.arange(lookup_table.shape[1], dtype=jnp.int32)[None, :] == col_index
    return jnp.sum(jnp.where(rows_hit & cols_hit, lookup_table, 0))


def routed_device(tokens, upstream, expert_ids, gates, relocate, w_gate_up, w_down):
    n_rows = lax.axis_size("dp")
    n_cols = lax.axis_size("expert")
    slot_count = n_rows // SLICES
    experts = slot_count * n_cols
    tok_dev, feature_width = tokens.shape
    top_count = expert_ids.shape[1]
    capacity = min(tok_dev, max(2, (3 * tok_dev * top_count + 2 * experts - 1) // (2 * experts)))
    pair_count = tok_dev * top_count
    buffer_rows = experts * capacity
    slice_width = w_down.shape[2]
    col_block = n_cols // SLICES
    col_here = lax.axis_index("expert")
    row_here = lax.axis_index("dp")
    slot_here = row_here // SLICES
    slice_here = row_here % SLICES
    far_bit = n_cols.bit_length() - 2
    half_cols = n_cols // 2
    flat_ids = expert_ids.reshape(pair_count)
    home_column = flat_ids // slot_count
    slot_of = flat_ids % slot_count
    expert_iota = jnp.arange(experts, dtype=jnp.int32)
    relocated = jnp.sum(
        jnp.where(flat_ids[:, None] == expert_iota[None, :], relocate.reshape(experts)[None, :], 0),
        axis=1,
    )
    column = (home_column + half_cols * relocated) % n_cols
    pair_iota = jnp.arange(pair_count, dtype=jnp.int32)
    earlier = (flat_ids[:, None] == flat_ids[None, :]) & (pair_iota[None, :] < pair_iota[:, None])
    slot_rank = jnp.sum(earlier.astype(jnp.int32), axis=1)
    target = (slot_of * n_cols + column) * capacity + slot_rank
    placing = (target[None, :] == jnp.arange(buffer_rows, dtype=jnp.int32)[:, None]).astype(
        jnp.bfloat16
    )
    x_pairs = jnp.repeat(tokens, top_count, axis=0)
    d_pairs = (
        gates.reshape(pair_count, 1) * jnp.repeat(upstream, top_count, axis=0).astype(jnp.float32)
    ).astype(jnp.bfloat16)
    pair_data = jnp.stack([x_pairs, d_pairs])
    sent = jnp.einsum("bp,kpw->kbw", placing, pair_data, preferred_element_type=jnp.float32).astype(
        jnp.bfloat16
    )
    sent = sent.reshape(2, slot_count, n_cols, capacity, feature_width)
    at_column = lax.all_to_all(sent, "expert", split_axis=2, concat_axis=2, tiled=True)
    swapped_here = pick_entry(relocate, col_here, slot_here)
    own_pack = jnp.concatenate([w_gate_up, w_down], axis=2)
    far_pack = swapped(own_pack, "expert", far_bit)
    own_pack = jnp.where(swapped_here == 1, far_pack, own_pack)
    gate_up = own_pack[0, 0, : 2 * slice_width]
    down_rows = own_pack[0, 0, 2 * slice_width :]
    grouped = at_column.reshape(2, n_rows, col_block, capacity, feature_width)
    at_row = lax.all_to_all(grouped, "dp", split_axis=1, concat_axis=1, tiled=True)
    gathered = at_row[:, None]
    for bit_index in range(SLICES.bit_length() - 1):
        far_rows = swapped(gathered, "dp", bit_index)
        lower_half = slice_here // (1 << bit_index) % 2 == 0
        first_part = jnp.where(lower_half, gathered, far_rows)
        second_part = jnp.where(lower_half, far_rows, gathered)
        gathered = jnp.concatenate([first_part, second_part], axis=1)
    all_rows = gathered.reshape(2, -1, feature_width)
    rows_x = all_rows[0]
    rows_d = all_rows[1]
    gate_and_up = lax.dot_general(
        rows_x, gate_up, contract_last, preferred_element_type=jnp.float32
    )
    gate_pre = gate_and_up[:, :slice_width]
    up_pre = gate_and_up[:, slice_width:]
    activated, slope_of = silu_parts(gate_pre)
    hidden = (activated * up_pre).astype(jnp.bfloat16)
    hidden_grad = lax.dot_general(
        rows_d, down_rows, contract_last, preferred_element_type=jnp.float32
    )
    pre_grads = jnp.concatenate(
        [
            (hidden_grad * up_pre * slope_of).astype(jnp.bfloat16),
            (hidden_grad * activated).astype(jnp.bfloat16),
        ],
        axis=1,
    )
    grad_gu = lax.dot_general(
        pre_grads, rows_x, contract_first, preferred_element_type=jnp.float32
    ).astype(jnp.bfloat16)
    grad_dn = lax.dot_general(
        hidden, rows_d, contract_first, preferred_element_type=jnp.float32
    ).astype(jnp.bfloat16)
    slice_part = jnp.dot(pre_grads, gate_up, preferred_element_type=jnp.float32).astype(
        jnp.bfloat16
    )
    grad_pack = jnp.concatenate([grad_gu, grad_dn], axis=0)
    blocks = slice_part.reshape(2, 2, n_rows, col_block, capacity, feature_width)
    upper_half = slice_here // 2 % 2 == 1
    keep_half = jnp.where(upper_half, blocks[1], blocks[0])
    send_half = jnp.where(upper_half, blocks[0], blocks[1])
    got_half = swapped(send_half, "dp", 1)
    pairsum = keep_half.astype(jnp.float32) + got_half.astype(jnp.float32)
    odd_slice = slice_here % 2 == 1
    keep_last = jnp.where(odd_slice, pairsum[1], pairsum[0])
    send_last = jnp.where(odd_slice, pairsum[0], pairsum[1])
    got_last = swapped(send_last, "dp", 0)
    summed = keep_last + got_last
    back_rows = lax.all_to_all(summed, "dp", split_axis=0, concat_axis=0, tiled=True).reshape(
        slot_count, n_cols, capacity, feature_width
    )
    home_rows = lax.all_to_all(
        back_rows, "expert", split_axis=1, concat_axis=1, tiled=True
    ).reshape(buffer_rows, feature_width)
    hits = (
        target.reshape(tok_dev, top_count)[:, :, None]
        == jnp.arange(buffer_rows, dtype=jnp.int32)[None, None, :]
    )
    gather_mat = jnp.sum(hits.astype(jnp.float32), axis=1)
    grad_tokens = jnp.dot(
        gather_mat, home_rows, precision=lax.Precision.HIGHEST, preferred_element_type=jnp.float32
    ).astype(jnp.bfloat16)
    grad_gate_up = grad_pack[: 2 * slice_width].reshape(w_gate_up.shape)
    grad_down = grad_pack[2 * slice_width :].reshape(w_down.shape)
    return (grad_tokens, grad_gate_up, grad_down)


def crossed(block, axis, apart):
    return lax.ppermute(block, axis, [(i, i ^ apart) for i in range(lax.axis_size(axis))])


def whole(count):
    return [pl.BlockSpec(memory_space=pltpu.VMEM)] * count


def packed(tokens, upstream, expert_ids, gates, n_cols):
    experts = jnp.arange(n_cols, dtype=jnp.int32)[None, None, :]
    by_expert = jnp.sum(jnp.where(expert_ids[:, :, None] == experts, gates[:, :, None], 0.0), axis=1)
    high = lax.reduce_precision(by_expert, 8, 7)
    middle = lax.reduce_precision(by_expert - high, 8, 7)
    low = by_expert - high - middle
    spare = jnp.zeros((tokens.shape[0], 128 - 3 * n_cols), jnp.bfloat16)
    summands = [part.astype(jnp.bfloat16) for part in (high, middle, low)]
    return jnp.concatenate([tokens, upstream] + summands + [spare], axis=1)


def case_kernel(n_cols, relocate_ref, case_ref):
    pairs = n_cols // 4
    case_ref[0] = sum(relocate_ref[col] * 3 ** (pairs - 1 - col // 2) for col in range(n_cols // 2)) - 1


def weights_kernel(wgu_hbm, wdn_hbm, weights_ref, sems):
    split = wgu_hbm.shape[0]
    copies = [
        pltpu.make_async_copy(wgu_hbm, weights_ref.at[pl.ds(0, split)], sems.at[0]),
        pltpu.make_async_copy(wdn_hbm, weights_ref.at[pl.ds(split, wdn_hbm.shape[0])], sems.at[1]),
    ]
    for copy in copies:
        copy.start()
    for copy in copies:
        copy.wait()


def forward_kernel(n_cols, n_rows, n_z, relocate_ref, *refs):
    columns = refs[: n_rows - 1]
    diagonal = refs[n_rows - 1 : n_rows - 1 + n_z]
    weights_own, wgu_sib, wdn_sib, plane_ref, acts_ref, one_ref, kept_ref, *sent_refs = refs[n_rows - 1 + n_z :]
    tok_dev = diagonal[0].shape[0]
    for z in range(n_z):
        for d in range(n_rows):
            start = (z * n_rows + d) * tok_dev
            if d < n_rows - 1:
                block = columns[d][z * tok_dev : (z + 1) * tok_dev]
            else:
                block = diagonal[z][...]
            plane_ref[start : start + tok_dev] = block
    units, width = wdn_sib.shape
    split = wgu_sib.shape[0]
    col_here = lax.axis_index("expert")
    lane = lax.broadcasted_iota(jnp.int32, (8, 128), 1)
    row = lax.broadcasted_iota(jnp.int32, (8, 128), 0)
    wanted = jnp.where(row == 0, col_here, col_here ^ 1)
    chosen = (row < 2) & (lane % n_cols == wanted) & (lane < 3 * n_cols)
    gate_rows = lax.dot_general(
        jnp.where(chosen, 1.0, 0.0).astype(jnp.bfloat16),
        plane_ref[:, 2 * width :],
        contract_last,
        preferred_element_type=jnp.float32,
    )
    rows_x = plane_ref[:, :width]
    rows_u = plane_ref[:, width : 2 * width]
    total = None
    for index, (wgu, wdn) in enumerate(((weights_own[:split], weights_own[split:]), (wgu_sib[...], wdn_sib[...]))):
        gate = gate_rows[index : index + 1, :]
        pre = lax.dot_general(wgu, rows_x, contract_last, preferred_element_type=jnp.float32)
        hidden_grad = gate * lax.dot_general(wdn, rows_u, contract_last, preferred_element_type=jnp.float32)
        activated, slope_of = silu_parts(pre[:units])
        up_pre = pre[units:]
        base = index * 3 * units
        acts_ref[base : base + units] = (hidden_grad * up_pre * slope_of).astype(jnp.bfloat16)
        acts_ref[base + units : base + 2 * units] = (hidden_grad * activated).astype(jnp.bfloat16)
        acts_ref[base + 2 * units : base + 3 * units] = (activated * up_pre * gate).astype(jnp.bfloat16)
        part = lax.dot_general(acts_ref[base : base + 2 * units], wgu, contract_first, preferred_element_type=jnp.float32)
        total = part if total is None else total + part
    for z in range(n_z):
        for d in range(n_rows):
            start = (z * n_rows + d) * tok_dev
            block = total[start : start + tok_dev]
            if d == 0:
                kept_ref[z] = block
            else:
                sent_refs[d - 1][z] = block.astype(jnp.bfloat16)
    one_ref[...] = jnp.where(relocate_ref[col_here] == 1, acts_ref[: 3 * units], acts_ref[3 * units :])


def weight_grad_kernel(relocate_ref, come_ref, acts_ref, cross_ref, plane_ref, other_ref, gu_ref, dn_ref):
    units, width = dn_ref.shape
    half = come_ref.shape[1] // 2
    moved = relocate_ref[lax.axis_index("expert")] == 1
    turned = jnp.concatenate([come_ref[:, half:], come_ref[:, :half]], axis=1)
    same = jnp.where(moved, turned, acts_ref[: 3 * units])
    for out, low, start in ((gu_ref, 0, 0), (dn_ref, 2 * units, width)):
        high = low + out.shape[0]
        out[...] = (
            jnp.dot(same[low:high], plane_ref[:, start : start + width], preferred_element_type=jnp.float32)
            + jnp.dot(cross_ref[low:high], other_ref[:, start : start + width], preferred_element_type=jnp.float32)
        ).astype(jnp.bfloat16)


def join_kernel(*refs):
    joined_ref = refs[-1]
    start = 0
    for block in refs[:-1]:
        joined_ref[start : start + block.shape[0]] = block[...]
        start += block.shape[0]


def sum_kernel(kept_ref, *refs):
    n_z = kept_ref.shape[0]
    got, outs = refs[:-n_z], refs[-n_z:]
    for z, out in enumerate(outs):
        total = kept_ref[z]
        for block in got:
            total += block[z].astype(jnp.float32)
        out[...] = total.astype(out.dtype)


def final_kernel(kept_ref, *refs):
    total = kept_ref[...]
    for block in refs[:-1]:
        total += block[...].astype(jnp.float32)
    refs[-1][...] = total.astype(jnp.bfloat16)


def place_kernel(moving, relocate_ref, acts_ref, *refs):
    count = len(set(moving) & {1, 2})
    arrived, other_ref = refs[:count], refs[count]
    rows, lanes = other_ref.shape
    half = lanes // 2
    col_here = lax.axis_index("expert")
    here = col_here // 2 % len(moving) == moving.index(1) if 1 in moving else False

    def come(low):
        if 2 not in moving:
            return arrived[0][...]
        if 1 not in moving:
            return arrived[-1][low : low + rows]
        return jnp.where(here, arrived[0][...], arrived[-1][low : low + rows])

    moved = relocate_ref[col_here ^ 1] == 1
    block = come(rows)
    other_ref[:, :half] = jnp.where(moved, block[:, half:], acts_ref[rows:, :half])
    other_ref[:, half:] = jnp.where(moved, block[:, :half], acts_ref[rows:, half:])
    if 2 in moving:
        refs[-1][...] = come(0)


def small(megabytes, flops=0, moved=0):
    return dict(
        compiler_params=pltpu.CompilerParams(vmem_limit_bytes=megabytes * 2**20),
        cost_estimate=pl.CostEstimate(flops=flops, bytes_accessed=moved, transcendentals=0),
    )


def exchanges(moving, relocate, acts, one, kept, sent_rows):
    n_cols = lax.axis_size("expert")
    half = n_cols // 2
    placed = jax.ShapeDtypeStruct(one.shape, one.dtype)
    block = kept.shape[1:]

    def route(count):
        return [(col, col ^ half) for col in range(n_cols) if moving[col % half // 2] == count]

    arrived = []
    if 1 in moving:
        arrived.append(lax.ppermute(one, "expert", route(1)))
    if 2 in moving:
        arrived.append(lax.ppermute(acts, "expert", route(2)))
    got = [crossed(rows, "dp", d + 1) for d, rows in enumerate(sent_rows)]
    parts = pl.pallas_call(
        sum_kernel,
        out_shape=[jax.ShapeDtypeStruct(block, jnp.float32)] + [jax.ShapeDtypeStruct(block, jnp.bfloat16)] * (half - 1),
        in_specs=whole(1 + len(got)),
        out_specs=whole(half),
        name="sums",
        **small(4),
    )(kept, *got)
    others, *own_come = pl.pallas_call(
        functools.partial(place_kernel, moving),
        out_shape=[placed] * (2 if 2 in moving else 1),
        in_specs=[pl.BlockSpec(memory_space=pltpu.SMEM)] + whole(1 + len(arrived)),
        out_specs=whole(2 if 2 in moving else 1),
        name="place",
        **small(4),
    )(relocate, acts, *arrived)
    return (own_come or arrived)[0], others, parts


def dense_device(tokens, upstream, expert_ids, gates, relocate, w_gate_up, w_down):
    n_rows = lax.axis_size("dp")
    n_cols = lax.axis_size("expert")
    n_z = n_cols // 2
    tok_dev = tokens.shape[0]
    half = n_cols // 2
    units, width = w_down.shape[2:]
    plane_rows = n_rows * n_z * tok_dev
    bf16 = jnp.bfloat16

    wgu_sib = crossed(w_gate_up[0, 0], "expert", 1)
    wdn_sib = crossed(w_down[0, 0], "expert", 1)
    own = packed(tokens, upstream, expert_ids, gates, n_cols)

    pairs = half // 2
    near_z = crossed(own, "expert", 2)
    across = crossed(own, "expert", half)
    diagonal = crossed(own, "dp", n_rows - 1)
    across, near_z, flags = lax.optimization_barrier((across, near_z, relocate[:, 0]))
    beyond = crossed(across, "expert", 2)
    along_z = [near_z, across, beyond]
    case = pl.pallas_call(
        functools.partial(case_kernel, n_cols),
        out_shape=jax.ShapeDtypeStruct((1,), jnp.int32),
        in_specs=[pl.BlockSpec(memory_space=pltpu.SMEM)],
        out_specs=pl.BlockSpec(memory_space=pltpu.SMEM),
        name="case",
        **small(4),
    )(flags)
    along_z, diagonal, wgu_sib, wdn_sib, case = lax.optimization_barrier((along_z, diagonal, wgu_sib, wdn_sib, case))
    column = pl.pallas_call(
        join_kernel,
        out_shape=jax.ShapeDtypeStruct((tok_dev * n_z, own.shape[1]), bf16),
        in_specs=whole(n_z),
        out_specs=whole(1)[0],
        name="join",
        **small(4),
    )(own, *along_z)
    columns = [crossed(column, "dp", d) for d in range(1, n_rows - 1)]
    diagonals = [crossed(diagonal, "expert", 2 * dz) for dz in range(1, n_z)]
    columns[1], wgu_own, wdn_own = lax.optimization_barrier((columns[1], w_gate_up[0, 0], w_down[0, 0]))
    weights_own = pl.pallas_call(
        weights_kernel,
        out_shape=jax.ShapeDtypeStruct((3 * units, width), bf16),
        in_specs=[pl.BlockSpec(memory_space=pl.ANY)] * 2,
        out_specs=whole(1)[0],
        scratch_shapes=[pltpu.SemaphoreType.DMA((2,))],
        name="weights",
        **small(4),
    )(wgu_own, wdn_own)

    plane, acts, one, kept, *sent = pl.pallas_call(
        functools.partial(forward_kernel, n_cols, n_rows, n_z),
        out_shape=[
            jax.ShapeDtypeStruct((plane_rows, own.shape[1]), bf16),
            jax.ShapeDtypeStruct((6 * units, plane_rows), bf16),
            jax.ShapeDtypeStruct((3 * units, plane_rows), bf16),
            jax.ShapeDtypeStruct((n_z, tok_dev, width), jnp.float32),
        ]
        + [jax.ShapeDtypeStruct((n_z, tok_dev, width), bf16)] * (n_rows - 1),
        in_specs=[pl.BlockSpec(memory_space=pltpu.SMEM)] + whole(n_rows - 1 + n_z + 3),
        out_specs=whole(3 + n_rows),
        name="forward",
        **small(16, flops=2 * 6 * units * 2 * width * plane_rows, moved=8 * 2**20),
    )(relocate[:, 0], column, *columns, diagonal, *diagonals, weights_own, wgu_sib, wdn_sib)

    plane_sib = crossed(plane, "expert", 1)
    cases = [tuple(number // 3 ** (pairs - 1 - p) % 3 for p in range(pairs)) for number in range(1, 3**pairs - 1)]
    come, others, parts = lax.switch(
        case[0], [functools.partial(exchanges, moving) for moving in cases], relocate[:, 0], acts, one, kept, sent
    )
    cross = crossed(others, "expert", 1)
    got_z = [crossed(parts[dz], "expert", 2 * dz) for dz in range(1, n_z)]
    grad_gu, grad_dn = pl.pallas_call(
        weight_grad_kernel,
        out_shape=[jax.ShapeDtypeStruct((2 * units, width), bf16), jax.ShapeDtypeStruct((units, width), bf16)],
        in_specs=[pl.BlockSpec(memory_space=pltpu.SMEM)] + whole(5),
        out_specs=whole(2),
        name="weight_grads",
        **small(16, flops=2 * 3 * units * width * 2 * plane_rows * 8, moved=32 * 2**20),
    )(relocate[:, 0], come, acts, cross, plane, plane_sib)
    kept, grad_dn = lax.optimization_barrier((parts[0], grad_dn))
    grad_tokens = pl.pallas_call(
        final_kernel,
        out_shape=jax.ShapeDtypeStruct((tok_dev, width), bf16),
        in_specs=whole(n_z),
        out_specs=whole(1)[0],
        name="grad_tokens",
        **small(4),
    )(kept, got_z[1], got_z[2], got_z[0])
    return grad_tokens, grad_gu.reshape(w_gate_up.shape), grad_dn.reshape(w_down.shape)


def solution(mesh):
    def per_device(*arrays):
        n_rows, n_cols = mesh.shape["dp"], mesh.shape["expert"]
        dense = n_rows == SLICES and arrays[2].shape[1] == n_cols == 2 * SLICES
        return (dense_device if dense else routed_device)(*arrays)

    return jax.shard_map(
        per_device,
        mesh=mesh,
        in_specs=(
            P(("dp", "expert"), None),
            P(("dp", "expert"), None),
            P(("dp", "expert"), None),
            P(("dp", "expert"), None),
            P(),
            P("expert", "dp", None, None),
            P("expert", "dp", None, None),
        ),
        out_specs=(
            P(("dp", "expert"), None),
            P("expert", "dp", None, None),
            P("expert", "dp", None, None),
        ),
        check_vma=False,
    )
```

```python
import functools

import jax
import jax.numpy as jnp
from jax import lax
from jax.experimental import pallas as pl
from jax.experimental.pallas import tpu as pltpu
from jax.sharding import PartitionSpec as P

SLICES = 4


contract_last = (((1,), (1,)), ((), ()))
contract_first = (((0,), (0,)), ((), ()))


def swapped(block, axis, apart):
    count = lax.axis_size(axis)
    route = []
    for low in range(count):
        high = low | 1 << apart
        if high != low and high < count:
            route += [(low, high), (high, low)]
    return lax.ppermute(block, axis, route)


def silu_parts(values_in):
    sigmoid_of = jax.nn.sigmoid(values_in)
    return (values_in * sigmoid_of, sigmoid_of * (1.0 + values_in * (1.0 - sigmoid_of)))


def pick_entry(lookup_table, row_index, col_index):
    rows_hit = jnp.arange(lookup_table.shape[0], dtype=jnp.int32)[:, None] == row_index
    cols_hit = jnp.arange(lookup_table.shape[1], dtype=jnp.int32)[None, :] == col_index
    return jnp.sum(jnp.where(rows_hit & cols_hit, lookup_table, 0))


def routed_device(tokens, upstream, expert_ids, gates, relocate, w_gate_up, w_down):
    n_rows = lax.axis_size("dp")
    n_cols = lax.axis_size("expert")
    slot_count = n_rows // SLICES
    experts = slot_count * n_cols
    tok_dev, feature_width = tokens.shape
    top_count = expert_ids.shape[1]
    capacity = min(tok_dev, max(2, (3 * tok_dev * top_count + 2 * experts - 1) // (2 * experts)))
    pair_count = tok_dev * top_count
    buffer_rows = experts * capacity
    slice_width = w_down.shape[2]
    col_block = n_cols // SLICES
    col_here = lax.axis_index("expert")
    row_here = lax.axis_index("dp")
    slot_here = row_here // SLICES
    slice_here = row_here % SLICES
    far_bit = n_cols.bit_length() - 2
    half_cols = n_cols // 2
    flat_ids = expert_ids.reshape(pair_count)
    home_column = flat_ids // slot_count
    slot_of = flat_ids % slot_count
    expert_iota = jnp.arange(experts, dtype=jnp.int32)
    relocated = jnp.sum(
        jnp.where(flat_ids[:, None] == expert_iota[None, :], relocate.reshape(experts)[None, :], 0),
        axis=1,
    )
    column = (home_column + half_cols * relocated) % n_cols
    pair_iota = jnp.arange(pair_count, dtype=jnp.int32)
    earlier = (flat_ids[:, None] == flat_ids[None, :]) & (pair_iota[None, :] < pair_iota[:, None])
    slot_rank = jnp.sum(earlier.astype(jnp.int32), axis=1)
    target = (slot_of * n_cols + column) * capacity + slot_rank
    placing = (target[None, :] == jnp.arange(buffer_rows, dtype=jnp.int32)[:, None]).astype(
        jnp.bfloat16
    )
    x_pairs = jnp.repeat(tokens, top_count, axis=0)
    d_pairs = (
        gates.reshape(pair_count, 1) * jnp.repeat(upstream, top_count, axis=0).astype(jnp.float32)
    ).astype(jnp.bfloat16)
    pair_data = jnp.stack([x_pairs, d_pairs])
    sent = jnp.einsum("bp,kpw->kbw", placing, pair_data, preferred_element_type=jnp.float32).astype(
        jnp.bfloat16
    )
    sent = sent.reshape(2, slot_count, n_cols, capacity, feature_width)
    at_column = lax.all_to_all(sent, "expert", split_axis=2, concat_axis=2, tiled=True)
    swapped_here = pick_entry(relocate, col_here, slot_here)
    own_pack = jnp.concatenate([w_gate_up, w_down], axis=2)
    far_pack = swapped(own_pack, "expert", far_bit)
    own_pack = jnp.where(swapped_here == 1, far_pack, own_pack)
    gate_up = own_pack[0, 0, : 2 * slice_width]
    down_rows = own_pack[0, 0, 2 * slice_width :]
    grouped = at_column.reshape(2, n_rows, col_block, capacity, feature_width)
    at_row = lax.all_to_all(grouped, "dp", split_axis=1, concat_axis=1, tiled=True)
    gathered = at_row[:, None]
    for bit_index in range(SLICES.bit_length() - 1):
        far_rows = swapped(gathered, "dp", bit_index)
        lower_half = slice_here // (1 << bit_index) % 2 == 0
        first_part = jnp.where(lower_half, gathered, far_rows)
        second_part = jnp.where(lower_half, far_rows, gathered)
        gathered = jnp.concatenate([first_part, second_part], axis=1)
    all_rows = gathered.reshape(2, -1, feature_width)
    rows_x = all_rows[0]
    rows_d = all_rows[1]
    gate_and_up = lax.dot_general(
        rows_x, gate_up, contract_last, preferred_element_type=jnp.float32
    )
    gate_pre = gate_and_up[:, :slice_width]
    up_pre = gate_and_up[:, slice_width:]
    activated, slope_of = silu_parts(gate_pre)
    hidden = (activated * up_pre).astype(jnp.bfloat16)
    hidden_grad = lax.dot_general(
        rows_d, down_rows, contract_last, preferred_element_type=jnp.float32
    )
    pre_grads = jnp.concatenate(
        [
            (hidden_grad * up_pre * slope_of).astype(jnp.bfloat16),
            (hidden_grad * activated).astype(jnp.bfloat16),
        ],
        axis=1,
    )
    grad_gu = lax.dot_general(
        pre_grads, rows_x, contract_first, preferred_element_type=jnp.float32
    ).astype(jnp.bfloat16)
    grad_dn = lax.dot_general(
        hidden, rows_d, contract_first, preferred_element_type=jnp.float32
    ).astype(jnp.bfloat16)
    slice_part = jnp.dot(pre_grads, gate_up, preferred_element_type=jnp.float32).astype(
        jnp.bfloat16
    )
    grad_pack = jnp.concatenate([grad_gu, grad_dn], axis=0)
    blocks = slice_part.reshape(2, 2, n_rows, col_block, capacity, feature_width)
    upper_half = slice_here // 2 % 2 == 1
    keep_half = jnp.where(upper_half, blocks[1], blocks[0])
    send_half = jnp.where(upper_half, blocks[0], blocks[1])
    got_half = swapped(send_half, "dp", 1)
    pairsum = keep_half.astype(jnp.float32) + got_half.astype(jnp.float32)
    odd_slice = slice_here % 2 == 1
    keep_last = jnp.where(odd_slice, pairsum[1], pairsum[0])
    send_last = jnp.where(odd_slice, pairsum[0], pairsum[1])
    got_last = swapped(send_last, "dp", 0)
    summed = keep_last + got_last
    back_rows = lax.all_to_all(summed, "dp", split_axis=0, concat_axis=0, tiled=True).reshape(
        slot_count, n_cols, capacity, feature_width
    )
    home_rows = lax.all_to_all(
        back_rows, "expert", split_axis=1, concat_axis=1, tiled=True
    ).reshape(buffer_rows, feature_width)
    hits = (
        target.reshape(tok_dev, top_count)[:, :, None]
        == jnp.arange(buffer_rows, dtype=jnp.int32)[None, None, :]
    )
    gather_mat = jnp.sum(hits.astype(jnp.float32), axis=1)
    grad_tokens = jnp.dot(
        gather_mat, home_rows, precision=lax.Precision.HIGHEST, preferred_element_type=jnp.float32
    ).astype(jnp.bfloat16)
    grad_gate_up = grad_pack[: 2 * slice_width].reshape(w_gate_up.shape)
    grad_down = grad_pack[2 * slice_width :].reshape(w_down.shape)
    return (grad_tokens, grad_gate_up, grad_down)


def crossed(block, axis, apart):
    return lax.ppermute(block, axis, [(i, i ^ apart) for i in range(lax.axis_size(axis))])


def whole(count):
    return [pl.BlockSpec(memory_space=pltpu.VMEM)] * count


def packed(tokens, upstream, expert_ids, gates, n_cols):
    experts = jnp.arange(n_cols, dtype=jnp.int32)[None, None, :]
    by_expert = jnp.sum(jnp.where(expert_ids[:, :, None] == experts, gates[:, :, None], 0.0), axis=1)
    high = lax.reduce_precision(by_expert, 8, 7)
    middle = lax.reduce_precision(by_expert - high, 8, 7)
    low = by_expert - high - middle
    spare = jnp.zeros((tokens.shape[0], 128 - 3 * n_cols), jnp.bfloat16)
    summands = [part.astype(jnp.bfloat16) for part in (high, middle, low)]
    return jnp.concatenate([tokens, upstream] + summands + [spare], axis=1)


def case_kernel(n_cols, relocate_ref, case_ref):
    pairs = n_cols // 4
    case_ref[0] = sum(relocate_ref[col] * 3 ** (pairs - 1 - col // 2) for col in range(n_cols // 2)) - 1


def weights_kernel(wgu_hbm, wdn_hbm, weights_ref, sems):
    split = wgu_hbm.shape[0]
    copies = [
        pltpu.make_async_copy(wgu_hbm, weights_ref.at[pl.ds(0, split)], sems.at[0]),
        pltpu.make_async_copy(wdn_hbm, weights_ref.at[pl.ds(split, wdn_hbm.shape[0])], sems.at[1]),
    ]
    for copy in copies:
        copy.start()
    for copy in copies:
        copy.wait()


def forward_kernel(n_cols, n_rows, n_z, relocate_ref, *refs):
    columns = refs[: n_rows - 1]
    own_diagonal, first, third, second = refs[n_rows - 1 : n_rows - 1 + n_z]
    diagonal = (own_diagonal, first, second, third)
    weights_own, wgu_sib, wdn_sib, plane_ref, acts_ref, one_ref, kept_ref, *sent_refs = refs[n_rows - 1 + n_z :]
    tok_dev = diagonal[0].shape[0]
    for z in range(n_z):
        for d in range(n_rows):
            start = (z * n_rows + d) * tok_dev
            if d < n_rows - 1:
                block = columns[d][z * tok_dev : (z + 1) * tok_dev]
            else:
                block = diagonal[z][...]
            plane_ref[start : start + tok_dev] = block
    units, width = wdn_sib.shape
    split = wgu_sib.shape[0]
    col_here = lax.axis_index("expert")
    lane = lax.broadcasted_iota(jnp.int32, (8, 128), 1)
    row = lax.broadcasted_iota(jnp.int32, (8, 128), 0)
    wanted = jnp.where(row == 0, col_here, col_here ^ 1)
    chosen = (row < 2) & (lane % n_cols == wanted) & (lane < 3 * n_cols)
    gate_rows = lax.dot_general(
        jnp.where(chosen, 1.0, 0.0).astype(jnp.bfloat16),
        plane_ref[:, 2 * width :],
        contract_last,
        preferred_element_type=jnp.float32,
    )
    rows_x = plane_ref[:, :width]
    rows_u = plane_ref[:, width : 2 * width]
    total = None
    for index, (wgu, wdn) in enumerate(((weights_own[:split], weights_own[split:]), (wgu_sib[...], wdn_sib[...]))):
        gate = gate_rows[index : index + 1, :]
        pre = lax.dot_general(wgu, rows_x, contract_last, preferred_element_type=jnp.float32)
        hidden_grad = gate * lax.dot_general(wdn, rows_u, contract_last, preferred_element_type=jnp.float32)
        activated, slope_of = silu_parts(pre[:units])
        up_pre = pre[units:]
        base = index * 3 * units
        acts_ref[base : base + units] = (hidden_grad * up_pre * slope_of).astype(jnp.bfloat16)
        acts_ref[base + units : base + 2 * units] = (hidden_grad * activated).astype(jnp.bfloat16)
        acts_ref[base + 2 * units : base + 3 * units] = (activated * up_pre * gate).astype(jnp.bfloat16)
        part = lax.dot_general(acts_ref[base : base + 2 * units], wgu, contract_first, preferred_element_type=jnp.float32)
        total = part if total is None else total + part
    for z in range(n_z):
        for d in range(n_rows):
            start = (z * n_rows + d) * tok_dev
            block = total[start : start + tok_dev]
            if d == 0:
                kept_ref[z] = block
            else:
                sent_refs[d - 1][z] = block.astype(jnp.bfloat16)
    one_ref[...] = jnp.where(relocate_ref[col_here] == 1, acts_ref[: 3 * units], acts_ref[3 * units :])


def weight_grad_kernel(same_ref, cross_ref, plane_ref, other_ref, gu_ref, dn_ref):
    units, width = dn_ref.shape
    for out, low, start in ((gu_ref, 0, 0), (dn_ref, 2 * units, width)):
        high = low + out.shape[0]
        out[...] = (
            jnp.dot(same_ref[low:high], plane_ref[:, start : start + width], preferred_element_type=jnp.float32)
            + jnp.dot(cross_ref[low:high], other_ref[:, start : start + width], preferred_element_type=jnp.float32)
        ).astype(jnp.bfloat16)


def join_kernel(*refs):
    joined_ref = refs[-1]
    start = 0
    for block in refs[:-1]:
        joined_ref[start : start + block.shape[0]] = block[...]
        start += block.shape[0]


def sum_kernel(kept_ref, *refs):
    n_z = kept_ref.shape[0]
    got, outs = refs[:-n_z], refs[-n_z:]
    for z, out in enumerate(outs):
        total = kept_ref[z]
        for block in got:
            total += block[z].astype(jnp.float32)
        out[...] = total.astype(out.dtype)


def final_kernel(kept_ref, *refs):
    total = kept_ref[...]
    for block in refs[:-1]:
        total += block[...].astype(jnp.float32)
    refs[-1][...] = total.astype(jnp.bfloat16)


def place_kernel(moving, relocate_ref, acts_ref, *refs):
    *arrived, same_ref, other_ref = refs
    rows, lanes = same_ref.shape
    half = lanes // 2
    col_here = lax.axis_index("expert")
    both = None if 2 not in moving else arrived[-1]
    one = None if 1 not in moving else arrived[0]
    for out, low, col in ((same_ref, 0, col_here), (other_ref, rows, col_here ^ 1)):
        if both is None:
            come = one[...]
        elif one is None:
            come = both[low : low + rows]
        else:
            chip = col_here // 2 % len(moving)
            come = jnp.where(chip == moving.index(1), one[...], both[low : low + rows])
        moved = relocate_ref[col] == 1
        out[:, :half] = jnp.where(moved, come[:, half:], acts_ref[low : low + rows, :half])
        out[:, half:] = jnp.where(moved, come[:, :half], acts_ref[low : low + rows, half:])


def small(megabytes, flops=0, moved=0):
    return dict(
        compiler_params=pltpu.CompilerParams(vmem_limit_bytes=megabytes * 2**20),
        cost_estimate=pl.CostEstimate(flops=flops, bytes_accessed=moved, transcendentals=0),
    )


def exchanges(moving, relocate, acts, one, kept, sent_rows):
    n_cols = lax.axis_size("expert")
    half = n_cols // 2
    placed = jax.ShapeDtypeStruct(one.shape, one.dtype)
    block = kept.shape[1:]

    def route(count):
        return [(col, col ^ half) for col in range(n_cols) if moving[col % half // 2] == count]

    arrived = []
    if 1 in moving:
        arrived.append(lax.ppermute(one, "expert", route(1)))
    if 2 in moving:
        arrived.append(lax.ppermute(acts, "expert", route(2)))
    got = [crossed(rows, "dp", d + 1) for d, rows in enumerate(sent_rows)]
    parts = pl.pallas_call(
        sum_kernel,
        out_shape=[jax.ShapeDtypeStruct(block, jnp.float32)] + [jax.ShapeDtypeStruct(block, jnp.bfloat16)] * (half - 1),
        in_specs=whole(1 + len(got)),
        out_specs=whole(half),
        name="sums",
        **small(4),
    )(kept, *got)
    same, others = pl.pallas_call(
        functools.partial(place_kernel, moving),
        out_shape=[placed, placed],
        in_specs=[pl.BlockSpec(memory_space=pltpu.SMEM)] + whole(1 + len(arrived)),
        out_specs=whole(2),
        name="place",
        **small(4),
    )(relocate, acts, *arrived)
    return same, others, parts


def dense_device(tokens, upstream, expert_ids, gates, relocate, w_gate_up, w_down):
    n_rows = lax.axis_size("dp")
    n_cols = lax.axis_size("expert")
    n_z = n_cols // 2
    tok_dev = tokens.shape[0]
    half = n_cols // 2
    units, width = w_down.shape[2:]
    plane_rows = n_rows * n_z * tok_dev
    bf16 = jnp.bfloat16

    wgu_sib = crossed(w_gate_up[0, 0], "expert", 1)
    wdn_sib = crossed(w_down[0, 0], "expert", 1)
    own = packed(tokens, upstream, expert_ids, gates, n_cols)

    pairs = half // 2
    near_z = crossed(own, "expert", 2)
    across = crossed(own, "expert", half)
    diagonal = crossed(own, "dp", n_rows - 1)
    across, near_z, flags = lax.optimization_barrier((across, near_z, relocate[:, 0]))
    beyond = crossed(across, "expert", 2)
    along_z = [near_z, across, beyond]
    case = pl.pallas_call(
        functools.partial(case_kernel, n_cols),
        out_shape=jax.ShapeDtypeStruct((1,), jnp.int32),
        in_specs=[pl.BlockSpec(memory_space=pltpu.SMEM)],
        out_specs=pl.BlockSpec(memory_space=pltpu.SMEM),
        name="case",
        **small(4),
    )(flags)
    along_z, diagonal, wgu_sib, wdn_sib, case = lax.optimization_barrier((along_z, diagonal, wgu_sib, wdn_sib, case))
    column = pl.pallas_call(
        join_kernel,
        out_shape=jax.ShapeDtypeStruct((tok_dev * n_z, own.shape[1]), bf16),
        in_specs=whole(n_z),
        out_specs=whole(1)[0],
        name="join",
        **small(4),
    )(own, *along_z)
    columns = [crossed(column, "dp", d) for d in range(1, n_rows - 1)]
    diagonals = [crossed(diagonal, "expert", 2 * dz) for dz in range(1, n_z)]
    columns[1], wgu_own, wdn_own = lax.optimization_barrier((columns[1], w_gate_up[0, 0], w_down[0, 0]))
    weights_own = pl.pallas_call(
        weights_kernel,
        out_shape=jax.ShapeDtypeStruct((3 * units, width), bf16),
        in_specs=[pl.BlockSpec(memory_space=pl.ANY)] * 2,
        out_specs=whole(1)[0],
        scratch_shapes=[pltpu.SemaphoreType.DMA((2,))],
        name="weights",
        **small(4),
    )(wgu_own, wdn_own)

    plane, acts, one, kept, *sent = pl.pallas_call(
        functools.partial(forward_kernel, n_cols, n_rows, n_z),
        out_shape=[
            jax.ShapeDtypeStruct((plane_rows, own.shape[1]), bf16),
            jax.ShapeDtypeStruct((6 * units, plane_rows), bf16),
            jax.ShapeDtypeStruct((3 * units, plane_rows), bf16),
            jax.ShapeDtypeStruct((n_z, tok_dev, width), jnp.float32),
        ]
        + [jax.ShapeDtypeStruct((n_z, tok_dev, width), bf16)] * (n_rows - 1),
        in_specs=[pl.BlockSpec(memory_space=pltpu.SMEM)] + whole(n_rows - 1 + n_z + 3),
        out_specs=whole(3 + n_rows),
        name="forward",
        **small(16, flops=2 * 6 * units * 2 * width * plane_rows, moved=8 * 2**20),
    )(relocate[:, 0], column, *columns, diagonal, diagonals[0], diagonals[2], diagonals[1], weights_own, wgu_sib, wdn_sib)

    plane_sib = crossed(plane, "expert", 1)
    cases = [tuple(number // 3 ** (pairs - 1 - p) % 3 for p in range(pairs)) for number in range(1, 3**pairs - 1)]
    same, others, parts = lax.switch(
        case[0], [functools.partial(exchanges, moving) for moving in cases], relocate[:, 0], acts, one, kept, sent
    )
    cross = crossed(others, "expert", 1)
    got_z = [crossed(parts[dz], "expert", 2 * dz) for dz in range(1, n_z)]
    grad_gu, grad_dn = pl.pallas_call(
        weight_grad_kernel,
        out_shape=[jax.ShapeDtypeStruct((2 * units, width), bf16), jax.ShapeDtypeStruct((units, width), bf16)],
        in_specs=whole(4),
        out_specs=whole(2),
        name="weight_grads",
        **small(16, flops=2 * 3 * units * width * 2 * plane_rows * 8, moved=32 * 2**20),
    )(same, cross, plane, plane_sib)
    kept, grad_dn = lax.optimization_barrier((parts[0], grad_dn))
    grad_tokens = pl.pallas_call(
        final_kernel,
        out_shape=jax.ShapeDtypeStruct((tok_dev, width), bf16),
        in_specs=whole(n_z),
        out_specs=whole(1)[0],
        name="grad_tokens",
        **small(4),
    )(kept, got_z[1], got_z[2], got_z[0])
    return grad_tokens, grad_gu.reshape(w_gate_up.shape), grad_dn.reshape(w_down.shape)


def solution(mesh):
    def per_device(*arrays):
        n_rows, n_cols = mesh.shape["dp"], mesh.shape["expert"]
        dense = n_rows == SLICES and arrays[2].shape[1] == n_cols == 2 * SLICES
        return (dense_device if dense else routed_device)(*arrays)

    return jax.shard_map(
        per_device,
        mesh=mesh,
        in_specs=(
            P(("dp", "expert"), None),
            P(("dp", "expert"), None),
            P(("dp", "expert"), None),
            P(("dp", "expert"), None),
            P(),
            P("expert", "dp", None, None),
            P("expert", "dp", None, None),
        ),
        out_specs=(
            P(("dp", "expert"), None),
            P("expert", "dp", None, None),
            P("expert", "dp", None, None),
        ),
        check_vma=False,
    )
```
